32 devices in a mesh: dp: 8 (over z, x), seq: 4 (over y, core).
Axes of the slice: x: 2, y: 2, z: 4, core: 2. Of those that a mesh axis runs over, the one named last changes fastest.
Arguments:
- tokens: bfloat16 [64, 512, 768], P('dp', 'seq'), may hold values from -6 to 6
- cotangent: bfloat16 [64, 512, 768], P('dp', 'seq'), may hold values from -6 to 6
- segments: int32 [64, 512], P('dp', 'seq'), may hold values from 0 to 3, as said below
- w_query: bfloat16 [768, 768], replicated, may hold values from -0.21875 to 0.21875
- b_query: bfloat16 [768], replicated, may hold values from -4 to 4
- w_key: bfloat16 [768, 768], replicated, may hold values from -0.21875 to 0.21875
- w_value: bfloat16 [768, 768], replicated, may hold values from -0.21875 to 0.21875
- b_value: bfloat16 [768], replicated, may hold values from -4 to 4
- w_out: bfloat16 [768, 768], replicated, may hold values from -1.75 to 1.75
- b_out: bfloat16 [768], replicated, may hold values from -4 to 4
- gain_one: bfloat16 [768], replicated, may hold values from 0.5 to 1.5
- shift_one: bfloat16 [768], replicated, may hold values from -4 to 4
- w_inner: bfloat16 [768, 3072], replicated, may hold values from -0.21875 to 0.21875
- b_inner: bfloat16 [3072], replicated, may hold values from -4 to 4
- w_outer: bfloat16 [3072, 768], replicated, may hold values from -0.109375 to 0.109375
- b_outer: bfloat16 [768], replicated, may hold values from -4 to 4
- gain_two: bfloat16 [768], replicated, may hold values from 0.5 to 1.5
- shift_two: bfloat16 [768], replicated, may hold values from -4 to 4
Outputs:
- output: bfloat16 [64, 512, 768], P('dp', 'seq')
- grad_tokens: bfloat16 [64, 512, 768], P('dp', 'seq')
- grad_w_query: float32 [768, 768], P('dp', 'seq')
- grad_b_query: float32 [768], P('dp')
- grad_w_key: float32 [768, 768], P('dp', 'seq')
- grad_w_value: float32 [768, 768], P('dp', 'seq')
- grad_b_value: float32 [768], P('dp')
- grad_w_out: float32 [768, 768], P('dp', 'seq')
- grad_b_out: float32 [768], P('dp')
- grad_gain_one: float32 [768], P('dp')
- grad_shift_one: float32 [768], P('dp')
- grad_w_inner: float32 [768, 3072], P('dp', 'seq')
- grad_b_inner: float32 [3072], P('dp')
- grad_w_outer: float32 [3072, 768], P('dp', 'seq')
- grad_b_outer: float32 [768], P('dp')
- grad_gain_two: float32 [768], P('dp')
- grad_shift_two: float32 [768], P('dp')
The draws below stay inside these ranges and needn't reach their ends.
Inputs may be any that keep to these rules, and one draw needn't show every extreme that they name: `segments`: in each row, ids never fall except to 0: an optional fragment 1, then fragment 2, which starts within the row's first 128 tokens and ends within its last 128, then fragment 3, then padding 0 up to the row's end.
All inputs are finite; a program needn't handle non-finite values.
Results may differ from the reference program's by a relative error of at most 0.019.
Values may be sent and summed in bfloat16 or wider, within the bound.
No kernel may reach another device: no remote copies, remote signals or barrier semaphores. Data moves between devices by JAX's collectives and lax.ppermute only.
A program may use at most 192 MiB of HBM per device.

```python
import jax
import jax.numpy as jnp
from jax import lax

D = 768
HEADS = 12
FF = 3072
LENGTH = 512
ROWS_MB = 2
ROWS = 64
SEQ_LOC = 128


def draw_segments(key, part):
    key_open, key_pad, key_tail = jax.random.split(key, 3)
    opening = jax.random.randint(key_open, (ROWS, 1), 0, SEQ_LOC // 2 + 1)
    padding = jax.random.randint(key_pad, (ROWS, 1), 0, SEQ_LOC // 2)
    trailing = jax.random.randint(key_tail, (ROWS, 1), 1, SEQ_LOC // 2)
    places = jnp.arange(LENGTH, dtype=jnp.int32)[None, :]
    closing = LENGTH - padding - trailing
    fragment_ids = jnp.where(places < opening, 1, jnp.where(places < closing, 2, jnp.where(places < LENGTH - padding, 3, 0)))
    return fragment_ids.astype(jnp.int32)


def with_spikes(values, stream_key, source, target, blocks, factor):
    def block_of(dim):
        return (jnp.arange(values.shape[dim]) // (values.shape[dim] // blocks)).reshape((-1,) + (1,) * (values.ndim - 1 - dim))

    near = jax.random.permutation(stream_key, blocks)[block_of(target)]
    other_side = (block_of(target) + blocks // 2) % blocks
    return jnp.where((block_of(source) == near) | (block_of(source) == other_side), factor * values, values)


def block_scale(own_key, dims, cuts, smallest, high):
    level, own = 1.0, jax.random.fold_in(own_key, 6)
    for position, shards_of in cuts:
        steps = jnp.exp(jax.random.uniform(jax.random.fold_in(own, position), (shards_of,), jnp.float32, smallest / len(cuts), high / len(cuts)))
        level = level * jnp.repeat(steps, dims[position] // shards_of).reshape([-1 if axis == position else 1 for axis in range(len(dims))])
    return level


def normal_values(stream_key, extent, spread, limit, cuts=(), held_as=jnp.bfloat16):
    values = jax.random.normal(stream_key, extent, jnp.float32) * spread
    if len(cuts) > 0:
        values = block_scale(stream_key, extent, cuts, -0.22, 0.18) * values
    return jnp.clip(values, min=-limit, max=limit).astype(held_as)


def bell_draw_with(rng, shape, scale, limit, pieces, heavy, held_as=jnp.bfloat16):
    values = scale * jax.random.normal(rng, shape, jnp.float32)
    if pieces:
        values = values * block_scale(rng, shape, pieces, -0.22, 0.18)
    return jnp.clip(with_spikes(values, jax.random.fold_in(rng, 3), *heavy), -limit, limit).astype(held_as)


def setup_inputs(seed: int = 0) -> dict:
    streams_of = jax.random.split(jax.random.key(seed), 19)
    tokens = normal_values(streams_of[0], (ROWS, LENGTH, D), 1.0, 6.0, ((0, 8), (1, 4)))
    cotangent = bell_draw_with(streams_of[1], (ROWS, LENGTH, D), 1.0, 6.0, ((0, 8), (1, 4)), (0, 2, 8, 2.0))
    segments = draw_segments(jax.random.fold_in(streams_of[18], 71), 0)
    w_query = normal_values(streams_of[3], (D, D), D ** -0.5, 0.21875)
    b_query = normal_values(streams_of[4], (D,), 0.3, 4.0)
    w_key = normal_values(streams_of[5], (D, D), D ** -0.5, 0.21875)
    w_value = normal_values(streams_of[6], (D, D), D ** -0.5, 0.21875)
    b_value = normal_values(streams_of[7], (D,), 0.3, 4.0)
    w_out = normal_values(streams_of[8], (D, D), (D // 64) ** -0.5, 1.75)
    b_out = normal_values(streams_of[9], (D,), 0.3, 4.0)
    gain_one = jnp.clip(1.0 + 0.1 * jax.random.normal(streams_of[10], (D,), jnp.float32), 0.5, 1.5).astype(jnp.bfloat16)
    shift_one = normal_values(streams_of[11], (D,), 0.3, 4.0)
    w_inner = normal_values(streams_of[12], (D, FF), D ** -0.5, 0.21875)
    b_inner = normal_values(streams_of[13], (FF,), 0.3, 4.0)
    w_outer = normal_values(streams_of[14], (FF, D), FF ** -0.5, 0.109375)
    b_outer = normal_values(streams_of[15], (D,), 0.3, 4.0)
    gain_two = jnp.clip(1.0 + 0.1 * jax.random.normal(streams_of[16], (D,), jnp.float32), 0.5, 1.5).astype(jnp.bfloat16)
    shift_two = normal_values(streams_of[17], (D,), 0.3, 4.0)
    return {"tokens": tokens, "cotangent": cotangent, "segments": segments, "w_query": w_query, "b_query": b_query, "w_key": w_key, "w_value": w_value, "b_value": b_value, "w_out": w_out, "b_out": b_out, "gain_one": gain_one, "shift_one": shift_one, "w_inner": w_inner, "b_inner": b_inner, "w_outer": w_outer, "b_outer": b_outer, "gain_two": gain_two, "shift_two": shift_two}


@jax.custom_vjp
def low(v):
    return lax.optimization_barrier(v.astype(jnp.bfloat16)).astype(jnp.float32)

@jax.custom_vjp
def low_back(v):
    return v

def low_keep(v):
    return (low(v), None)

def low_pass(kept, grad):
    return (grad,)

def back_keep(v):
    return (v, None)

def back_low(kept, grad):
    return (low(grad),)
low.defvjp(low_keep, low_pass)
low_back.defvjp(back_keep, back_low)

def project(inputs, weight):
    return jnp.einsum('rtd,de->rte', inputs, weight, precision=lax.Precision.HIGHEST)

def layer_norm(values, gain, shift):
    centred = values - lax.optimization_barrier(jnp.mean(values, -1, keepdims=True))
    normed = centred * lax.rsqrt(lax.optimization_barrier(jnp.mean(centred * centred, -1, keepdims=True)) + 1e-05)
    return normed * gain + shift

def layer(inputs, fragments, params):
    w_query, b_query, w_key, w_value, b_value, w_out, b_out, gain_one, shift_one, w_inner, b_inner, w_outer, b_outer, gain_two, shift_two = params
    rows, length, width = inputs.shape
    head_dim = width // HEADS
    query = low(low_back(project(inputs, w_query) + b_query))
    keys = low(low_back(project(inputs, w_key)))
    values = low(low_back(project(inputs, w_value) + b_value))
    query = query.reshape(rows, length, HEADS, head_dim)
    keys = keys.reshape(rows, length, HEADS, head_dim)
    values = values.reshape(rows, length, HEADS, head_dim)
    raw = jnp.einsum('rqhd,rkhd->rhqk', query, keys, precision=lax.Precision.HIGHEST)
    scores = low_back(raw * head_dim ** (-0.5))
    masking = (fragments[:, :, None] == fragments[:, None, :])[:, None]
    scores = jnp.where(masking, scores, -1e+30)
    highest = lax.optimization_barrier(jnp.max(scores, -1, keepdims=True))
    expo = jnp.exp(scores - highest)
    prob = expo / lax.optimization_barrier(jnp.sum(expo, -1, keepdims=True))
    context = jnp.einsum('rhqk,rkhd->rqhd', low(prob), values, precision=lax.Precision.HIGHEST)
    context = low(low_back(context.reshape(rows, length, width)))
    attention = low_back(project(context, w_out) + b_out)
    hidden_one = layer_norm(inputs + attention, gain_one, shift_one)
    inner = low_back(project(low(hidden_one), w_inner) + b_inner)
    active = low(jax.nn.gelu(inner, approximate=False))
    branch = low_back(project(active, w_outer) + b_outer)
    return layer_norm(hidden_one + branch, gain_two, shift_two)

def reference(tokens, cotangent, segments, w_query, b_query, w_key, w_value, b_value, w_out, b_out, gain_one, shift_one, w_inner, b_inner, w_outer, b_outer, gain_two, shift_two):
    params = tuple((weight.astype(jnp.float32) for weight in (w_query, b_query, w_key, w_value, b_value, w_out, b_out, gain_one, shift_one, w_inner, b_inner, w_outer, b_outer, gain_two, shift_two)))
    blocks = tokens.shape[0] // ROWS_MB

    def shaped(array):
        return array.reshape((blocks, ROWS_MB) + array.shape[1:])

    def step(carry, block):
        inputs, upstream, fragments = block

        def forward(values, weights):
            return layer(values, fragments, weights)
        result, pull = jax.vjp(forward, inputs.astype(jnp.float32), params)
        grad_inputs, grad_params = pull(upstream.astype(jnp.float32))
        carry = tuple((total + piece for total, piece in zip(carry, grad_params)))
        return (carry, (result.astype(jnp.bfloat16), grad_inputs.astype(jnp.bfloat16)))
    zeros = tuple((jnp.zeros(weight.shape, jnp.float32) for weight in params))
    totals, (results, grad_inputs) = lax.scan(step, zeros, (shaped(tokens), shaped(cotangent), shaped(segments)))
    grad_w_query, grad_b_query, grad_w_key, grad_w_value, grad_b_value, grad_w_out, grad_b_out, grad_gain_one, grad_shift_one, grad_w_inner, grad_b_inner, grad_w_outer, grad_b_outer, grad_gain_two, grad_shift_two = totals
    return (results.reshape(tokens.shape), grad_inputs.reshape(tokens.shape), grad_w_query, grad_b_query, grad_w_key, grad_w_value, grad_b_value, grad_w_out, grad_b_out, grad_gain_one, grad_shift_one, grad_w_inner, grad_b_inner, grad_w_outer, grad_b_outer, grad_gain_two, grad_shift_two)
```

```python
import jax
import jax.numpy as jnp
from jax import lax
from jax.sharding import PartitionSpec as P

HEADS = 12
BF = jnp.bfloat16
F32 = jnp.float32


def layer_norm(values, gain, shift):
    centred = values - jnp.mean(values, -1, keepdims=True)
    inverse = lax.rsqrt(jnp.mean(centred * centred, -1, keepdims=True) + 1e-05)
    normed = centred * inverse
    return (normed * gain.astype(F32) + shift.astype(F32), normed, inverse)


def norm_back(upstream, normed, inverse, gain):
    scaled = upstream * gain.astype(F32)
    return inverse * (
        scaled
        - jnp.mean(scaled, -1, keepdims=True)
        - normed * jnp.mean(scaled * normed, -1, keepdims=True)
    )


def matmul(pattern, left, right):
    return jnp.einsum(pattern, left, right, preferred_element_type=F32)


def column_sum(values):
    return jnp.sum(values.astype(F32), 0)


def swap(array, axis, mask):
    size = lax.axis_size(axis)
    return lax.ppermute(array, axis, [(i, i ^ mask) for i in range(size)])


def rows_in(array):
    n = lax.axis_size("seq")
    me = lax.axis_index("seq")
    rows = array.shape[0] // n
    blocks = []
    for k in range(n):
        block = lax.dynamic_slice_in_dim(array, (me ^ k) * rows, rows, 0)
        blocks.append(swap(block, "seq", k) if k else block)
    return jnp.concatenate(blocks, 1)


def rows_out(array):
    n = lax.axis_size("seq")
    me = lax.axis_index("seq")
    rows, length = array.shape[0], array.shape[1] // n
    whole = jnp.zeros((rows * n, length) + array.shape[2:], array.dtype)
    for k in range(n):
        block = lax.slice_in_dim(array, k * length, (k + 1) * length, axis=1)
        block = swap(block, "seq", k) if k else block
        whole = lax.dynamic_update_slice_in_dim(whole, block, (me ^ k) * rows, 0)
    return whole


def bits_of(size):
    return [1 << b for b in range(size.bit_length() - 1)]


def halving_order():
    seq_bits = [("seq", m) for m in bits_of(lax.axis_size("seq"))]
    dp_bits = [("dp", m) for m in bits_of(lax.axis_size("dp"))]
    return [seq_bits[0], dp_bits[0]] + seq_bits[1:] + dp_bits[1:]


def reduce_matrix(grad):
    sn, dn = lax.axis_size("seq"), lax.axis_size("dp")
    ms, md = lax.axis_index("seq"), lax.axis_index("dp")
    high, wide = grad.shape[0] // dn, grad.shape[1] // sn
    blocks = grad.astype(BF).reshape(dn, high, sn, wide).transpose(2, 0, 1, 3)
    blocks = jnp.take(blocks, ms ^ jnp.arange(sn), axis=0)
    blocks = jnp.take(blocks, md ^ jnp.arange(dn), axis=1)
    left = {"seq": sn, "dp": dn}
    for axis, mask in halving_order():
        size = left[axis]
        dim = 0 if axis == "seq" else 1
        shape = blocks.shape[:dim] + (size // 2, 2) + blocks.shape[dim + 1 :]
        split = blocks.reshape(shape)
        keep = lax.index_in_dim(split, 0, dim + 1, keepdims=False)
        send = lax.index_in_dim(split, 1, dim + 1, keepdims=False)
        blocks = keep + swap(send, axis, mask)
        left[axis] = size // 2
    return blocks.reshape(high, wide).astype(F32)


def reduce_vectors(vectors):
    scattered = lax.psum_scatter(tuple(vectors), "dp", scatter_dimension=0, tiled=True)
    return lax.psum(scattered, "seq")


def body(
    tokens,
    cotangent,
    segments,
    w_query,
    b_query,
    w_key,
    w_value,
    b_value,
    w_out,
    b_out,
    gain_one,
    shift_one,
    w_inner,
    b_inner,
    w_outer,
    b_outer,
    gain_two,
    shift_two,
):
    width = tokens.shape[-1]
    head_dim = width // HEADS
    scale = head_dim ** (-0.5)
    x_rows = rows_in(tokens)
    up_rows = rows_in(cotangent)
    seg_rows = rows_in(segments)
    rows, length = seg_rows.shape
    count = rows * length
    inputs = x_rows.reshape(count, width)
    upstream = up_rows.reshape(count, width).astype(F32)
    masking = (seg_rows[:, :, None] == seg_rows[:, None, :])[:, None]

    def split(values):
        return values.reshape(rows, length, HEADS, head_dim)

    query = (matmul("nd,de->ne", inputs, w_query) + b_query).astype(BF)
    keys = matmul("nd,de->ne", inputs, w_key).astype(BF)
    values = (matmul("nd,de->ne", inputs, w_value) + b_value).astype(BF)
    query_h, keys_h, values_h = split(query), split(keys), split(values)

    def masked_scores():
        raw = matmul("rqhd,rkhd->rhqk", query_h, keys_h) * scale
        return jnp.where(masking, raw, -1e30)

    scores = masked_scores()
    highest = jnp.max(scores, -1, keepdims=True)
    expo = jnp.exp(scores - highest)
    totals = jnp.sum(expo, -1, keepdims=True)
    prob = expo / totals
    log_total = highest + jnp.log(totals)
    context = matmul("rhqk,rkhd->rqhd", prob.astype(BF), values_h).astype(BF).reshape(count, width)
    resid_one = inputs.astype(F32) + matmul("nd,de->ne", context, w_out) + b_out
    hidden_one, normed_one, inverse_one = layer_norm(resid_one, gain_one, shift_one)
    hidden_low = hidden_one.astype(BF)
    inner = matmul("nd,df->nf", hidden_low, w_inner) + b_inner
    phi = 0.5 * (1.0 + lax.erf(inner * 0.7071067811865476))
    active = (inner * phi).astype(BF)
    resid_two = hidden_one + matmul("nf,fd->nd", active, w_outer) + b_outer
    result, normed_two, inverse_two = layer_norm(resid_two, gain_two, shift_two)
    output = rows_out(result.astype(BF).reshape(rows, length, width))
    grad_gain_two = jnp.sum(upstream * normed_two, 0)
    grad_shift_two = jnp.sum(upstream, 0)
    grad_resid_two = norm_back(upstream, normed_two, inverse_two, gain_two)
    grad_branch = grad_resid_two.astype(BF)
    grad_b_outer = column_sum(grad_branch)
    grad_w_outer = reduce_matrix(matmul("nf,nd->fd", active, grad_branch))
    slope = phi + inner * jnp.exp(-0.5 * inner * inner) * 0.3989422804014327
    grad_inner = (matmul("nd,fd->nf", grad_branch, w_outer) * slope).astype(BF)
    grad_b_inner = column_sum(grad_inner)
    grad_w_inner = reduce_matrix(matmul("nd,nf->df", hidden_low, grad_inner))
    grad_hidden = grad_resid_two + matmul("nf,df->nd", grad_inner, w_inner)
    grad_gain_one = jnp.sum(grad_hidden * normed_one, 0)
    grad_shift_one = jnp.sum(grad_hidden, 0)
    grad_resid_one = norm_back(grad_hidden, normed_one, inverse_one, gain_one)
    grad_attn = grad_resid_one.astype(BF)
    grad_b_out = column_sum(grad_attn)
    grad_w_out = reduce_matrix(matmul("nd,ne->de", context, grad_attn))
    grad_context = split(matmul("ne,de->nd", grad_attn, w_out).astype(BF))
    prob_back = jnp.exp(masked_scores() - log_total)
    grad_prob = matmul("rqhd,rkhd->rhqk", grad_context, values_h)
    inner_sum = jnp.sum(prob_back * grad_prob, -1, keepdims=True)
    grad_scores = (prob_back * (grad_prob - inner_sum)).astype(BF)
    grad_query = (matmul("rhqk,rkhd->rqhd", grad_scores, keys_h) * scale).astype(BF)
    grad_keys = (matmul("rhqk,rqhd->rkhd", grad_scores, query_h) * scale).astype(BF)
    grad_values = matmul("rhqk,rqhd->rkhd", prob_back.astype(BF), grad_context).astype(BF)
    grad_query, grad_keys, grad_values = (
        piece.reshape(count, width) for piece in (grad_query, grad_keys, grad_values)
    )
    grad_w_query = reduce_matrix(matmul("nd,ne->de", inputs, grad_query))
    grad_w_key = reduce_matrix(matmul("nd,ne->de", inputs, grad_keys))
    grad_w_value = reduce_matrix(matmul("nd,ne->de", inputs, grad_values))
    grad_b_query = column_sum(grad_query)
    grad_b_value = column_sum(grad_values)
    grad_input = (
        grad_resid_one
        + matmul("ne,de->nd", grad_query, w_query)
        + matmul("ne,de->nd", grad_keys, w_key)
        + matmul("ne,de->nd", grad_values, w_value)
    ).astype(BF)
    grad_tokens = rows_out(grad_input.reshape(rows, length, width))
    (
        grad_b_query,
        grad_b_value,
        grad_b_out,
        grad_gain_one,
        grad_shift_one,
        grad_b_inner,
        grad_b_outer,
        grad_gain_two,
        grad_shift_two,
    ) = reduce_vectors(
        (
            grad_b_query,
            grad_b_value,
            grad_b_out,
            grad_gain_one,
            grad_shift_one,
            grad_b_inner,
            grad_b_outer,
            grad_gain_two,
            grad_shift_two,
        )
    )
    return (
        output,
        grad_tokens,
        grad_w_query,
        grad_b_query,
        grad_w_key,
        grad_w_value,
        grad_b_value,
        grad_w_out,
        grad_b_out,
        grad_gain_one,
        grad_shift_one,
        grad_w_inner,
        grad_b_inner,
        grad_w_outer,
        grad_b_outer,
        grad_gain_two,
        grad_shift_two,
    )


def solution(mesh):
    token = P("dp", "seq", None)
    matrix = P("dp", "seq")
    vector = P("dp")
    return jax.shard_map(
        body,
        mesh=mesh,
        in_specs=(token, token, P("dp", "seq")) + (P(),) * 15,
        out_specs=(
            token,
            token,
            matrix,
            vector,
            matrix,
            matrix,
            vector,
            matrix,
            vector,
            vector,
            vector,
            matrix,
            vector,
            matrix,
            vector,
            vector,
            vector,
        ),
        check_vma=False,
    )
```

```python
import functools

import jax
import jax.numpy as jnp
from jax import lax
from jax.experimental import pallas as pl
from jax.experimental.pallas import tpu as pltpu
from jax.sharding import PartitionSpec as P

HEADS = 12
BF = jnp.bfloat16
F32 = jnp.float32
MIB = 1 << 20
VMEM = 60 * MIB
LONG = pl.CostEstimate(flops=60_000_000_000, bytes_accessed=1, transcendentals=0)
TINY = pl.CostEstimate(flops=1, bytes_accessed=1, transcendentals=0)


def dot_nn(a, b):
    return lax.dot_general(a, b, (((1,), (0,)), ((), ())), preferred_element_type=F32)


def dot_nt(a, b):
    return lax.dot_general(a, b, (((1,), (1,)), ((), ())), preferred_element_type=F32)


def dot_tn(a, b):
    return lax.dot_general(a, b, (((0,), (0,)), ((), ())), preferred_element_type=F32)


def normal_laws(a):
    gauss = jnp.exp(a * a * -0.5)
    return 0.5 + 0.5 * lax.erf(a * 0.7071067811865476), a * (gauss * 0.3989422804014327)


def norm_parts(values):
    mean = jnp.mean(values, -1, keepdims=True)
    centred = values - mean
    inverse = lax.rsqrt(jnp.mean(centred * centred, -1, keepdims=True) + 1e-05)
    return centred * inverse, inverse


def norm_back(scaled, normed, inverse):
    return inverse * (
        scaled
        - jnp.mean(scaled, -1, keepdims=True)
        - normed * jnp.mean(scaled * normed, -1, keepdims=True)
    )


def lane_of(shape):
    return lax.broadcasted_iota(jnp.int32, shape, 1)


def place_of(me_ref):
    return me_ref[0], me_ref[1], me_ref[2]


def dp_rel(position):
    return (position % 4) * 2 + position // 4


def split_rows(position_c, position_d, me):
    core, _, place = me
    return pl.multiple_of((place ^ dp_rel(position_d)) * 96 + (core ^ position_c) * 48, 16)


def attend_kernel(n, row, aliased, local, me_ref, *refs):
    x_refs, refs = refs[:n], refs[n:]
    seg_refs, refs = refs[:n], refs[n:]
    wq_ref, wk_ref, wv_ref, vec_ref, vecs_ref, wo_ref = refs[:6]
    refs = refs[6 + aliased :]
    q_out, k_out, v_out, ctx_out, lse_out, resid_out, xt_out, ctxt_out, mq_out, mk_out = refs[:10]
    x_s, acc_s, ctx_s, t_s = refs[10:]
    step = pl.program_id(0)
    me = place_of(me_ref)

    @pl.when(step == 0)
    def _():
        for k in range(n):
            x_s[k * local : (k + 1) * local, :] = x_refs[k][0, :local, :]
        lse_out[...] = jnp.zeros_like(lse_out)
        seg = jnp.concatenate([ref[0, :, :local].astype(F32)[row : row + 1] for ref in seg_refs], 1)
        spot = lax.broadcasted_iota(jnp.int32, (128, seg.shape[1]), 0) % 64
        same = spot.astype(F32) == seg
        mq_out[...] = jnp.where(same, -1e30, 0.0).T.astype(BF)
        mk_out[...] = jnp.where((spot < 7) & jnp.logical_not(same), 1.0, 0.0).T.astype(BF)

    x = x_s[...]
    q = ((dot_nn(x, wq_ref[...]) + vec_ref[0:1, :]).astype(BF).astype(F32) * 0.125).astype(BF)
    kk = dot_nn(x, wk_ref[...]).astype(BF)
    v = (dot_nn(x, wv_ref[...]) + vec_ref[1:2, :]).astype(BF)
    q_out[...] = q
    k_out[...] = kk
    v_out[...] = v
    mq, mk = mq_out[...], mk_out[...]
    low = lane_of(mq.shape) < 64
    stats = lse_out[...]
    lanes = lane_of(stats.shape)
    parts = []
    for pair in range(2):
        cols = slice(pair * 128, pair * 128 + 128)
        q2, k2, v2 = q[:, cols], kk[:, cols], v[:, cols]
        halves = []
        for half in range(2):
            mine = low if half == 0 else jnp.logical_not(low)
            s = dot_nt(jnp.where(mine, q2, mq), jnp.where(mine, k2, mk))
            top = jnp.max(s, -1, keepdims=True)
            e = jnp.exp(s - top)
            total = jnp.sum(e, -1, keepdims=True)
            halves.append(dot_nn(e.astype(BF), v2) * (1.0 / total))
            stats = jnp.where(lanes == step * 4 + pair * 2 + half, top + jnp.log(total), stats)
        parts.append(jnp.where(low, halves[0], halves[1]).astype(BF))
    lse_out[...] = stats
    ctx = jnp.concatenate(parts, 1)
    ctx_out[...] = ctx
    ctx_s[:, pl.ds(pl.multiple_of(step * 256, 256), 256)] = ctx
    add = dot_nn(ctx, wo_ref[...])

    @pl.when(step == 0)
    def _():
        acc_s[...] = add

    @pl.when(step == 1)
    def _():
        acc_s[...] += add

    @pl.when(step == 2)
    def _():
        resid_out[...] = x_s[...].astype(F32) + (acc_s[...] + add) + vecs_ref[2:3, :]
        for source, target in ((x_s, xt_out), (ctx_s, ctxt_out)):
            t_s[...] = source[...].T
            for c in range(2):
                for d in range(8):
                    target[0, c, d] = t_s[pl.ds(split_rows(c, d, me), 48), :]


def attend(me, row, rows, x_blocks, seg_blocks, w, before):
    n, local, width = len(x_blocks), seg_blocks[0].shape[1] - 16, x_blocks[0].shape[2]
    length = n * local
    count = rows * length
    full = lambda shape: pl.BlockSpec(shape, lambda g, m: (0,) * len(shape))
    col = pl.BlockSpec((width, 256), lambda g, m: (0, g))
    vec = pl.BlockSpec((16, 256), lambda g, m: (0, g))
    out_col = pl.BlockSpec((length, 256), lambda g, m: (row, g))
    out_t = pl.BlockSpec((1, 2, 8, 48, length), lambda g, m: (row, 0, 0, 0, 0))
    out_shape = [
        jax.ShapeDtypeStruct((count, width), BF),
        jax.ShapeDtypeStruct((count, width), BF),
        jax.ShapeDtypeStruct((count, width), BF),
        jax.ShapeDtypeStruct((count, width), BF),
        jax.ShapeDtypeStruct((count, 128), F32),
        jax.ShapeDtypeStruct((count, width), F32),
        jax.ShapeDtypeStruct((rows, 2, 8, 48, length), BF),
        jax.ShapeDtypeStruct((rows, 2, 8, 48, length), BF),
        jax.ShapeDtypeStruct((count, 128), BF),
        jax.ShapeDtypeStruct((count, 128), BF),
    ]
    aliased = [] if before is None else list(before)
    first = 1 + 2 * n + 6
    return pl.pallas_call(
        functools.partial(attend_kernel, n, row, len(aliased), local),
        grid_spec=pltpu.PrefetchScalarGridSpec(
            num_scalar_prefetch=1,
            grid=(width // 256,),
            in_specs=[full(x_blocks[0].shape)] * n
            + [pl.BlockSpec((1, 16, width), lambda g, m: (0, local // 16, 0))] * n
            + [col, col, col, vec, full((16, width))]
            + [pl.BlockSpec((256, width), lambda g, m: (g, 0))]
            + [pl.BlockSpec(memory_space=pl.ANY)] * len(aliased),
            out_specs=[out_col] * 4
            + [
                pl.BlockSpec((length, 128), lambda g, m: (row, 0)),
                pl.BlockSpec((length, width), lambda g, m: (row, 0)),
                out_t,
                out_t,
                pl.BlockSpec((length, 128), lambda g, m: (row, 0)),
                pl.BlockSpec((length, 128), lambda g, m: (row, 0)),
            ],
            scratch_shapes=[
                pltpu.VMEM((length, width), BF),
                pltpu.VMEM((length, width), F32),
                pltpu.VMEM((length, width), BF),
                pltpu.VMEM((width, length), BF),
            ],
        ),
        out_shape=out_shape,
        input_output_aliases={first + i: i for i in range(len(aliased))},
        compiler_params=pltpu.CompilerParams(vmem_limit_bytes=VMEM),
        cost_estimate=LONG,
        name=f"attend_row{row}",
    )(me, *x_blocks, *seg_blocks, w["wq"], w["wk"], w["wv"], w["vec"], w["vec"], w["wo"], *aliased)


FF_STEP = 768
FF_SUB = 768
TILE = 256


def forward_kernel(n, rows, me_ref, resid_ref, wi_ref, wo_ref, vec_ref, *refs):
    up_refs, refs = refs[:n], refs[n:]
    act_out, slope_out, branch_out, grad_out, vec_out, ht_out = refs[:6]
    y_outs, refs = refs[6 : 6 + n], refs[6 + n :]
    h_s, low_s, t_s = refs
    place = me_ref[2]
    step = pl.program_id(0)
    count = resid_ref.shape[0]
    local = up_refs[0].shape[1]

    @pl.when(step == 0)
    def _():
        for first in range(0, count, TILE):
            at = slice(first, first + TILE)
            normed, _ = norm_parts(resid_ref[at, :])
            hidden = normed * vec_ref[3:4, :] + vec_ref[4:5, :]
            h_s[at, :] = hidden
            low_s[at, :] = hidden.astype(BF)
            t_s[:, at] = hidden.astype(BF).T
        for p in range(8):
            source = pl.multiple_of((place ^ dp_rel(p)) * 96, 32)
            ht_out[p * 96 : (p + 1) * 96, :] = t_s[pl.ds(source, 96), :]

    bi = vec_ref[pl.ds(8 + step, 1), :]
    spots = [
        (slice(first, first + TILE), slice(col, col + FF_SUB))
        for col in range(0, FF_STEP, FF_SUB)
        for first in range(0, count, TILE)
    ]
    project = lambda spot: dot_nn(low_s[spot[0], :], wi_ref[:, spot[1]]) + bi[:, spot[1]]
    ahead = project(spots[0])
    for i, (at, cols) in enumerate(spots):
        inner = ahead
        if i + 1 < len(spots):
            ahead = project(spots[i + 1])
        phi, rest = normal_laws(inner)
        active = (inner * phi).astype(BF)
        act_out[at, cols] = active
        slope_out[at, cols] = (phi + rest).astype(BF)
        h_s[at, :] += dot_nn(active, wo_ref[cols, :])

    @pl.when(step == pl.num_programs(0) - 1)
    def _():
        gain, shift, bias = vec_ref[5:6, :], vec_ref[6:7, :], vec_ref[7:8, :]
        sums = [jnp.zeros((1, gain.shape[1]), F32)] * 3
        for r in range(rows):
            for k in range(n):
                first = (r * n + k) * local
                at = slice(first, first + local)
                normed, inverse = norm_parts(h_s[at, :] + bias)
                up = up_refs[k][r].astype(F32)
                y_outs[k][r] = (normed * gain + shift).astype(BF)
                grad = norm_back(up * gain, normed, inverse)
                grad_out[at, :] = grad
                branch = grad.astype(BF)
                branch_out[at, :] = branch
                for i, piece in enumerate((up * normed, up, branch.astype(F32))):
                    sums[i] = sums[i] + jnp.sum(piece, 0, keepdims=True)
        vec_out[...] = jnp.zeros_like(vec_out)
        for i in range(3):
            vec_out[i : i + 1, :] = sums[i]


def forward(me, rows, resid, up_blocks, w):
    count, width = resid.shape
    n, local = len(up_blocks), up_blocks[0].shape[1]
    ff = w["wi"].shape[1]
    once = pl.Buffered(1)
    full = lambda shape: pl.BlockSpec(shape, lambda c, m: (0,) * len(shape), pipeline_mode=once)
    token = full((rows, local, width))
    return pl.pallas_call(
        functools.partial(forward_kernel, n, rows),
        grid_spec=pltpu.PrefetchScalarGridSpec(
            num_scalar_prefetch=1,
            grid=(ff // FF_STEP,),
            in_specs=[
                full((count, width)),
                pl.BlockSpec((width, FF_STEP), lambda c, m: (0, c)),
                pl.BlockSpec((FF_STEP, width), lambda c, m: (c, 0)),
                full((16, width)),
            ]
            + [token] * n,
            out_specs=[
                pl.BlockSpec((count, FF_STEP), lambda c, m: (0, c)),
                pl.BlockSpec((count, FF_STEP), lambda c, m: (0, c)),
                full((count, width)),
                full((count, width)),
                full((8, width)),
                full((width, count)),
            ]
            + [token] * n,
            scratch_shapes=[
                pltpu.VMEM((count, width), F32),
                pltpu.VMEM((count, width), BF),
                pltpu.VMEM((width, count), BF),
            ],
        ),
        out_shape=[
            jax.ShapeDtypeStruct((count, ff), BF),
            jax.ShapeDtypeStruct((count, ff), BF),
            jax.ShapeDtypeStruct((count, width), BF),
            jax.ShapeDtypeStruct((count, width), F32),
            jax.ShapeDtypeStruct((8, width), F32),
            jax.ShapeDtypeStruct((width, count), BF),
        ]
        + [jax.ShapeDtypeStruct((rows, local, width), BF)] * n,
        compiler_params=pltpu.CompilerParams(vmem_limit_bytes=VMEM),
        cost_estimate=LONG,
        name="feed_forward",
    )(me, resid, w["wi"], w["wo2"], w["vec"], *up_blocks)


def outer_kernel(me_ref, branch_ref, act_ref, keep_out, send_out, gt_s, t_s):
    me = place_of(me_ref)
    core, y, place = me

    @pl.when(pl.program_id(0) == 0)
    def _():
        t_s[...] = branch_ref[...].T
        for c in range(2):
            for yy in range(2):
                source = pl.multiple_of(((y ^ yy) * 2 + (core ^ c)) * 192, 64)
                gt_s[(c * 2 + yy) * 192 : (c * 2 + yy + 1) * 192, :] = t_s[pl.ds(source, 192), :]

    product = dot_nn(gt_s[...], act_ref[...]).astype(BF)
    for x in range(2):
        slot = x ^ (place & 1)
        for c, out in ((0, keep_out), (1, send_out)):
            for yy in range(2):
                for half in range(2):
                    first = (c * 2 + yy) * 192 + half * 96
                    out[yy, slot, 0, :, half * 384 : half * 384 + 384] = product[
                        first : first + 96, x * 384 : (x + 1) * 384
                    ]


def outer_grad(me, branch, active):
    count, width = branch.shape
    shape = (2, 2, 4, width // 8, 768)
    out_spec = pl.BlockSpec((2, 2, 1, width // 8, 768), lambda z, m: (0, 0, z, 0, 0))
    return pl.pallas_call(
        outer_kernel,
        grid_spec=pltpu.PrefetchScalarGridSpec(
            num_scalar_prefetch=1,
            grid=(4,),
            in_specs=[
                pl.BlockSpec((count, width), lambda z, m: (0, 0)),
                pl.BlockSpec((count, 768), lambda z, m: (0, (m[2] >> 1) ^ z)),
            ],
            out_specs=[out_spec, out_spec],
            scratch_shapes=[pltpu.VMEM((width, count), BF), pltpu.VMEM((width, count), BF)],
        ),
        out_shape=[jax.ShapeDtypeStruct(shape, BF)] * 2,
        compiler_params=pltpu.CompilerParams(vmem_limit_bytes=VMEM),
        cost_estimate=LONG,
        name="grad_w_outer",
    )(me, branch, active)


def backward_kernel(last, ndeps, me_ref, branch_ref, slope_ref, wi_ref, wo_ref, ht_ref, acc_ref, *refs):
    if last:
        (resid_ref, vec_ref), refs = refs[:2], refs[2:]
    refs = refs[ndeps:]
    grad_out, acc_out, bi_out = refs[:3]
    if last:
        attn_out, sums_out = refs[3:5]
    acc_s, gi_s, sem = refs[-3:]
    step = pl.program_id(0)
    count = branch_ref.shape[0]
    load = pltpu.make_async_copy(acc_ref, acc_s, sem)

    @pl.when(step == 0)
    def _():
        load.start()

    wi, wo = wi_ref[...], wo_ref[...]
    bias = jnp.zeros((1, wi.shape[1]), F32)
    ahead = dot_nt(branch_ref[0:TILE, :], wo)
    for first in range(0, count, TILE):
        at = slice(first, first + TILE)
        gi = (ahead * slope_ref[at, :].astype(F32)).astype(BF)
        if first + TILE < count:
            ahead = dot_nt(branch_ref[first + TILE : first + 2 * TILE, :], wo)
        gi_s[at, :] = gi
        bias = bias + jnp.sum(gi.astype(F32), 0, keepdims=True)
    bi_out[...] = jnp.broadcast_to(bias, bi_out.shape)
    for first in range(0, 768, 192):
        product = dot_nn(ht_ref[first : first + 192, :], gi_s[...]).astype(BF)
        for p in range(2):
            grad_out[0, first // 96 + p] = product[p * 96 : p * 96 + 96, :]

    @pl.when(step == 0)
    def _():
        load.wait()

    for first in range(0, count, TILE):
        at = slice(first, first + TILE)
        acc_s[at, :] += dot_nt(gi_s[at, :], wi)

    @pl.when(step == 1)
    def _():
        if not last:
            acc_out[...] = acc_s[...]
        else:
            gain = vec_ref[3:4, :]
            sums = [jnp.zeros(gain.shape, F32)] * 3
            for first in range(0, count, TILE):
                at = slice(first, first + TILE)
                normed, inverse = norm_parts(resid_ref[at, :])
                hidden = acc_s[at, :]
                grad = norm_back(hidden * gain, normed, inverse)
                low = grad.astype(BF)
                acc_out[at, :] = grad
                attn_out[at, :] = low
                for i, piece in enumerate((hidden * normed, hidden, low.astype(F32))):
                    sums[i] = sums[i] + jnp.sum(piece, 0, keepdims=True)
            sums_out[...] = jnp.zeros_like(sums_out)
            for i in range(3):
                sums_out[i : i + 1, :] = sums[i]


def backward(me, last, branch, slope, ht, acc, resid, w, deps):
    count, width = resid.shape
    ff = w["wi"].shape[1]
    wide = ff // 4
    once = pl.Buffered(1)
    full = lambda shape: pl.BlockSpec(shape, lambda t, m: (0,) * len(shape), pipeline_mode=once)

    def chunk(t, m):
        return (m[1] ^ t) * 2 + (m[0] ^ (0 if last else 1))

    extra = [(full((count, width)), resid), (full((16, width)), w["vec"])] if last else []
    extra_out = [((count, width), BF), ((8, width), F32)] if last else []
    return pl.pallas_call(
        functools.partial(backward_kernel, last, len(deps)),
        grid_spec=pltpu.PrefetchScalarGridSpec(
            num_scalar_prefetch=1,
            grid=(2,),
            in_specs=[
                full((count, width)),
                pl.BlockSpec((count, wide), lambda t, m: (0, chunk(t, m))),
                pl.BlockSpec((width, wide), lambda t, m: (0, chunk(t, m))),
                pl.BlockSpec((wide, width), lambda t, m: (chunk(t, m), 0)),
                full((width, count)),
                pl.BlockSpec(memory_space=pl.ANY),
            ]
            + [spec for spec, _ in extra]
            + [pl.BlockSpec(memory_space=pl.ANY)] * len(deps),
            out_specs=[
                pl.BlockSpec((1, 8, 96, wide), lambda t, m: (t, 0, 0, 0)),
                full((count, width)),
                pl.BlockSpec((8, wide), lambda t, m: (0, t)),
            ]
            + [full(shape) for shape, _ in extra_out],
            scratch_shapes=[
                pltpu.VMEM((count, width), F32),
                pltpu.VMEM((count, wide), BF),
                pltpu.SemaphoreType.DMA,
            ],
        ),
        out_shape=[
            jax.ShapeDtypeStruct((2, 8, 96, wide), BF),
            jax.ShapeDtypeStruct((count, width), F32),
            jax.ShapeDtypeStruct((8, ff // 2), F32),
        ]
        + [jax.ShapeDtypeStruct(shape, dtype) for shape, dtype in extra_out],
        compiler_params=pltpu.CompilerParams(vmem_limit_bytes=VMEM),
        cost_estimate=LONG,
        name="feed_forward_back" + ("_last" if last else ""),
    )(me, branch, slope, w["wi"], w["wo2"], ht, acc, *[a for _, a in extra], *deps)


def attend_back_kernel(part, n, last, ndeps, me_ref, *refs):
    heads, refs = refs[:8], refs[8:]
    lse_ref, attn_ref, mq_ref, mk_ref, xt_ref, acc_ref = refs[:6]
    weights, refs = refs[6:14], refs[14:]
    if part == 0:
        (ctxt_ref, shares_ref), refs = refs[:2], refs[2:]
    refs = refs[ndeps:]
    keep_out, send_out, vec_out = refs[:3]
    tok_outs, w_s = refs[3:-1], refs[-1]
    _, y, place = place_of(me_ref)
    row = pl.program_id(0)
    length = attn_ref.shape[0]
    width = attn_ref.shape[1]
    attn = attn_ref[...]
    mq, mk = mq_ref[...], mk_ref[...]
    lse_all = lse_ref[...]
    lanes = lane_of(mq.shape)
    low = lanes < 64
    spot = lanes % 64
    ones = jnp.where((spot >= 4) & (spot < 7), 1.0, 0.0).astype(BF)

    def split3(column):
        high = column.astype(BF)
        rest = column - high.astype(F32)
        middle = rest.astype(BF)
        return high, middle, (rest - middle.astype(F32)).astype(BF)

    def with_columns(base, column):
        for i, piece in enumerate(split3(-column)):
            base = jnp.where(spot == 4 + i, piece, base)
        return base

    wo = jnp.concatenate([weights[0][...], weights[1][...]], 0)
    grad_ctx = dot_nt(attn, wo).astype(BF)
    grads = [[], [], []]
    block = 256
    for pair in range(2):
        q2, k2, v2, ctx2 = (heads[2 * j + pair][...] for j in range(4))
        do2 = grad_ctx[:, pair * 128 : pair * 128 + 128]
        both = do2.astype(F32) * ctx2.astype(F32)
        dq, dk, dv = [None, None], [[], []], [[], []]
        for half in range(2):
            mine = low if half == 0 else jnp.logical_not(low)
            head = (part + 3 * pair) * 2 + half
            lse = lse_all[:, head : head + 1]
            delta = jnp.sum(jnp.where(mine, both, 0.0), -1, keepdims=True)
            q_ext = jnp.where(mine, q2, with_columns(mq, lse))
            do_ext = jnp.where(mine, do2, with_columns(jnp.zeros_like(mq), delta))
            k_ext = jnp.where(mine, k2, mk)
            v_ext = jnp.where(mine, v2, ones)
            for first in range(0, length, block):
                at = slice(first, first + block)
                prob = jnp.exp(dot_nt(k_ext[at], q_ext))
                ds = (prob * dot_nt(v_ext[at], do_ext)).astype(BF)
                dv[half].append(dot_nn(prob.astype(BF), do2))
                dk[half].append(dot_nn(ds, q2))
                add = dot_tn(ds, k2[at])
                dq[half] = add if dq[half] is None else dq[half] + add
        grads[0].append((jnp.where(low, dq[0], dq[1]) * 0.125).astype(BF))
        for j, pieces in ((1, dk), (2, dv)):
            whole = [jnp.concatenate(p, 0) for p in pieces]
            grads[j].append(jnp.where(low, whole[0], whole[1]).astype(BF))
    token = acc_ref[...]
    for j in range(3):
        grad = jnp.concatenate(grads[j], 1)
        weight = jnp.concatenate([weights[2 + 2 * j][...], weights[3 + 2 * j][...]], 1)
        token = token + dot_nt(grad, weight)
        part_w = dot_nn(xt_ref[0].reshape(width, length), grad)
        at = slice(j * 256, j * 256 + 256)

        @pl.when(row == 0)
        def _():
            w_s[:, at] = part_w

        @pl.when(row > 0)
        def _():
            w_s[:, at] += part_w

    if part == 0:
        part_w = dot_nn(ctxt_ref[0].reshape(width, length), attn)

        @pl.when(row == 0)
        def _():
            w_s[:, 768:1536] = part_w

        @pl.when(row > 0)
        def _():
            w_s[:, 768:1536] += part_w

    sums = [
        jnp.sum(jnp.concatenate(grads[j], 1).astype(F32), 0, keepdims=True) for j in (0, 2)
    ]

    @pl.when(row == 0)
    def _():
        vec_out[...] = jnp.zeros_like(vec_out)

    for i in range(2):
        vec_out[i : i + 1, :] += sums[i]

    if last:
        local = length // n
        low_token = token.astype(BF)
        for k in range(n):
            tok_outs[k][0] = low_token[k * local : (k + 1) * local, :]
    else:
        tok_outs[0][...] = token

    @pl.when(row == pl.num_programs(0) - 1)
    def _():
        columns = [[j * 256 + yy * 128 for j in range(3)] for yy in range(2)]
        if part == 0:
            columns = [c + [768 + yy * 384 + j * 128 for j in range(3)] for yy, c in enumerate(columns)]
        bias = vec_out[...]
        bias = jnp.concatenate([bias[:, :128], bias[:, 128:]], 0).astype(BF)
        for c, out in ((0, keep_out), (1, send_out)):
            for yy in range(2):
                for p in range(8):
                    for j, first in enumerate(columns[yy]):
                        out[yy ^ y, p, j * 48 : (j + 1) * 48, :] = w_s[
                            (c * 8 + p) * 48 : (c * 8 + p + 1) * 48, first : first + 128
                        ].astype(BF)
                    used = len(columns[yy]) * 48
                    out[yy, p, used : used + 16, :] = bias
                    if part == 0:
                        out[yy, p, used + 16 : used + 32, :] = shares_ref[place ^ dp_rel(p)]


def attend_back(me, part, n, rows, saved, attn, acc, w, extra, deps):
    q, k, v, ctx, lse, xt, ctxt, mq, mk = saved
    count, width = attn.shape
    length = count // rows
    local = length // n
    last = part == 2
    pair = lambda i: pl.BlockSpec((length, 128), lambda r, m: (r, part + 3 * i))
    row = lambda wide: pl.BlockSpec((length, wide), lambda r, m: (r, 0))
    w_row = lambda i: pl.BlockSpec((128, width), lambda r, m: (part + 3 * i, 0))
    w_col = lambda i: pl.BlockSpec((width, 128), lambda r, m: (0, part + 3 * i))
    t_spec = pl.BlockSpec((1, 2, 8, 48, length), lambda r, m: (r, 0, 0, 0, 0))
    shape = (2, 8, (6 if part == 0 else 3) * 48 + (32 if part == 0 else 16), 128)
    out_w = pl.BlockSpec(shape, lambda r, m: (0,) * 4)
    if last:
        tok_shape = [jax.ShapeDtypeStruct((rows, local, width), BF)] * n
        tok_spec = [pl.BlockSpec((1, local, width), lambda r, m: (r, 0, 0))] * n
        aliases = {}
    else:
        tok_shape = [jax.ShapeDtypeStruct((count, width), F32)]
        tok_spec = [row(width)]
        aliases = {1 + 8 + 5: 3}
    more = (ctxt, extra) if part == 0 else ()
    more_specs = [t_spec, pl.BlockSpec((8, 16, 128), lambda r, m: (0, 0, 0))] if part == 0 else []
    return pl.pallas_call(
        functools.partial(attend_back_kernel, part, n, last, len(deps)),
        grid_spec=pltpu.PrefetchScalarGridSpec(
            num_scalar_prefetch=1,
            grid=(rows,),
            in_specs=[pair(0), pair(1)] * 4
            + [row(128), row(width), row(128), row(128), t_spec, row(width)]
            + [w_row(0), w_row(1)]
            + [w_col(0), w_col(1)] * 3
            + more_specs
            + [pl.BlockSpec(memory_space=pl.ANY)] * len(deps),
            out_specs=[out_w, out_w, pl.BlockSpec((8, 256), lambda r, m: (0, 0))] + tok_spec,
            scratch_shapes=[pltpu.VMEM((width, 1536 if part == 0 else 768), F32)],
        ),
        out_shape=[jax.ShapeDtypeStruct(shape, BF)] * 2 + [jax.ShapeDtypeStruct((8, 256), F32)] + tok_shape,
        input_output_aliases=aliases,
        compiler_params=pltpu.CompilerParams(vmem_limit_bytes=VMEM),
        cost_estimate=LONG,
        name=f"attend_back{part}",
    )(
        me, q, q, k, k, v, v, ctx, ctx, lse, attn, mq, mk, xt, acc,
        w["wo"], w["wo"], w["wq"], w["wq"], w["wk"], w["wk"], w["wv"], w["wv"], *more, *deps,
    )


def swap(array, axis, mask):
    size = lax.axis_size(axis)
    return lax.ppermute(array, axis, [(i, i ^ mask) for i in range(size)])


def pack_tokens(place, tokens, segments, row):
    n = lax.axis_size("seq")
    own, local, width = tokens.shape[0] // n, tokens.shape[1], tokens.shape[2]

    def kernel(me_ref, seg_ref, *refs):
        for k in range(n):
            source, out = refs[k], refs[n + k]
            out[0, :local, :] = source[0]
            out[0, local:, :] = jnp.zeros((16, width), BF)
            at = (me_ref[0] ^ k) * own
            ids = jnp.concatenate([seg_ref[pl.ds(at + r, 1), :] for r in range(own)] + [seg_ref[:1, :]] * (16 - own), 0)
            out[0, local:, :local] = ids.astype(F32).astype(BF)

    return pl.pallas_call(
        kernel,
        grid_spec=pltpu.PrefetchScalarGridSpec(
            num_scalar_prefetch=1,
            grid=(1,),
            in_specs=[pl.BlockSpec(segments.shape, lambda i, m: (0, 0))]
            + [pl.BlockSpec((1, local, width), lambda i, m, k=k: ((m[0] ^ k) * own + row, 0, 0)) for k in range(n)],
            out_specs=[pl.BlockSpec((1, local + 16, width), lambda i, m: (0, 0, 0))] * n,
        ),
        out_shape=[jax.ShapeDtypeStruct((1, local + 16, width), BF)] * n,
        compiler_params=pltpu.CompilerParams(vmem_limit_bytes=VMEM),
        cost_estimate=TINY,
        name="pack_first",
    )(place, segments, *[tokens] * n)


def pack_rest(place, tokens, cotangent, first_row, deps):
    n = lax.axis_size("seq")
    own, local, width = tokens.shape[0] // n, tokens.shape[1], tokens.shape[2]
    rows = range(first_row, own)
    count = len(rows) * n + n

    def kernel(me_ref, *refs):
        for source, out in zip(refs[:count], refs[count + len(deps) :]):
            out[...] = source[...]

    one = [
        pl.BlockSpec((1, local, width), lambda i, m, k=k, r=r: ((m[0] ^ k) * own + r, 0, 0))
        for r in rows
        for k in range(n)
    ]
    many = [pl.BlockSpec((own, local, width), lambda i, m, k=k: (m[0] ^ k, 0, 0)) for k in range(n)]
    return pl.pallas_call(
        kernel,
        grid_spec=pltpu.PrefetchScalarGridSpec(
            num_scalar_prefetch=1,
            grid=(1,),
            in_specs=one + many + [pl.BlockSpec(memory_space=pl.ANY)] * len(deps),
            out_specs=[pl.BlockSpec((1, local, width), lambda i, m: (0, 0, 0))] * len(one)
            + [pl.BlockSpec((own, local, width), lambda i, m: (0, 0, 0))] * n,
        ),
        out_shape=[jax.ShapeDtypeStruct((1, local, width), BF)] * len(one)
        + [jax.ShapeDtypeStruct((own, local, width), BF)] * n,
        compiler_params=pltpu.CompilerParams(vmem_limit_bytes=VMEM),
        cost_estimate=TINY,
        name="pack_rest",
    )(place, *[tokens] * len(one), *[cotangent] * n, *deps)


def unpack(place, blocks):
    n = len(blocks)
    own, local, width = blocks[0].shape

    any_spec = pl.BlockSpec(memory_space=pl.ANY)

    def kernel(me_ref, *refs):
        sources, (out, held, sem) = refs[:n], refs[n:]
        ins = [pltpu.make_async_copy(sources[k], held.at[k], sem.at[k]) for k in range(n)]
        outs = [
            pltpu.make_async_copy(held.at[k], out.at[pl.ds((me_ref[0] ^ k) * own, own)], sem.at[n + k]) for k in range(n)
        ]
        for copy in ins:
            copy.start()
        for k in range(n):
            ins[k].wait()
            outs[k].start()
        for copy in outs:
            copy.wait()

    return pl.pallas_call(
        kernel,
        grid_spec=pltpu.PrefetchScalarGridSpec(
            num_scalar_prefetch=1,
            grid=(1,),
            in_specs=[any_spec] * n,
            out_specs=any_spec,
            scratch_shapes=[pltpu.VMEM((n, own, local, width), blocks[0].dtype), pltpu.SemaphoreType.DMA((2 * n,))],
        ),
        out_shape=jax.ShapeDtypeStruct((own * n, local, width), blocks[0].dtype),
        compiler_params=pltpu.CompilerParams(vmem_limit_bytes=VMEM),
        cost_estimate=TINY,
        name="unpack_rows",
    )(place, *blocks)


def exchange(blocks):
    return [swap(block, "seq", k) if k else block for k, block in enumerate(blocks)]


def bits_of(size):
    return [1 << b for b in range(size.bit_length() - 1)]


def reduce_matrix(grad):
    sn, dn = lax.axis_size("seq"), lax.axis_size("dp")
    ms, md = lax.axis_index("seq"), lax.axis_index("dp")
    high, wide = grad.shape[0] // dn, grad.shape[1] // sn
    blocks = grad.astype(BF).reshape(dn, high, sn, wide).transpose(2, 0, 1, 3)
    blocks = jnp.take(blocks, ms ^ jnp.arange(sn), axis=0)
    blocks = jnp.take(blocks, md ^ jnp.arange(dn), axis=1)
    left = {"seq": sn, "dp": dn}
    for axis, mask in [("seq", m) for m in bits_of(sn)] + [("dp", m) for m in bits_of(dn)]:
        size = left[axis]
        dim = 0 if axis == "seq" else 1
        split = blocks.reshape(blocks.shape[:dim] + (size // 2, 2) + blocks.shape[dim + 1 :])
        keep = lax.index_in_dim(split, 0, dim + 1, keepdims=False)
        send = lax.index_in_dim(split, 1, dim + 1, keepdims=False)
        blocks = keep + swap(send, axis, mask)
        left[axis] = size // 2
    return blocks.reshape(high, wide).astype(F32)


def reduce_vectors(vectors):
    for axis in ("seq", "dp"):
        for mask in bits_of(lax.axis_size(axis)):
            vectors = vectors + swap(vectors, axis, mask)
    return vectors


def my_share(vector):
    own = vector.shape[0] // lax.axis_size("dp")
    return lax.dynamic_slice_in_dim(vector, lax.axis_index("dp") * own, own, 0)


X, Y = ("dp", 1), ("seq", 2)


def stage(name, work, arrays, shapes, deps=(), place=None):
    scalars = [] if place is None else [place]

    def kernel(*refs):
        lead, refs = refs[: len(scalars)], refs[len(scalars) :]
        work(*lead, *refs[: len(arrays)], *refs[len(arrays) + len(deps) :])

    full = lambda shape: pl.BlockSpec(shape, lambda i, *m: (0,) * len(shape))
    return pl.pallas_call(
        kernel,
        grid_spec=pltpu.PrefetchScalarGridSpec(
            num_scalar_prefetch=len(scalars),
            grid=(1,),
            in_specs=[full(a.shape) for a in arrays] + [pl.BlockSpec(memory_space=pl.ANY)] * len(deps),
            out_specs=[full(shape) for shape, _ in shapes],
        ),
        out_shape=[jax.ShapeDtypeStruct(shape, dtype) for shape, dtype in shapes],
        compiler_params=pltpu.CompilerParams(vmem_limit_bytes=VMEM),
        cost_estimate=LONG,
        name=name,
    )(*scalars, *arrays, *deps)


def halves(kept, came, keep_out, send_out, lead, rows=None):
    tail = () if rows is None else (Ellipsis, rows, slice(None))
    for i, out in ((0, keep_out), (1, send_out)):
        at = (slice(None),) * lead + (i,) + tail
        out[...] = kept[at] + came[at]


def body(
    tokens,
    cotangent,
    segments,
    w_query,
    b_query,
    w_key,
    w_value,
    b_value,
    w_out,
    b_out,
    gain_one,
    shift_one,
    w_inner,
    b_inner,
    w_outer,
    b_outer,
    gain_two,
    shift_two,
):
    width = tokens.shape[-1]
    n, dn = lax.axis_size("seq"), lax.axis_size("dp")
    ms, md = lax.axis_index("seq"), lax.axis_index("dp")
    fast = n == 4 and dn == 8
    me = (jnp.stack([ms % 2, ms // 2, md]) if fast else jnp.zeros((3,))).astype(jnp.int32)
    seq_place = ms.astype(jnp.int32).reshape(1)
    rows, local = tokens.shape[0] // n, tokens.shape[1]
    length = n * local
    vectors = (b_query, b_value, b_out, gain_one, shift_one, gain_two, shift_two, b_outer, b_inner)
    packed = jnp.concatenate(vectors + (jnp.zeros((4 * width,), BF),)).reshape(16, width).astype(F32)
    w = dict(wq=w_query, wk=w_key, wv=w_value, wo=w_out, wi=w_inner, wo2=w_outer, vec=packed)

    first_blocks = pack_tokens(seq_place, tokens, segments, 0)
    x_blocks = [exchange(first_blocks)]
    seg_blocks = x_blocks[0]
    rest = pack_rest(seq_place, tokens, cotangent, 1, first_blocks[:1])
    for r in range(1, rows):
        x_blocks.append(exchange(rest[(r - 1) * n : r * n]))
    up_blocks = exchange(rest[(rows - 1) * n :])

    before = None
    for r in range(rows):
        before = attend(me, r, rows, x_blocks[r], seg_blocks, w, before)
    q, k, v, ctx, lse, resid, xt, ctxt, mq, mk = before
    active, slope, branch, grad2, vec2, ht, *y_blocks = forward(me, rows, resid, up_blocks, w)
    y_blocks = exchange(y_blocks)
    outer = outer_grad(me, branch, active)
    inner_send, acc, bi_send = backward(me, False, branch, slope, ht, grad2, resid, w, [outer[0]])
    saved = (q, k, v, ctx, lse, xt, ctxt, mq, mk)

    if not fast:
        inner_keep, grad1, bi_keep, attn, vec1 = backward(me, True, branch, slope, ht, acc, resid, w, [])
        shares = jnp.zeros((8, 16, 128), BF)
        early = jnp.concatenate([vec2[:3], vec1[:3]], 0)
        vec_bi = jnp.stack([bi_keep[0].reshape(2, -1), bi_send[0].reshape(2, -1)], 1).reshape(1, -1)
        parts, vec_parts = [], []
        acc = grad1
        for part in range(3):
            keep, send, vec, *tail = attend_back(me, part, n, rows, saved, attn, acc, w, shares, [])
            parts.append((keep, send))
            vec_parts.append(vec)
            acc = tail[0]
        output = unpack(seq_place, y_blocks)
        grad_tokens = unpack(seq_place, exchange(tail))
        early = reduce_vectors(jnp.concatenate([early, vec_bi[:1].reshape(4, width)], 0))
        late = jnp.stack([p[:2] for p in vec_parts], 1).reshape(2, 3, 2, 128)
        late = reduce_vectors(late.transpose(0, 2, 1, 3).reshape(2, width))
        stack = lambda pair: jnp.stack(list(pair))
        outer_t = stack(outer).reshape(2, 2, 2, 4, 96, 2, 384).transpose(1, 0, 5, 4, 3, 2, 6).reshape(width, -1)
        inner_b = stack((inner_keep, inner_send)).reshape(2, 2, 2, 4, 96, -1).transpose(3, 2, 4, 1, 0, 5)
        inner_b = inner_b.reshape(width, -1)
        three = [stack(pair)[:, :, :, -160:-16] if i else stack(pair)[:, :, :, :144] for i, pair in enumerate(parts)]
        qkv = jnp.stack(three).reshape(3, 2, 2, 2, 4, 3, 48, 128).transpose(5, 4, 3, 1, 6, 2, 0, 7).reshape(3, width, width)
        out_b = stack(parts[0])[:, :, :, 144:288].reshape(2, 2, 2, 4, 3, 48, 128).transpose(3, 2, 0, 5, 1, 4, 6)
        grad_w_outer = reduce_matrix(outer_t.T)
        grad_w_inner = reduce_matrix(inner_b)
        grad_w_out = reduce_matrix(out_b.reshape(width, width))
        grad_w_query, grad_w_key, grad_w_value = (reduce_matrix(qkv[i]) for i in range(3))
        b_query_g, b_value_g = my_share(late[0]), my_share(late[1])
        gain2_g, shift2_g, b_outer_g, gain1_g, shift1_g, b_out_g = (my_share(early[i]) for i in range(6))
        b_inner_g = my_share(early[6:10].reshape(-1))
    else:
        by_axes = lambda a: a.reshape((2, 2, 4) + a.shape[2:])
        one = lambda *shape: (shape, BF)
        top, low = slice(0, 48), slice(48, 96)
        z_swap = lambda pieces: [pieces[0]] + [swap(pieces[j], "dp", 2 * j) for j in (1, 2, 3)]
        first_shapes, second_shapes, z_shapes = [one(2, 4, 48, 768)] * 4, [one(4, 48, 768)] * 4, [one(96, 768)] * 4

        def z_split(top_keep, top_came, low_keep, low_came, outs):
            for j, out in enumerate(outs):
                out[0:48, :] = top_keep[j] + top_came[j]
                out[48:96, :] = low_keep[j] + low_came[j]

        outer_came = swap(outer[1], "seq", 1)

        def stage_a(kept, came, a_keep, a_send, b_keep, b_send):
            halves(kept, came, a_keep, a_send, 1, top)
            halves(kept, came, b_keep, b_send, 0, low)

        a_keep, a_send, b_keep, b_send = stage(
            "stage_a", stage_a, [outer[0], outer_came], first_shapes, [inner_send]
        )

        a_came, b_came = swap(a_send, *X), swap(b_send, *Y)
        inner_came = swap(inner_send, "seq", 1)
        inner_keep, grad1, bi_keep, attn, vec1 = backward(
            me, True, branch, slope, ht, acc, resid, w, [a_keep, *y_blocks]
        )

        def stage_b(
            me_ref, a_keep, a_came, b_keep, b_came, i_keep, i_came, vec2, vec1, bi_keep, bi_send,
            a2_keep, a2_send, b2_keep, b2_send, c_keep, c_send, d_keep, d_send, shares,
        ):
            halves(a_keep, a_came, a2_keep, a2_send, 0)
            halves(b_keep, b_came, b2_keep, b2_send, 0)
            halves(i_keep, i_came, c_keep, c_send, 1, top)
            halves(i_keep, i_came, d_keep, d_send, 0, low)
            early = jnp.concatenate([vec2[0:3], vec1[0:3]], 0)
            kept, sent = bi_keep[0:1], bi_send[0:1]
            blank = jnp.zeros((6, 32), F32)
            for d in range(8):
                core, y = me_ref[0], me_ref[1]
                at = slice((d % 2) * 384, (d % 2) * 384 + 384)
                other = slice(768 + at.start, 768 + at.stop)
                own_core = core == (d // 2) % 2
                own_y = y == d // 4
                piece = jnp.where(
                    own_core,
                    jnp.where(own_y, kept[:, at], kept[:, other]),
                    jnp.where(own_y, sent[:, at], sent[:, other]),
                )
                rows = [jnp.concatenate([early[:, d * 96 : d * 96 + 96], blank], 1)]
                rows += [piece[:, j * 128 : j * 128 + 128] for j in range(3)] + [jnp.zeros((7, 128), F32)]
                shares[d] = jnp.concatenate(rows, 0).astype(BF)

        *stage_b_outs, shares = stage(
            "stage_b",
            stage_b,
            [a_keep, a_came, b_keep, b_came, by_axes(inner_keep), by_axes(inner_came), vec2, vec1, bi_keep, bi_send],
            second_shapes + first_shapes + [one(8, 16, 128)],
            place=me,
        )
        a_keep, a_send, b_keep, b_send, c_keep, c_send, d_keep, d_send = stage_b_outs

        a_came, b_came = swap(a_send, *Y), swap(b_send, *X)
        c_came, d_came = swap(c_send, *X), swap(d_send, *Y)
        keep0, send0, vec_0, acc = attend_back(me, 0, n, rows, saved, attn, grad1, w, shares, [a_keep])

        def stage_c(a_keep, a_came, b_keep, b_came, c_keep, c_came, d_keep, d_came, *outs):
            z_split(a_keep, a_came, b_keep, b_came, outs[:4])
            halves(c_keep, c_came, outs[4], outs[5], 0)
            halves(d_keep, d_came, outs[6], outs[7], 0)

        *outer_z, c_keep, c_send, d_keep, d_send = stage(
            "stage_c",
            stage_c,
            [a_keep, a_came, b_keep, b_came, c_keep, c_came, d_keep, d_came],
            z_shapes + second_shapes,
            [keep0],
        )

        c_came, d_came = swap(c_send, *Y), swap(d_send, *X)
        came0 = swap(send0, "seq", 1)
        outer_z = z_swap(outer_z)
        output = unpack(seq_place, y_blocks)
        keep1, send1, vec_1, acc = attend_back(me, 1, n, rows, saved, attn, acc, w, None, [c_keep, output])

        def stage_d(c_keep, c_came, d_keep, d_came, keep0, came0, *outs):
            z_split(c_keep, c_came, d_keep, d_came, outs[:4])
            halves(keep0, came0, outs[4], outs[5], 0)

        *inner_z, p0_keep, p0_send = stage(
            "stage_d",
            stage_d,
            [c_keep, c_came, d_keep, d_came, by_axes(keep0), by_axes(came0)],
            z_shapes + [one(2, 4, 320, 128)] * 2,
            outer_z[1:],
        )

        p0_came = swap(p0_send, *Y)
        came1 = swap(send1, "seq", 1)
        inner_z = z_swap(inner_z)
        keep2, send2, vec_2, *tok_blocks = attend_back(me, 2, n, rows, saved, attn, acc, w, None, [p0_keep])

        came2 = swap(send2, "seq", 1)
        tok_blocks = exchange(tok_blocks)
        add = lambda four: sum(r[...].astype(F32) for r in four)
        x_split = lambda kept, came, a, b: halves(kept, came, a, b, 1)
        y_split = lambda kept, came, a, b: halves(kept, came, a, b, 0)
        quarter, eighth = [one(2, 4, 160, 128)] * 2, [one(4, 160, 128)] * 2
        p1_keep, p1_send = stage(
            "stage_e", x_split, [by_axes(keep1), by_axes(came1)], quarter, [keep2]
        )
        p1_came = swap(p1_send, *X)
        p2_keep, p2_send = stage(
            "stage_f", x_split, [by_axes(keep2), by_axes(came2)], quarter, [p1_keep]
        )
        p2_came = swap(p2_send, *X)
        p0_keep, p0_send = stage(
            "stage_g", y_split, [p0_keep, p0_came], [one(4, 320, 128)] * 2, [p2_keep, *inner_z[1:]]
        )
        p0_came = swap(p0_send, *X)

        def forward_grads(*refs):
            refs[9][...] = add(refs[4:8])
            outer_z = add(refs[0:4])
            refs[8][:, 0:96] = outer_z[:, :384].T
            refs[8][:, 96:192] = outer_z[:, 384:].T

        grad_w_outer, grad_w_inner = stage(
            "forward_grads", forward_grads, outer_z + inner_z, [((384, 192), F32), ((96, 768), F32)], [p0_keep]
        )

        def stage_h(p1_keep, p1_came, p2_keep, p2_came, keep, send):
            for i, out in ((0, keep), (1, send)):
                out[:, 0:160, :] = p1_keep[i] + p1_came[i]
                out[:, 160:320, :] = p2_keep[i] + p2_came[i]

        p12_keep, p12_send = stage(
            "stage_h",
            stage_h,
            [p1_keep, p1_came, p2_keep, p2_came],
            [one(4, 320, 128)] * 2,
            [grad_w_inner, tok_blocks[2]],
        )
        p12_came = swap(p12_send, *Y)

        def stage_i(p0_keep, p0_came, p12_keep, p12_came, *outs):
            for j in range(4):
                outs[j][0:320, :] = p0_keep[j] + p0_came[j]
                outs[j][320:640, :] = p12_keep[j] + p12_came[j]

        z_pieces = z_swap(
            stage("stage_i", stage_i, [p0_keep, p0_came, p12_keep, p12_came], [one(640, 128)] * 4, [tok_blocks[3]])
        )
        grad_tokens = unpack(seq_place, tok_blocks)

        def gather_up(me_ref, *refs):
            total = add(refs[0:4])
            z0, z12 = total[0:320], total[320:640]
            mine, other, bq_out, bv_out, bi_out, *vec_outs = refs[4:]
            place = me_ref[2]
            for i, out in enumerate(vec_outs):
                out[...] = z0[304 + i : 305 + i, 0:96]
            bi_out[...] = jnp.concatenate([z0[310 + j : 311 + j] for j in range(3)], 1)
            first_rows = [z0[288:304], z12[144:160], z12[304:320]]
            for i, out in enumerate((bq_out, bv_out)):
                whole = [first_rows[j % 3][(j // 3) * 8 + i : (j // 3) * 8 + i + 1] for j in range(6)]
                whole = jnp.concatenate(whole, 1)
                total = jnp.zeros((1, 96), F32)
                for d in range(8):
                    total = jnp.where(place == d, whole[:, d * 96 : d * 96 + 96], total)
                out[...] = total
            rows = lambda z, first: [z[first + 48 * j : first + 48 * j + 48] for j in range(3)]
            out_w = rows(z0, 144)
            parts = [rows(z0, 0), rows(z12, 0), rows(z12, 160)]
            for i in range(4):
                pieces = out_w if i == 0 else [part[i - 1] for part in parts]
                whole = jnp.concatenate(pieces, 1)
                left, right = whole[:, :192], whole[:, 192:]
                first = me_ref[0] == 0
                mine[i] = jnp.where(first, left, right)
                other[i] = jnp.where(first, right, left).astype(BF)

        mine, other, b_query_g, b_value_g, b_inner_g, *vecs = stage(
            "gather_up",
            gather_up,
            z_pieces,
            [((4, 48, 192), F32), ((4, 48, 192), BF), ((1, 96), F32), ((1, 96), F32), ((1, 384), F32)]
            + [((1, 96), F32)] * 6,
            place=me,
        )
        other = swap(other, "seq", 1)

        def assemble(me_ref, mine, other, *outs):
            for i, out in enumerate(outs):
                kept, came = mine[i], other[i].astype(F32)
                first = me_ref[0] == 0
                out[0:48, :] = jnp.where(first, kept, came)
                out[48:96, :] = jnp.where(first, came, kept)

        grad_w_out, grad_w_query, grad_w_key, grad_w_value = stage(
            "assemble", assemble, [mine, other], [((96, 192), F32)] * 4, place=me
        )
        b_query_g, b_value_g, b_inner_g = (v.reshape(-1) for v in (b_query_g, b_value_g, b_inner_g))
        gain2_g, shift2_g, b_outer_g, gain1_g, shift1_g, b_out_g = (v.reshape(-1) for v in vecs)

    return (
        output,
        grad_tokens,
        grad_w_query,
        b_query_g,
        grad_w_key,
        grad_w_value,
        b_value_g,
        grad_w_out,
        b_out_g,
        gain1_g,
        shift1_g,
        grad_w_inner,
        b_inner_g,
        grad_w_outer,
        b_outer_g,
        gain2_g,
        shift2_g,
    )


def solution(mesh):
    token = P("dp", "seq", None)
    matrix = P("dp", "seq")
    vector = P("dp")
    return jax.shard_map(
        body,
        mesh=mesh,
        in_specs=(token, token, P("dp", "seq")) + (P(),) * 15,
        out_specs=(
            token,
            token,
            matrix,
            vector,
            matrix,
            matrix,
            vector,
            matrix,
            vector,
            vector,
            vector,
            matrix,
            vector,
            matrix,
            vector,
            vector,
            vector,
        ),
        check_vma=False,
    )
```

```python
import functools

import jax
import jax.numpy as jnp
from jax import lax
from jax.experimental import pallas as pl
from jax.experimental.pallas import tpu as pltpu
from jax.sharding import PartitionSpec as P

HEADS = 12
BF = jnp.bfloat16
F32 = jnp.float32
MIB = 1 << 20
VMEM = 60 * MIB
LONG = pl.CostEstimate(flops=60_000_000_000, bytes_accessed=1, transcendentals=0)
TINY = pl.CostEstimate(flops=1, bytes_accessed=1, transcendentals=0)


def dot_nn(a, b):
    return lax.dot_general(a, b, (((1,), (0,)), ((), ())), preferred_element_type=F32)


def dot_nt(a, b):
    return lax.dot_general(a, b, (((1,), (1,)), ((), ())), preferred_element_type=F32)


def dot_tn(a, b):
    return lax.dot_general(a, b, (((0,), (0,)), ((), ())), preferred_element_type=F32)


def normal_laws(a):
    gauss = jnp.exp(a * a * -0.5)
    return 0.5 + 0.5 * lax.erf(a * 0.7071067811865476), a * (gauss * 0.3989422804014327)


def norm_parts(values):
    mean = jnp.mean(values, -1, keepdims=True)
    centred = values - mean
    inverse = lax.rsqrt(jnp.mean(centred * centred, -1, keepdims=True) + 1e-05)
    return centred * inverse, inverse


def norm_back(scaled, normed, inverse):
    return inverse * (
        scaled
        - jnp.mean(scaled, -1, keepdims=True)
        - normed * jnp.mean(scaled * normed, -1, keepdims=True)
    )


def lane_of(shape):
    return lax.broadcasted_iota(jnp.int32, shape, 1)


def place_of(me_ref):
    return me_ref[0], me_ref[1], me_ref[2]


def dp_rel(position):
    return (position % 4) * 2 + position // 4


def split_rows(position_c, position_d, me):
    core, _, place = me
    return pl.multiple_of((place ^ dp_rel(position_d)) * 96 + (core ^ position_c) * 48, 16)


def attend_kernel(n, row, aliased, local, me_ref, *refs):
    x_refs, refs = refs[:n], refs[n:]
    seg_refs, refs = refs[:n], refs[n:]
    wq_ref, wk_ref, wv_ref, vec_ref, vecs_ref, wo_ref = refs[:6]
    refs = refs[6 + aliased :]
    q_out, k_out, v_out, ctx_out, lse_out, resid_out, xt_out, ctxt_out, mq_out, mk_out = refs[:10]
    x_s, acc_s, ctx_s, t_s = refs[10:]
    step = pl.program_id(0)
    me = place_of(me_ref)

    @pl.when(step == 0)
    def _():
        for k in range(n):
            x_s[k * local : (k + 1) * local, :] = x_refs[k][0, :local, :]
        lse_out[...] = jnp.zeros_like(lse_out)
        seg = jnp.concatenate([ref[0, :, :local].astype(F32)[row : row + 1] for ref in seg_refs], 1)
        spot = lax.broadcasted_iota(jnp.int32, (128, seg.shape[1]), 0) % 64
        same = spot.astype(F32) == seg
        mq_out[...] = jnp.where(same, -1e30, 0.0).T.astype(BF)
        mk_out[...] = jnp.where((spot < 7) & jnp.logical_not(same), 1.0, 0.0).T.astype(BF)

    x = x_s[...]
    q = ((dot_nn(x, wq_ref[...]) + vec_ref[0:1, :]).astype(BF).astype(F32) * 0.125).astype(BF)
    kk = dot_nn(x, wk_ref[...]).astype(BF)
    v = (dot_nn(x, wv_ref[...]) + vec_ref[1:2, :]).astype(BF)
    q_out[...] = q
    k_out[...] = kk
    v_out[...] = v
    mq, mk = mq_out[...], mk_out[...]
    low = lane_of(mq.shape) < 64
    stats = lse_out[...]
    lanes = lane_of(stats.shape)

    def scores(head):
        cols = slice(head // 2 * 128, head // 2 * 128 + 128)
        mine = low if head % 2 == 0 else jnp.logical_not(low)
        return dot_nt(jnp.where(mine, q[:, cols], mq), jnp.where(mine, kk[:, cols], mk))

    heads = []
    ahead = scores(0)
    for head in range(4):
        s = ahead
        if head < 3:
            ahead = scores(head + 1)
        top = jnp.max(s, -1, keepdims=True)
        e = jnp.exp(s - top)
        total = jnp.sum(e, -1, keepdims=True)
        v2 = v[:, head // 2 * 128 : head // 2 * 128 + 128]
        heads.append(dot_nn(e.astype(BF), v2) * (1.0 / total))
        stats = jnp.where(lanes == step * 4 + head, top + jnp.log(total), stats)
    parts = [jnp.where(low, heads[i], heads[i + 1]).astype(BF) for i in (0, 2)]
    lse_out[...] = stats
    ctx = jnp.concatenate(parts, 1)
    ctx_out[...] = ctx
    ctx_s[:, pl.ds(pl.multiple_of(step * 256, 256), 256)] = ctx
    add = dot_nn(ctx, wo_ref[...])

    @pl.when(step == 0)
    def _():
        acc_s[...] = add

    @pl.when(step == 1)
    def _():
        acc_s[...] += add

    @pl.when(step == 2)
    def _():
        resid_out[...] = x_s[...].astype(F32) + (acc_s[...] + add) + vecs_ref[2:3, :]
        for source, target in ((x_s, xt_out), (ctx_s, ctxt_out)):
            t_s[...] = source[...].T
            for c in range(2):
                for d in range(8):
                    target[0, c, d] = t_s[pl.ds(split_rows(c, d, me), 48), :]


def attend(me, row, rows, x_blocks, seg_blocks, w, before):
    n, local, width = len(x_blocks), seg_blocks[0].shape[1] - 16, x_blocks[0].shape[2]
    length = n * local
    count = rows * length
    full = lambda shape: pl.BlockSpec(shape, lambda g, m: (0,) * len(shape))
    col = pl.BlockSpec((width, 256), lambda g, m: (0, g))
    vec = pl.BlockSpec((16, 256), lambda g, m: (0, g))
    out_col = pl.BlockSpec((length, 256), lambda g, m: (row, g))
    out_t = pl.BlockSpec((1, 2, 8, 48, length), lambda g, m: (row, 0, 0, 0, 0))
    out_shape = [
        jax.ShapeDtypeStruct((count, width), BF),
        jax.ShapeDtypeStruct((count, width), BF),
        jax.ShapeDtypeStruct((count, width), BF),
        jax.ShapeDtypeStruct((count, width), BF),
        jax.ShapeDtypeStruct((count, 128), F32),
        jax.ShapeDtypeStruct((count, width), F32),
        jax.ShapeDtypeStruct((rows, 2, 8, 48, length), BF),
        jax.ShapeDtypeStruct((rows, 2, 8, 48, length), BF),
        jax.ShapeDtypeStruct((count, 128), BF),
        jax.ShapeDtypeStruct((count, 128), BF),
    ]
    aliased = [] if before is None else list(before)
    first = 1 + 2 * n + 6
    return pl.pallas_call(
        functools.partial(attend_kernel, n, row, len(aliased), local),
        grid_spec=pltpu.PrefetchScalarGridSpec(
            num_scalar_prefetch=1,
            grid=(width // 256,),
            in_specs=[full(x_blocks[0].shape)] * n
            + [pl.BlockSpec((1, 16, width), lambda g, m: (0, local // 16, 0))] * n
            + [col, col, col, vec, full((16, width))]
            + [pl.BlockSpec((256, width), lambda g, m: (g, 0))]
            + [pl.BlockSpec(memory_space=pl.ANY)] * len(aliased),
            out_specs=[out_col] * 4
            + [
                pl.BlockSpec((length, 128), lambda g, m: (row, 0)),
                pl.BlockSpec((length, width), lambda g, m: (row, 0)),
                out_t,
                out_t,
                pl.BlockSpec((length, 128), lambda g, m: (row, 0)),
                pl.BlockSpec((length, 128), lambda g, m: (row, 0)),
            ],
            scratch_shapes=[
                pltpu.VMEM((length, width), BF),
                pltpu.VMEM((length, width), F32),
                pltpu.VMEM((length, width), BF),
                pltpu.VMEM((width, length), BF),
            ],
        ),
        out_shape=out_shape,
        input_output_aliases={first + i: i for i in range(len(aliased))},
        compiler_params=pltpu.CompilerParams(vmem_limit_bytes=VMEM),
        cost_estimate=LONG,
        name=f"attend_row{row}",
    )(me, *x_blocks, *seg_blocks, w["wq"], w["wk"], w["wv"], w["vec"], w["vec"], w["wo"], *aliased)


CHUNK = 768
TILE = 256


def lines(index, size):
    return pl.ds(pl.multiple_of(index * size, size), size)


def forward_kernel(
    n, rows, me_ref, vec_ref, resid_ref, wi_ref, wo_ref, *refs,
):
    up_refs, refs = refs[:n], refs[n:]
    slope_out, branch_out, grad_out, ht_out, keep_out, send_out, vec_out = refs[:7]
    y_outs, refs = refs[7 : 7 + n], refs[7 + n :]
    h_s, low_s, wi_s, wo_s, act_s, slope_s, up_s, y_s, t_s, ht_s, branch_s, gt_s, keep_s, send_s, sem = refs
    core, y, place = place_of(me_ref)
    count, width = h_s.shape
    local = up_s.shape[2]
    tiles, chunks = count // TILE, wi_s.shape[1] // CHUNK
    move = pltpu.make_async_copy
    at_wi, at_wo, at_up = tiles, tiles + chunks, tiles + chunks + 1
    at_out = at_up + n
    resid_in = lambda i: move(resid_ref.at[lines(i, TILE)], h_s.at[lines(i, TILE)], sem.at[i])
    wi_in = lambda c: move(wi_ref.at[:, lines(c, CHUNK)], wi_s.at[:, lines(c, CHUNK)], sem.at[at_wi + c])
    wo_in = move(wo_ref, wo_s, sem.at[at_wo])
    up_in = [move(up_refs[k], up_s.at[k], sem.at[at_up + k]) for k in range(n)]
    slope_to = lambda c: move(slope_s.at[:, lines(c, CHUNK)], slope_out.at[:, lines(c, CHUNK)], sem.at[at_out + c])
    keep_to = lambda z: move(keep_s.at[:, :, z], keep_out.at[:, :, z], sem.at[at_out + chunks + z])
    send_to = lambda z: move(send_s.at[:, :, z], send_out.at[:, :, z], sem.at[at_out + chunks + 4 + z])
    at_late = at_out + chunks + 8
    ht_to = move(ht_s, ht_out, sem.at[at_late])
    late = []

    for i in range(tiles):
        resid_in(i).start()
    for c in range(chunks):
        wi_in(c).start()
    wo_in.start()
    for copy in up_in:
        copy.start()

    def first_norm(i, carry):
        at = lines(i, TILE)
        resid_in(i).wait()
        normed, _ = norm_parts(h_s[at, :])
        hidden = normed * vec_ref[3:4, :] + vec_ref[4:5, :]
        h_s[at, :] = hidden
        low = hidden.astype(BF)
        low_s[at, :] = low
        t_s[:, at] = low.T
        return carry

    lax.fori_loop(0, tiles, first_norm, 0)
    for p in range(8):
        source = pl.multiple_of((place ^ dp_rel(p)) * 96, 32)
        ht_s[p * 96 : (p + 1) * 96, :] = t_s[pl.ds(source, 96), :]
    ht_to.start()

    def hidden_chunk(c, carry):
        cols = lines(c, CHUNK)
        wi_in(c).wait()
        bias = vec_ref[pl.ds(8 + c, 1), :]
        project = lambda i: dot_nn(low_s[i * TILE : (i + 1) * TILE, :], wi_s[:, cols]) + bias
        ahead = project(0)
        for i in range(tiles):
            inner = ahead
            if i + 1 < tiles:
                ahead = project(i + 1)
            phi, rest = normal_laws(inner)
            act_s[i * TILE : (i + 1) * TILE, cols] = (inner * phi).astype(BF)
            slope_s[i * TILE : (i + 1) * TILE, cols] = (phi + rest).astype(BF)
        slope_to(c).start()
        return carry

    lax.fori_loop(0, chunks, hidden_chunk, 0)
    wo_in.wait()
    for copy in up_in:
        copy.wait()
    gain, shift, bias = vec_ref[5:6, :], vec_ref[6:7, :], vec_ref[7:8, :]
    sums = [jnp.zeros((1, width), F32)] * 3
    second = lambda i: dot_nn(act_s[i * TILE : (i + 1) * TILE, :], wo_s[...])
    ahead = second(0)
    per_tile = TILE // local
    for i in range(tiles):
        product = ahead
        if i + 1 < tiles:
            ahead = second(i + 1)
        for j in range(per_tile):
            block = i * per_tile + j
            r, k = block // n, block % n
            at = slice(block * local, (block + 1) * local)
            normed, inverse = norm_parts(h_s[at, :] + product[j * local : (j + 1) * local] + bias)
            up = up_s[k, r].astype(F32)
            y_s[k, r] = (normed * gain + shift).astype(BF)
            grad = norm_back(up * gain, normed, inverse)
            h_s[at, :] = grad
            branch = grad.astype(BF)
            branch_s[at, :] = branch
            t_s[:, at] = branch.T
            for q, piece in enumerate((up * normed, up, branch.astype(F32))):
                sums[q] = sums[q] + jnp.sum(piece, 0, keepdims=True)
    late += [move(h_s, grad_out, sem.at[at_late + 1]), move(branch_s, branch_out, sem.at[at_late + 2])]
    late += [move(y_s.at[k], y_outs[k], sem.at[at_late + 3 + k]) for k in range(n)]
    for copy in late:
        copy.start()
    vec_out[...] = jnp.concatenate(sums + [jnp.zeros((5, width), F32)], 0)
    for c in range(2):
        for yy in range(2):
            source = pl.multiple_of(((y ^ yy) * 2 + (core ^ c)) * 192, 64)
            gt_s[(c * 2 + yy) * 192 : (c * 2 + yy + 1) * 192, :] = t_s[pl.ds(source, 192), :]

    def outer_grad(z, carry):
        cols = lines((place >> 1) ^ z, 768)
        for c, out in ((1, send_s), (0, keep_s)):
            for yy in range(2):
                first = (c * 2 + yy) * 192
                product = dot_nn(gt_s[first : first + 192, :], act_s[:, cols]).astype(BF)
                for x in range(2):
                    for half in range(2):
                        out[yy, x ^ (place & 1), z, :, half * 384 : half * 384 + 384] = product[
                            half * 96 : half * 96 + 96, x * 384 : (x + 1) * 384
                        ]
        send_to(z).start()
        keep_to(z).start()
        return carry

    lax.fori_loop(0, 4, outer_grad, 0)
    ht_to.wait()
    for copy in late:
        copy.wait()
    for c in range(chunks):
        slope_to(c).wait()
    for z in range(4):
        send_to(z).wait()
        keep_to(z).wait()


def forward(me, rows, resid, up_blocks, w):
    count, width = resid.shape
    n, local = len(up_blocks), up_blocks[0].shape[1]
    ff = w["wi"].shape[1]
    any_spec = pl.BlockSpec(memory_space=pl.ANY)
    blocks = (2, 2, 4, 96, 768)
    out_shape = [
        ((count, ff), BF),
        ((count, width), BF),
        ((count, width), F32),
        ((width, count), BF),
        (blocks, BF),
        (blocks, BF),
        ((8, width), F32),
    ] + [((rows, local, width), BF)] * n
    specs = [any_spec] * len(out_shape)
    specs[6] = pl.BlockSpec((8, width), lambda i, m: (0, 0))
    semaphores = count // TILE + ff // CHUNK + 1 + n + ff // CHUNK + 8 + 3 + n
    return pl.pallas_call(
        functools.partial(forward_kernel, n, rows),
        grid_spec=pltpu.PrefetchScalarGridSpec(
            num_scalar_prefetch=1,
            grid=(1,),
            in_specs=[pl.BlockSpec((16, width), lambda i, m: (0, 0))] + [any_spec] * (3 + n),
            out_specs=specs,
            scratch_shapes=[
                pltpu.VMEM((count, width), F32),
                pltpu.VMEM((count, width), BF),
                pltpu.VMEM((width, ff), BF),
                pltpu.VMEM((ff, width), BF),
                pltpu.VMEM((count, ff), BF),
                pltpu.VMEM((count, ff), BF),
                pltpu.VMEM((n, rows, local, width), BF),
                pltpu.VMEM((n, rows, local, width), BF),
                pltpu.VMEM((width, count), BF),
                pltpu.VMEM((width, count), BF),
                pltpu.VMEM((count, width), BF),
                pltpu.VMEM((width, count), BF),
                pltpu.VMEM(blocks, BF),
                pltpu.VMEM(blocks, BF),
                pltpu.SemaphoreType.DMA((semaphores,)),
            ],
        ),
        out_shape=[jax.ShapeDtypeStruct(shape, dtype) for shape, dtype in out_shape],
        compiler_params=pltpu.CompilerParams(vmem_limit_bytes=VMEM),
        cost_estimate=LONG,
        name="feed_forward",
    )(me, w["vec"], resid, w["wi"], w["wo2"], *up_blocks)


def backward_kernel(last, ndeps, me_ref, vec_ref, branch_ref, slope_ref, wi_ref, wo_ref, ht_ref, *refs):
    if last:
        (resid_ref, grad2_ref, partial_ref), refs = refs[:3], refs[3:]
    refs = refs[ndeps:]
    grad_out, acc_out, bi_out = refs[:3]
    refs = refs[3:]
    if last:
        (attn_out, sums_out, resid_s, grad2_s, attn_s), refs = refs[:5], refs[5:]
    branch_s, slope_s, wi_s, wo_s, ht_s, gi_s, acc_s, grad_s, sem = refs
    core, y, _ = place_of(me_ref)
    count, width = branch_s.shape
    tiles = count // TILE
    move = pltpu.make_async_copy
    chunk = lambda c: lines((y ^ c) * 2 + (core ^ (0 if last else 1)), CHUNK)
    branch_in, ht_in = move(branch_ref, branch_s, sem.at[0]), move(ht_ref, ht_s, sem.at[1])
    wo_in = lambda c: move(wo_ref.at[chunk(c)], wo_s.at[lines(c, CHUNK)], sem.at[2 + c])
    slope_in = lambda c: move(slope_ref.at[:, chunk(c)], slope_s.at[:, lines(c, CHUNK)], sem.at[4 + c])
    wi_in = lambda c: move(wi_ref.at[:, chunk(c)], wi_s.at[:, lines(c, CHUNK)], sem.at[6 + c])
    grad_to = lambda c: move(grad_s.at[c], grad_out.at[c], sem.at[8 + c])
    acc_to = lambda i: move(acc_s.at[lines(i, TILE)], acc_out.at[lines(i, TILE)], sem.at[10 + i])
    attn_to = lambda i: move(attn_s.at[lines(i, TILE)], attn_out.at[lines(i, TILE)], sem.at[10 + tiles + i])
    late_in = []
    if last:
        late_in = [move(partial_ref, acc_s, sem.at[10 + 2 * tiles])]
        late_in += [move(grad2_ref, grad2_s, sem.at[11 + 2 * tiles]), move(resid_ref, resid_s, sem.at[12 + 2 * tiles])]

    branch_in.start()
    wo_in(0).start()
    slope_in(0).start()
    ht_in.start()
    wo_in(1).start()
    slope_in(1).start()
    wi_in(0).start()
    wi_in(1).start()
    for copy in late_in:
        copy.start()
    branch_in.wait()

    def hidden_chunk(c, carry):
        cols = lines(c, CHUNK)
        wo_in(c).wait()
        slope_in(c).wait()
        back = lambda i: dot_nt(branch_s[i * TILE : (i + 1) * TILE, :], wo_s[cols, :])
        bias = jnp.zeros((1, CHUNK), F32)
        ahead = back(0)
        for i in range(tiles):
            at = slice(i * TILE, (i + 1) * TILE)
            gi = (ahead * slope_s[at, cols].astype(F32)).astype(BF)
            if i + 1 < tiles:
                ahead = back(i + 1)
            gi_s[at, cols] = gi
            bias = bias + jnp.sum(gi.astype(F32), 0, keepdims=True)
        bi_out[:, cols] = jnp.broadcast_to(bias, (8, CHUNK))

        @pl.when(c == 0)
        def _():
            ht_in.wait()

        for first in range(0, width, 192):
            product = dot_nn(ht_s[first : first + 192, :], gi_s[:, cols]).astype(BF)
            for p in range(2):
                grad_s[c, first // 96 + p] = product[p * 96 : p * 96 + 96, :]
        grad_to(c).start()
        return carry

    lax.fori_loop(0, 2, hidden_chunk, 0)
    wi_in(0).wait()
    wi_in(1).wait()
    for copy in late_in:
        copy.wait()
    gain = vec_ref[3:4, :]
    sums = [jnp.zeros((1, width), F32)] * 3
    back = lambda i: dot_nt(gi_s[i * TILE : (i + 1) * TILE, :], wi_s[...])
    ahead = back(0)
    for i in range(tiles):
        at = slice(i * TILE, (i + 1) * TILE)
        hidden = ahead
        if i + 1 < tiles:
            ahead = back(i + 1)
        if last:
            hidden = hidden + acc_s[at, :] + grad2_s[at, :]
            normed, inverse = norm_parts(resid_s[at, :])
            grad = norm_back(hidden * gain, normed, inverse)
            low = grad.astype(BF)
            acc_s[at, :] = grad
            attn_s[at, :] = low
            for q, piece in enumerate((hidden * normed, hidden, low.astype(F32))):
                sums[q] = sums[q] + jnp.sum(piece, 0, keepdims=True)
            attn_to(i).start()
        else:
            acc_s[at, :] = hidden
        acc_to(i).start()
    if last:
        sums_out[...] = jnp.concatenate(sums + [jnp.zeros((5, width), F32)], 0)
    for i in range(tiles):
        acc_to(i).wait()
        if last:
            attn_to(i).wait()
    for c in range(2):
        grad_to(c).wait()


def backward(me, last, branch, slope, ht, w, more, deps):
    count, width = branch.shape
    ff = w["wi"].shape[1]
    any_spec = pl.BlockSpec(memory_space=pl.ANY)
    row = lambda wide: pl.BlockSpec((8, wide), lambda i, m: (0, 0))
    out_shape = [((2, 8, 96, CHUNK), BF), ((count, width), F32), ((8, ff // 2), F32)]
    out_specs = [any_spec, any_spec, row(ff // 2)]
    scratch = []
    if last:
        out_shape += [((count, width), BF), ((8, width), F32)]
        out_specs += [any_spec, row(width)]
        scratch = [pltpu.VMEM((count, width), F32), pltpu.VMEM((count, width), F32), pltpu.VMEM((count, width), BF)]
    return pl.pallas_call(
        functools.partial(backward_kernel, last, len(deps)),
        grid_spec=pltpu.PrefetchScalarGridSpec(
            num_scalar_prefetch=1,
            grid=(1,),
            in_specs=[pl.BlockSpec((16, width), lambda i, m: (0, 0))] + [any_spec] * (5 + len(more) + len(deps)),
            out_specs=out_specs,
            scratch_shapes=scratch
            + [
                pltpu.VMEM((count, width), BF),
                pltpu.VMEM((count, 2 * CHUNK), BF),
                pltpu.VMEM((width, 2 * CHUNK), BF),
                pltpu.VMEM((2 * CHUNK, width), BF),
                pltpu.VMEM((width, count), BF),
                pltpu.VMEM((count, 2 * CHUNK), BF),
                pltpu.VMEM((count, width), F32),
                pltpu.VMEM((2, 8, 96, CHUNK), BF),
                pltpu.SemaphoreType.DMA((13 + 2 * (count // TILE),)),
            ],
        ),
        out_shape=[jax.ShapeDtypeStruct(shape, dtype) for shape, dtype in out_shape],
        compiler_params=pltpu.CompilerParams(vmem_limit_bytes=VMEM),
        cost_estimate=LONG,
        name="feed_forward_back" + ("_last" if last else ""),
    )(me, w["vec"], branch, slope, w["wi"], w["wo2"], ht, *more, *deps)


def attend_back_kernel(part, n, last, ndeps, me_ref, *refs):
    heads, refs = refs[:8], refs[8:]
    lse_ref, attn_ref, mq_ref, mk_ref, xt_ref, acc_ref = refs[:6]
    weights, refs = refs[6:14], refs[14:]
    if part == 0:
        (ctxt_ref, shares_ref), refs = refs[:2], refs[2:]
    refs = refs[ndeps:]
    keep_out, send_out, vec_out = refs[:3]
    tok_outs, w_s = refs[3:-1], refs[-1]
    _, y, place = place_of(me_ref)
    row = pl.program_id(0)
    length = attn_ref.shape[0]
    width = attn_ref.shape[1]
    attn = attn_ref[...]
    mq, mk = mq_ref[...], mk_ref[...]
    lse_all = lse_ref[...]
    lanes = lane_of(mq.shape)
    low = lanes < 64
    spot = lanes % 64
    ones = jnp.where((spot >= 4) & (spot < 7), 1.0, 0.0).astype(BF)

    def split3(column):
        high = column.astype(BF)
        rest = column - high.astype(F32)
        middle = rest.astype(BF)
        return high, middle, (rest - middle.astype(F32)).astype(BF)

    def with_columns(base, column):
        for i, piece in enumerate(split3(-column)):
            base = jnp.where(spot == 4 + i, piece, base)
        return base

    wo = jnp.concatenate([weights[0][...], weights[1][...]], 0)
    grad_ctx = dot_nt(attn, wo).astype(BF)
    block = 256
    items = [(pair, half, first) for pair in range(2) for half in range(2) for first in range(0, length, block)]
    pairs, halves_of = [], {}
    for pair in range(2):
        q2, k2, v2, ctx2 = (heads[2 * j + pair][...] for j in range(4))
        do2 = grad_ctx[:, pair * 128 : pair * 128 + 128]
        pairs.append((q2, k2, v2, do2, do2.astype(F32) * ctx2.astype(F32)))

    def operands(pair, half):
        if (pair, half) not in halves_of:
            q2, k2, v2, do2, both = pairs[pair]
            mine = low if half == 0 else jnp.logical_not(low)
            head = (part + 3 * pair) * 2 + half
            delta = jnp.sum(jnp.where(mine, both, 0.0), -1, keepdims=True)
            halves_of[pair, half] = (
                jnp.where(mine, q2, with_columns(mq, lse_all[:, head : head + 1])),
                jnp.where(mine, do2, with_columns(jnp.zeros_like(mq), delta)),
                jnp.where(mine, k2, mk),
                jnp.where(mine, v2, ones),
            )
        return halves_of[pair, half]

    def products(pair, half, first):
        q_ext, do_ext, k_ext, v_ext = operands(pair, half)
        at = slice(first, first + block)
        return dot_nt(k_ext[at], q_ext), dot_nt(v_ext[at], do_ext)

    dq, dk, dv = {}, {}, {}
    ahead = products(*items[0])
    for i, (pair, half, first) in enumerate(items):
        power, slope = ahead
        if i + 1 < len(items):
            ahead = products(*items[i + 1])
        q2, k2, _, do2, _ = pairs[pair]
        prob = jnp.exp(power)
        ds = (prob * slope).astype(BF)
        key = (pair, half)
        dv.setdefault(key, []).append(dot_nn(prob.astype(BF), do2))
        dk.setdefault(key, []).append(dot_nn(ds, q2))
        add = dot_tn(ds, k2[first : first + block])
        dq[key] = dq[key] + add if key in dq else add
    grads = [[], [], []]
    for pair in range(2):
        grads[0].append((jnp.where(low, dq[pair, 0], dq[pair, 1]) * 0.125).astype(BF))
        for j, pieces in ((1, dk), (2, dv)):
            whole = [jnp.concatenate(pieces[pair, half], 0) for half in range(2)]
            grads[j].append(jnp.where(low, whole[0], whole[1]).astype(BF))
    token = acc_ref[...]
    for j in range(3):
        grad = jnp.concatenate(grads[j], 1)
        weight = jnp.concatenate([weights[2 + 2 * j][...], weights[3 + 2 * j][...]], 1)
        token = token + dot_nt(grad, weight)
        part_w = dot_nn(xt_ref[0].reshape(width, length), grad)
        at = slice(j * 256, j * 256 + 256)

        @pl.when(row == 0)
        def _():
            w_s[:, at] = part_w

        @pl.when(row > 0)
        def _():
            w_s[:, at] += part_w

    if part == 0:
        part_w = dot_nn(ctxt_ref[0].reshape(width, length), attn)

        @pl.when(row == 0)
        def _():
            w_s[:, 768:1536] = part_w

        @pl.when(row > 0)
        def _():
            w_s[:, 768:1536] += part_w

    sums = [
        jnp.sum(jnp.concatenate(grads[j], 1).astype(F32), 0, keepdims=True) for j in (0, 2)
    ]

    @pl.when(row == 0)
    def _():
        vec_out[...] = jnp.zeros_like(vec_out)

    for i in range(2):
        vec_out[i : i + 1, :] += sums[i]

    if last:
        local = length // n
        low_token = token.astype(BF)
        for k in range(n):
            tok_outs[k][0] = low_token[k * local : (k + 1) * local, :]
    else:
        tok_outs[0][...] = token

    @pl.when(row == pl.num_programs(0) - 1)
    def _():
        columns = [[j * 256 + yy * 128 for j in range(3)] for yy in range(2)]
        if part == 0:
            columns = [c + [768 + yy * 384 + j * 128 for j in range(3)] for yy, c in enumerate(columns)]
        bias = vec_out[...]
        bias = jnp.concatenate([bias[:, :128], bias[:, 128:]], 0).astype(BF)
        for c, out in ((0, keep_out), (1, send_out)):
            for yy in range(2):
                for p in range(8):
                    for j, first in enumerate(columns[yy]):
                        out[yy ^ y, p, j * 48 : (j + 1) * 48, :] = w_s[
                            (c * 8 + p) * 48 : (c * 8 + p + 1) * 48, first : first + 128
                        ].astype(BF)
                    used = len(columns[yy]) * 48
                    out[yy, p, used : used + 16, :] = bias
                    if part == 0:
                        out[yy, p, used + 16 : used + 32, :] = shares_ref[place ^ dp_rel(p)]


def attend_back(me, part, n, rows, saved, attn, acc, w, extra, deps):
    q, k, v, ctx, lse, xt, ctxt, mq, mk = saved
    count, width = attn.shape
    length = count // rows
    local = length // n
    last = part == 2
    pair = lambda i: pl.BlockSpec((length, 128), lambda r, m: (r, part + 3 * i))
    row = lambda wide: pl.BlockSpec((length, wide), lambda r, m: (r, 0))
    w_row = lambda i: pl.BlockSpec((128, width), lambda r, m: (part + 3 * i, 0))
    w_col = lambda i: pl.BlockSpec((width, 128), lambda r, m: (0, part + 3 * i))
    t_spec = pl.BlockSpec((1, 2, 8, 48, length), lambda r, m: (r, 0, 0, 0, 0))
    shape = (2, 8, (6 if part == 0 else 3) * 48 + (32 if part == 0 else 16), 128)
    out_w = pl.BlockSpec(shape, lambda r, m: (0,) * 4)
    if last:
        tok_shape = [jax.ShapeDtypeStruct((rows, local, width), BF)] * n
        tok_spec = [pl.BlockSpec((1, local, width), lambda r, m: (r, 0, 0))] * n
        aliases = {}
    else:
        tok_shape = [jax.ShapeDtypeStruct((count, width), F32)]
        tok_spec = [row(width)]
        aliases = {1 + 8 + 5: 3}
    more = (ctxt, extra) if part == 0 else ()
    more_specs = [t_spec, pl.BlockSpec((8, 16, 128), lambda r, m: (0, 0, 0))] if part == 0 else []
    return pl.pallas_call(
        functools.partial(attend_back_kernel, part, n, last, len(deps)),
        grid_spec=pltpu.PrefetchScalarGridSpec(
            num_scalar_prefetch=1,
            grid=(rows,),
            in_specs=[pair(0), pair(1)] * 4
            + [row(128), row(width), row(128), row(128), t_spec, row(width)]
            + [w_row(0), w_row(1)]
            + [w_col(0), w_col(1)] * 3
            + more_specs
            + [pl.BlockSpec(memory_space=pl.ANY)] * len(deps),
            out_specs=[out_w, out_w, pl.BlockSpec((8, 256), lambda r, m: (0, 0))] + tok_spec,
            scratch_shapes=[pltpu.VMEM((width, 1536 if part == 0 else 768), F32)],
        ),
        out_shape=[jax.ShapeDtypeStruct(shape, BF)] * 2 + [jax.ShapeDtypeStruct((8, 256), F32)] + tok_shape,
        input_output_aliases=aliases,
        compiler_params=pltpu.CompilerParams(vmem_limit_bytes=VMEM),
        cost_estimate=LONG,
        name=f"attend_back{part}",
    )(
        me, q, q, k, k, v, v, ctx, ctx, lse, attn, mq, mk, xt, acc,
        w["wo"], w["wo"], w["wq"], w["wq"], w["wk"], w["wk"], w["wv"], w["wv"], *more, *deps,
    )


def swap(array, axis, mask):
    size = lax.axis_size(axis)
    return lax.ppermute(array, axis, [(i, i ^ mask) for i in range(size)])


def pack_tokens(place, tokens, segments, row):
    n = lax.axis_size("seq")
    own, local, width = tokens.shape[0] // n, tokens.shape[1], tokens.shape[2]

    def kernel(me_ref, seg_ref, *refs):
        for k in range(n):
            source, out = refs[k], refs[n + k]
            out[0, :local, :] = source[0]
            out[0, local:, :] = jnp.zeros((16, width), BF)
            at = (me_ref[0] ^ k) * own
            ids = jnp.concatenate([seg_ref[pl.ds(at + r, 1), :] for r in range(own)] + [seg_ref[:1, :]] * (16 - own), 0)
            out[0, local:, :local] = ids.astype(F32).astype(BF)

    return pl.pallas_call(
        kernel,
        grid_spec=pltpu.PrefetchScalarGridSpec(
            num_scalar_prefetch=1,
            grid=(1,),
            in_specs=[pl.BlockSpec(segments.shape, lambda i, m: (0, 0))]
            + [pl.BlockSpec((1, local, width), lambda i, m, k=k: ((m[0] ^ k) * own + row, 0, 0)) for k in range(n)],
            out_specs=[pl.BlockSpec((1, local + 16, width), lambda i, m: (0, 0, 0))] * n,
        ),
        out_shape=[jax.ShapeDtypeStruct((1, local + 16, width), BF)] * n,
        compiler_params=pltpu.CompilerParams(vmem_limit_bytes=VMEM),
        cost_estimate=TINY,
        name="pack_first",
    )(place, segments, *[tokens] * n)


def pack_rest(place, tokens, cotangent, first_row, deps):
    n = lax.axis_size("seq")
    own, local, width = tokens.shape[0] // n, tokens.shape[1], tokens.shape[2]
    rows = range(first_row, own)
    count = len(rows) * n + n

    def kernel(me_ref, *refs):
        for source, out in zip(refs[:count], refs[count + len(deps) :]):
            out[...] = source[...]

    one = [
        pl.BlockSpec((1, local, width), lambda i, m, k=k, r=r: ((m[0] ^ k) * own + r, 0, 0))
        for r in rows
        for k in range(n)
    ]
    many = [pl.BlockSpec((own, local, width), lambda i, m, k=k: (m[0] ^ k, 0, 0)) for k in range(n)]
    return pl.pallas_call(
        kernel,
        grid_spec=pltpu.PrefetchScalarGridSpec(
            num_scalar_prefetch=1,
            grid=(1,),
            in_specs=one + many + [pl.BlockSpec(memory_space=pl.ANY)] * len(deps),
            out_specs=[pl.BlockSpec((1, local, width), lambda i, m: (0, 0, 0))] * len(one)
            + [pl.BlockSpec((own, local, width), lambda i, m: (0, 0, 0))] * n,
        ),
        out_shape=[jax.ShapeDtypeStruct((1, local, width), BF)] * len(one)
        + [jax.ShapeDtypeStruct((own, local, width), BF)] * n,
        compiler_params=pltpu.CompilerParams(vmem_limit_bytes=VMEM),
        cost_estimate=TINY,
        name="pack_rest",
    )(place, *[tokens] * len(one), *[cotangent] * n, *deps)


def unpack(place, blocks):
    n = len(blocks)
    own, local, width = blocks[0].shape

    any_spec = pl.BlockSpec(memory_space=pl.ANY)

    def kernel(me_ref, *refs):
        sources, (out, held, sem) = refs[:n], refs[n:]
        ins = [pltpu.make_async_copy(sources[k], held.at[k], sem.at[k]) for k in range(n)]
        outs = [
            pltpu.make_async_copy(held.at[k], out.at[pl.ds((me_ref[0] ^ k) * own, own)], sem.at[n + k]) for k in range(n)
        ]
        for copy in ins:
            copy.start()
        for k in range(n):
            ins[k].wait()
            outs[k].start()
        for copy in outs:
            copy.wait()

    return pl.pallas_call(
        kernel,
        grid_spec=pltpu.PrefetchScalarGridSpec(
            num_scalar_prefetch=1,
            grid=(1,),
            in_specs=[any_spec] * n,
            out_specs=any_spec,
            scratch_shapes=[pltpu.VMEM((n, own, local, width), blocks[0].dtype), pltpu.SemaphoreType.DMA((2 * n,))],
        ),
        out_shape=jax.ShapeDtypeStruct((own * n, local, width), blocks[0].dtype),
        compiler_params=pltpu.CompilerParams(vmem_limit_bytes=VMEM),
        cost_estimate=TINY,
        name="unpack_rows",
    )(place, *blocks)


def exchange(blocks):
    return [swap(block, "seq", k) if k else block for k, block in enumerate(blocks)]


def bits_of(size):
    return [1 << b for b in range(size.bit_length() - 1)]


def reduce_matrix(grad):
    sn, dn = lax.axis_size("seq"), lax.axis_size("dp")
    ms, md = lax.axis_index("seq"), lax.axis_index("dp")
    high, wide = grad.shape[0] // dn, grad.shape[1] // sn
    blocks = grad.astype(BF).reshape(dn, high, sn, wide).transpose(2, 0, 1, 3)
    blocks = jnp.take(blocks, ms ^ jnp.arange(sn), axis=0)
    blocks = jnp.take(blocks, md ^ jnp.arange(dn), axis=1)
    left = {"seq": sn, "dp": dn}
    for axis, mask in [("seq", m) for m in bits_of(sn)] + [("dp", m) for m in bits_of(dn)]:
        size = left[axis]
        dim = 0 if axis == "seq" else 1
        split = blocks.reshape(blocks.shape[:dim] + (size // 2, 2) + blocks.shape[dim + 1 :])
        keep = lax.index_in_dim(split, 0, dim + 1, keepdims=False)
        send = lax.index_in_dim(split, 1, dim + 1, keepdims=False)
        blocks = keep + swap(send, axis, mask)
        left[axis] = size // 2
    return blocks.reshape(high, wide).astype(F32)


def reduce_vectors(vectors):
    for axis in ("seq", "dp"):
        for mask in bits_of(lax.axis_size(axis)):
            vectors = vectors + swap(vectors, axis, mask)
    return vectors


def my_share(vector):
    own = vector.shape[0] // lax.axis_size("dp")
    return lax.dynamic_slice_in_dim(vector, lax.axis_index("dp") * own, own, 0)


X, Y = ("dp", 1), ("seq", 2)


def stage(name, work, arrays, shapes, deps=(), place=None, room=24 * MIB):
    scalars = [] if place is None else [place]

    def kernel(*refs):
        lead, refs = refs[: len(scalars)], refs[len(scalars) :]
        work(*lead, *refs[: len(arrays)], *refs[len(arrays) + len(deps) :])

    full = lambda shape: pl.BlockSpec(shape, lambda i, *m: (0,) * len(shape))
    return pl.pallas_call(
        kernel,
        grid_spec=pltpu.PrefetchScalarGridSpec(
            num_scalar_prefetch=len(scalars),
            grid=(1,),
            in_specs=[full(a.shape) for a in arrays] + [pl.BlockSpec(memory_space=pl.ANY)] * len(deps),
            out_specs=[full(shape) for shape, _ in shapes],
        ),
        out_shape=[jax.ShapeDtypeStruct(shape, dtype) for shape, dtype in shapes],
        compiler_params=pltpu.CompilerParams(vmem_limit_bytes=room),
        cost_estimate=LONG,
        name=name,
    )(*scalars, *arrays, *deps)


def halves(kept, came, keep_out, send_out, lead, rows=None):
    tail = () if rows is None else (Ellipsis, rows, slice(None))
    for i, out in ((0, keep_out), (1, send_out)):
        at = (slice(None),) * lead + (i,) + tail
        out[...] = kept[at] + came[at]


def body(
    tokens,
    cotangent,
    segments,
    w_query,
    b_query,
    w_key,
    w_value,
    b_value,
    w_out,
    b_out,
    gain_one,
    shift_one,
    w_inner,
    b_inner,
    w_outer,
    b_outer,
    gain_two,
    shift_two,
):
    width = tokens.shape[-1]
    n, dn = lax.axis_size("seq"), lax.axis_size("dp")
    ms, md = lax.axis_index("seq"), lax.axis_index("dp")
    fast = n == 4 and dn == 8
    me = (jnp.stack([ms % 2, ms // 2, md]) if fast else jnp.zeros((3,))).astype(jnp.int32)
    seq_place = ms.astype(jnp.int32).reshape(1)
    rows, local = tokens.shape[0] // n, tokens.shape[1]
    length = n * local
    vectors = (b_query, b_value, b_out, gain_one, shift_one, gain_two, shift_two, b_outer, b_inner)
    packed = jnp.concatenate(vectors + (jnp.zeros((4 * width,), BF),)).reshape(16, width).astype(F32)
    w = dict(wq=w_query, wk=w_key, wv=w_value, wo=w_out, wi=w_inner, wo2=w_outer, vec=packed)

    first_blocks = pack_tokens(seq_place, tokens, segments, 0)
    x_blocks = [exchange(first_blocks)]
    seg_blocks = x_blocks[0]
    rest = pack_rest(seq_place, tokens, cotangent, 1, first_blocks[:1])
    for r in range(1, rows):
        x_blocks.append(exchange(rest[(r - 1) * n : r * n]))
    up_blocks = exchange(rest[(rows - 1) * n :])

    before = None
    for r in range(rows):
        before = attend(me, r, rows, x_blocks[r], seg_blocks, w, before)
    q, k, v, ctx, lse, resid, xt, ctxt, mq, mk = before
    slope, branch, grad2, ht, outer_keep, outer_send, vec2, *y_blocks = forward(me, rows, resid, up_blocks, w)
    outer = (outer_keep, outer_send)
    y_blocks = exchange(y_blocks)
    inner_send, partial, bi_send = backward(me, False, branch, slope, ht, w, [], [])
    saved = (q, k, v, ctx, lse, xt, ctxt, mq, mk)

    if not fast:
        inner_keep, grad1, bi_keep, attn, vec1 = backward(me, True, branch, slope, ht, w, [resid, grad2, partial], [])
        shares = jnp.zeros((8, 16, 128), BF)
        early = jnp.concatenate([vec2[:3], vec1[:3]], 0)
        vec_bi = jnp.stack([bi_keep[0].reshape(2, -1), bi_send[0].reshape(2, -1)], 1).reshape(1, -1)
        parts, vec_parts = [], []
        acc = grad1
        for part in range(3):
            keep, send, vec, *tail = attend_back(me, part, n, rows, saved, attn, acc, w, shares, [])
            parts.append((keep, send))
            vec_parts.append(vec)
            acc = tail[0]
        output = unpack(seq_place, y_blocks)
        grad_tokens = unpack(seq_place, exchange(tail))
        early = reduce_vectors(jnp.concatenate([early, vec_bi[:1].reshape(4, width)], 0))
        late = jnp.stack([p[:2] for p in vec_parts], 1).reshape(2, 3, 2, 128)
        late = reduce_vectors(late.transpose(0, 2, 1, 3).reshape(2, width))
        stack = lambda pair: jnp.stack(list(pair))
        outer_t = stack(outer).reshape(2, 2, 2, 4, 96, 2, 384).transpose(1, 0, 5, 4, 3, 2, 6).reshape(width, -1)
        inner_b = stack((inner_keep, inner_send)).reshape(2, 2, 2, 4, 96, -1).transpose(3, 2, 4, 1, 0, 5)
        inner_b = inner_b.reshape(width, -1)
        three = [stack(pair)[:, :, :, -160:-16] if i else stack(pair)[:, :, :, :144] for i, pair in enumerate(parts)]
        qkv = jnp.stack(three).reshape(3, 2, 2, 2, 4, 3, 48, 128).transpose(5, 4, 3, 1, 6, 2, 0, 7).reshape(3, width, width)
        out_b = stack(parts[0])[:, :, :, 144:288].reshape(2, 2, 2, 4, 3, 48, 128).transpose(3, 2, 0, 5, 1, 4, 6)
        grad_w_outer = reduce_matrix(outer_t.T)
        grad_w_inner = reduce_matrix(inner_b)
        grad_w_out = reduce_matrix(out_b.reshape(width, width))
        grad_w_query, grad_w_key, grad_w_value = (reduce_matrix(qkv[i]) for i in range(3))
        b_query_g, b_value_g = my_share(late[0]), my_share(late[1])
        gain2_g, shift2_g, b_outer_g, gain1_g, shift1_g, b_out_g = (my_share(early[i]) for i in range(6))
        b_inner_g = my_share(early[6:10].reshape(-1))
    else:
        by_axes = lambda a: a.reshape((2, 2, 4) + a.shape[2:])
        one = lambda *shape: (shape, BF)
        top, low = slice(0, 48), slice(48, 96)
        z_swap = lambda pieces: [pieces[0]] + [swap(pieces[j], "dp", 2 * j) for j in (1, 2, 3)]
        first_shapes, second_shapes, z_shapes = [one(2, 4, 48, 768)] * 4, [one(4, 48, 768)] * 4, [one(96, 768)] * 4

        def z_split(top_keep, top_came, low_keep, low_came, outs):
            for j, out in enumerate(outs):
                out[0:48, :] = top_keep[j] + top_came[j]
                out[48:96, :] = low_keep[j] + low_came[j]

        outer_came = swap(outer[1], "seq", 1)

        def stage_a(kept, came, a_keep, a_send, b_keep, b_send):
            halves(kept, came, a_keep, a_send, 1, top)
            halves(kept, came, b_keep, b_send, 0, low)

        a_keep, a_send, b_keep, b_send = stage(
            "stage_a", stage_a, [outer[0], outer_came], first_shapes, [inner_send], room=VMEM
        )

        a_came, b_came = swap(a_send, *X), swap(b_send, *Y)
        inner_came = swap(inner_send, "seq", 1)
        inner_keep, grad1, bi_keep, attn, vec1 = backward(
            me, True, branch, slope, ht, w, [resid, grad2, partial], [a_keep, *y_blocks]
        )

        def stage_b(
            me_ref, a_keep, a_came, b_keep, b_came, i_keep, i_came, vec2, vec1, bi_keep, bi_send,
            a2_keep, a2_send, b2_keep, b2_send, c_keep, c_send, d_keep, d_send, shares,
        ):
            halves(a_keep, a_came, a2_keep, a2_send, 0)
            halves(b_keep, b_came, b2_keep, b2_send, 0)
            halves(i_keep, i_came, c_keep, c_send, 1, top)
            halves(i_keep, i_came, d_keep, d_send, 0, low)
            early = jnp.concatenate([vec2[0:3], vec1[0:3]], 0)
            kept, sent = bi_keep[0:1], bi_send[0:1]
            blank = jnp.zeros((6, 32), F32)
            for d in range(8):
                core, y = me_ref[0], me_ref[1]
                at = slice((d % 2) * 384, (d % 2) * 384 + 384)
                other = slice(768 + at.start, 768 + at.stop)
                own_core = core == (d // 2) % 2
                own_y = y == d // 4
                piece = jnp.where(
                    own_core,
                    jnp.where(own_y, kept[:, at], kept[:, other]),
                    jnp.where(own_y, sent[:, at], sent[:, other]),
                )
                rows = [jnp.concatenate([early[:, d * 96 : d * 96 + 96], blank], 1)]
                rows += [piece[:, j * 128 : j * 128 + 128] for j in range(3)] + [jnp.zeros((7, 128), F32)]
                shares[d] = jnp.concatenate(rows, 0).astype(BF)

        *stage_b_outs, shares = stage(
            "stage_b",
            stage_b,
            [a_keep, a_came, b_keep, b_came, by_axes(inner_keep), by_axes(inner_came), vec2, vec1, bi_keep, bi_send],
            second_shapes + first_shapes + [one(8, 16, 128)],
            place=me,
            room=VMEM,
        )
        a_keep, a_send, b_keep, b_send, c_keep, c_send, d_keep, d_send = stage_b_outs

        a_came, b_came = swap(a_send, *Y), swap(b_send, *X)
        c_came, d_came = swap(c_send, *X), swap(d_send, *Y)
        keep0, send0, vec_0, acc = attend_back(me, 0, n, rows, saved, attn, grad1, w, shares, [a_keep])

        def stage_c(a_keep, a_came, b_keep, b_came, c_keep, c_came, d_keep, d_came, *outs):
            z_split(a_keep, a_came, b_keep, b_came, outs[:4])
            halves(c_keep, c_came, outs[4], outs[5], 0)
            halves(d_keep, d_came, outs[6], outs[7], 0)

        *outer_z, c_keep, c_send, d_keep, d_send = stage(
            "stage_c",
            stage_c,
            [a_keep, a_came, b_keep, b_came, c_keep, c_came, d_keep, d_came],
            z_shapes + second_shapes,
            [keep0],
            room=VMEM,
        )

        c_came, d_came = swap(c_send, *Y), swap(d_send, *X)
        came0 = swap(send0, "seq", 1)
        outer_z = z_swap(outer_z)
        output = unpack(seq_place, y_blocks)
        keep1, send1, vec_1, acc = attend_back(me, 1, n, rows, saved, attn, acc, w, None, [c_keep, output])

        def stage_d(c_keep, c_came, d_keep, d_came, keep0, came0, *outs):
            z_split(c_keep, c_came, d_keep, d_came, outs[:4])
            halves(keep0, came0, outs[4], outs[5], 0)

        *inner_z, p0_keep, p0_send = stage(
            "stage_d",
            stage_d,
            [c_keep, c_came, d_keep, d_came, by_axes(keep0), by_axes(came0)],
            z_shapes + [one(2, 4, 320, 128)] * 2,
            outer_z[1:],
            room=VMEM,
        )

        p0_came = swap(p0_send, *Y)
        came1 = swap(send1, "seq", 1)
        inner_z = z_swap(inner_z)
        keep2, send2, vec_2, *tok_blocks = attend_back(me, 2, n, rows, saved, attn, acc, w, None, [p0_keep])

        came2 = swap(send2, "seq", 1)
        tok_blocks = exchange(tok_blocks)
        add = lambda four: sum(r[...].astype(F32) for r in four)
        x_split = lambda kept, came, a, b: halves(kept, came, a, b, 1)
        y_split = lambda kept, came, a, b: halves(kept, came, a, b, 0)
        quarter, eighth = [one(2, 4, 160, 128)] * 2, [one(4, 160, 128)] * 2

        def stage_e(p0_keep, p0_came, keep1, came1, *outs):
            halves(p0_keep, p0_came, outs[0], outs[1], 0)
            halves(keep1, came1, outs[2], outs[3], 0)

        p0_keep, p0_send, p1_keep, p1_send = stage(
            "stage_e",
            stage_e,
            [p0_keep, p0_came, by_axes(keep1), by_axes(came1)],
            [one(4, 320, 128)] * 2 + quarter,
            [keep2, *inner_z[1:]],
        )
        p1_came, p0_came = swap(p1_send, *Y), swap(p0_send, *X)
        p2_keep, p2_send = stage(
            "stage_f", x_split, [by_axes(keep2), by_axes(came2)], quarter, [p1_keep]
        )
        p2_came = swap(p2_send, *X)

        def forward_grads(*refs):
            refs[9][...] = add(refs[4:8])
            outer_z = add(refs[0:4])
            refs[8][0:96, :] = outer_z[:, :384]
            refs[8][96:192, :] = outer_z[:, 384:]

        grad_w_outer, grad_w_inner = stage(
            "forward_grads", forward_grads, outer_z + inner_z, [((192, 384), F32), ((96, 768), F32)], [p2_keep]
        )
        grad_w_outer = grad_w_outer.T

        def stage_g(p0_keep, p0_came, p1_keep, p1_came, *outs):
            for j in range(4):
                outs[j][...] = p0_keep[j] + p0_came[j]
            halves(p1_keep, p1_came, outs[4], outs[5], 0)

        *z0, p1_keep, p1_send = stage(
            "stage_g",
            stage_g,
            [p0_keep, p0_came, p1_keep, p1_came],
            [one(320, 128)] * 4 + eighth,
            [grad_w_inner],
        )
        p1_came = swap(p1_send, *X)
        z0 = z_swap(z0)
        p2_keep, p2_send = stage(
            "stage_h", y_split, [p2_keep, p2_came], eighth, [p1_keep, tok_blocks[2]]
        )
        p2_came = swap(p2_send, *Y)

        def stage_i(p1_keep, p1_came, p2_keep, p2_came, *outs):
            for j in range(4):
                outs[j][0:160, :] = p1_keep[j] + p1_came[j]
                outs[j][160:320, :] = p2_keep[j] + p2_came[j]

        z12 = z_swap(stage("stage_i", stage_i, [p1_keep, p1_came, p2_keep, p2_came], [one(320, 128)] * 4, z0[1:]))
        grad_tokens = unpack(seq_place, tok_blocks)

        def gather_up(me_ref, *refs):
            z0, z12 = add(refs[0:4]), add(refs[4:8])
            mine, other, bq_out, bv_out, bi_out, *vec_outs = refs[8:]
            place = me_ref[2]
            for i, out in enumerate(vec_outs):
                out[...] = z0[304 + i : 305 + i, 0:96]
            bi_out[...] = jnp.concatenate([z0[310 + j : 311 + j] for j in range(3)], 1)
            first_rows = [z0[288:304], z12[144:160], z12[304:320]]
            for i, out in enumerate((bq_out, bv_out)):
                whole = [first_rows[j % 3][(j // 3) * 8 + i : (j // 3) * 8 + i + 1] for j in range(6)]
                whole = jnp.concatenate(whole, 1)
                total = jnp.zeros((1, 96), F32)
                for d in range(8):
                    total = jnp.where(place == d, whole[:, d * 96 : d * 96 + 96], total)
                out[...] = total
            rows = lambda z, first: [z[first + 48 * j : first + 48 * j + 48] for j in range(3)]
            out_w = rows(z0, 144)
            parts = [rows(z0, 0), rows(z12, 0), rows(z12, 160)]
            for i in range(4):
                pieces = out_w if i == 0 else [part[i - 1] for part in parts]
                whole = jnp.concatenate(pieces, 1)
                left, right = whole[:, :192], whole[:, 192:]
                first = me_ref[0] == 0
                mine[i] = jnp.where(first, left, right)
                other[i] = jnp.where(first, right, left).astype(BF)

        mine, other, b_query_g, b_value_g, b_inner_g, *vecs = stage(
            "gather_up",
            gather_up,
            z0 + z12,
            [((4, 48, 192), F32), ((4, 48, 192), BF), ((1, 96), F32), ((1, 96), F32), ((1, 384), F32)]
            + [((1, 96), F32)] * 6,
            [grad_tokens],
            place=me,
        )
        other = swap(other, "seq", 1)

        def assemble(me_ref, mine, other, *outs):
            for i, out in enumerate(outs):
                kept, came = mine[i], other[i].astype(F32)
                first = me_ref[0] == 0
                out[0:48, :] = jnp.where(first, kept, came)
                out[48:96, :] = jnp.where(first, came, kept)

        grad_w_out, grad_w_query, grad_w_key, grad_w_value = stage(
            "assemble", assemble, [mine, other], [((96, 192), F32)] * 4, place=me
        )
        b_query_g, b_value_g, b_inner_g = (v.reshape(-1) for v in (b_query_g, b_value_g, b_inner_g))
        gain2_g, shift2_g, b_outer_g, gain1_g, shift1_g, b_out_g = (v.reshape(-1) for v in vecs)

    return (
        output,
        grad_tokens,
        grad_w_query,
        b_query_g,
        grad_w_key,
        grad_w_value,
        b_value_g,
        grad_w_out,
        b_out_g,
        gain1_g,
        shift1_g,
        grad_w_inner,
        b_inner_g,
        grad_w_outer,
        b_outer_g,
        gain2_g,
        shift2_g,
    )


def solution(mesh):
    token = P("dp", "seq", None)
    matrix = P("dp", "seq")
    vector = P("dp")
    return jax.shard_map(
        body,
        mesh=mesh,
        in_specs=(token, token, P("dp", "seq")) + (P(),) * 15,
        out_specs=(
            token,
            token,
            matrix,
            vector,
            matrix,
            matrix,
            vector,
            matrix,
            vector,
            vector,
            vector,
            matrix,
            vector,
            matrix,
            vector,
            vector,
            vector,
        ),
        check_vma=False,
    )
```

```python
import functools

import jax
import jax.numpy as jnp
from jax import lax
from jax.experimental import pallas as pl
from jax.experimental.pallas import tpu as pltpu
from jax.sharding import PartitionSpec as P

HEADS = 12
BF = jnp.bfloat16
F32 = jnp.float32
MIB = 1 << 20
VMEM = 60 * MIB
LONG = pl.CostEstimate(flops=60_000_000_000, bytes_accessed=1, transcendentals=0)
TINY = pl.CostEstimate(flops=1, bytes_accessed=1, transcendentals=0)


def dot_nn(a, b):
    return lax.dot_general(a, b, (((1,), (0,)), ((), ())), preferred_element_type=F32)


def dot_nt(a, b):
    return lax.dot_general(a, b, (((1,), (1,)), ((), ())), preferred_element_type=F32)


def dot_tn(a, b):
    return lax.dot_general(a, b, (((0,), (0,)), ((), ())), preferred_element_type=F32)


def normal_laws(a):
    gauss = jnp.exp(a * a * -0.5)
    return 0.5 + 0.5 * lax.erf(a * 0.7071067811865476), a * (gauss * 0.3989422804014327)


def norm_parts(values):
    mean = jnp.mean(values, -1, keepdims=True)
    centred = values - mean
    inverse = lax.rsqrt(jnp.mean(centred * centred, -1, keepdims=True) + 1e-05)
    return centred * inverse, inverse


def norm_back(scaled, normed, inverse):
    return inverse * (
        scaled
        - jnp.mean(scaled, -1, keepdims=True)
        - normed * jnp.mean(scaled * normed, -1, keepdims=True)
    )


def lines(index, size):
    return pl.ds(pl.multiple_of(index * size, size), size)


def lane_of(shape):
    return lax.broadcasted_iota(jnp.int32, shape, 1)


def place_of(me_ref):
    return me_ref[0], me_ref[1], me_ref[2]


def dp_rel(position):
    return (position % 4) * 2 + position // 4


def split_rows(position_c, position_d, me):
    core, _, place = me
    return pl.multiple_of((place ^ dp_rel(position_d)) * 96 + (core ^ position_c) * 48, 16)


def attend_kernel(n, row, aliased, local, me_ref, *refs):
    x_refs, seg_refs, refs = refs[:n], refs[n : 2 * n], refs[2 * n :]
    w_refs, (wo_ref, vec_ref), refs = refs[:3], refs[3:5], refs[5 + aliased :]
    outs, refs = refs[:10], refs[10:]
    x_s, seg_s, w_s, wo_s, vec_s, qkvc_s, lse_s, resid_s, t_s, xt_s, ctxt_s, mask_s, sem = refs
    q_out, k_out, v_out, ctx_out, lse_out, resid_out, xt_out, ctxt_out, mq_out, mk_out = outs
    length, width = x_s.shape
    groups = width // 256
    me = place_of(me_ref)
    move = pltpu.make_async_copy
    here = slice(row * length, (row + 1) * length)
    x_in = [move(x_refs[k].at[0, slice(0, local)], x_s.at[slice(k * local, (k + 1) * local)], sem.at[k]) for k in range(n)]
    seg_in = [move(seg_refs[k].at[0, slice(local, local + 16)], seg_s.at[k], sem.at[n + k]) for k in range(n)]
    wo_in, vec_in = move(wo_ref, wo_s, sem.at[2 * n]), move(vec_ref, vec_s, sem.at[2 * n + 1])
    at_w = 2 * n + 2

    def w_in(g):
        cols = lines(g, 256)
        return [move(w_refs[j].at[:, cols], w_s.at[j, :, cols], sem.at[at_w + 3 * g + j]) for j in range(3)]

    at_out = at_w + 3 * groups

    def qkvc_to(g):
        cols = lines(g, 256)
        return [
            move(qkvc_s.at[j, :, cols], out.at[here, cols], sem.at[at_out + 4 * g + j])
            for j, out in enumerate((q_out, k_out, v_out, ctx_out))
        ]

    at_late = at_out + 4 * groups
    mask_to = [move(mask_s.at[i], out.at[here], sem.at[at_late + i]) for i, out in enumerate((mq_out, mk_out))]
    xt_to, ctxt_to = move(xt_s, xt_out.at[row], sem.at[at_late + 2]), move(ctxt_s, ctxt_out.at[row], sem.at[at_late + 3])
    lse_to, resid_to = move(lse_s, lse_out.at[here], sem.at[at_late + 4]), move(resid_s, resid_out.at[here], sem.at[at_late + 5])
    for copy in x_in + seg_in + [vec_in] + w_in(0) + w_in(1) + w_in(2) + [wo_in]:
        copy.start()
    for copy in seg_in:
        copy.wait()
    seg = jnp.concatenate([seg_s[k][:, :local].astype(F32)[row : row + 1] for k in range(n)], 1)
    spot = lax.broadcasted_iota(jnp.int32, (128, length), 0) % 64
    same = spot.astype(F32) == seg
    mask_s[0] = jnp.where(same, -1e30, 0.0).T.astype(BF)
    mask_s[1] = jnp.where((spot < 7) & jnp.logical_not(same), 1.0, 0.0).T.astype(BF)
    lse_s[...] = jnp.zeros_like(lse_s)
    for copy in mask_to:
        copy.start()
    for copy in x_in:
        copy.wait()

    def transposed(source, target):
        t_s[...] = source.T
        for c in range(2):
            for d in range(8):
                target[c, d] = t_s[pl.ds(split_rows(c, d, me), 48), :]

    transposed(x_s[...], xt_s)
    xt_to.start()
    vec_in.wait()
    low = lane_of((length, 128)) < 64

    def group(g, carry):
        cols = lines(g, 256)
        for copy in w_in(g):
            copy.wait()
        x, mq, mk = x_s[...], mask_s[0], mask_s[1]
        q = ((dot_nn(x, w_s[0, :, cols]) + vec_s[0:1, cols]).astype(BF).astype(F32) * 0.125).astype(BF)
        kk = dot_nn(x, w_s[1, :, cols]).astype(BF)
        v = (dot_nn(x, w_s[2, :, cols]) + vec_s[1:2, cols]).astype(BF)
        for j, value in enumerate((q, kk, v)):
            qkvc_s[j, :, cols] = value

        def scores(head):
            pair = slice(head // 2 * 128, head // 2 * 128 + 128)
            mine = low if head % 2 == 0 else jnp.logical_not(low)
            return dot_nt(jnp.where(mine, q[:, pair], mq), jnp.where(mine, kk[:, pair], mk))

        stats = lse_s[...]
        lanes = lane_of(stats.shape)
        heads = []
        ahead = scores(0)
        for head in range(4):
            s = ahead
            if head < 3:
                ahead = scores(head + 1)
            top = jnp.max(s, -1, keepdims=True)
            e = jnp.exp(s - top)
            total = jnp.sum(e, -1, keepdims=True)
            v2 = v[:, head // 2 * 128 : head // 2 * 128 + 128]
            heads.append(dot_nn(e.astype(BF), v2) * (1.0 / total))
            stats = jnp.where(lanes == g * 4 + head, top + jnp.log(total), stats)
        lse_s[...] = stats
        qkvc_s[3, :, cols] = jnp.concatenate([jnp.where(low, heads[i], heads[i + 1]).astype(BF) for i in (0, 2)], 1)
        for copy in qkvc_to(g):
            copy.start()
        return carry

    lax.fori_loop(0, groups, group, 0)
    lse_to.start()
    wo_in.wait()
    for first in range(0, length, 256):
        at = slice(first, first + 256)
        resid_s[at, :] = x_s[at, :].astype(F32) + dot_nn(qkvc_s[3, at, :], wo_s[...]) + vec_s[2:3, :]
    resid_to.start()
    transposed(qkvc_s[3], ctxt_s)
    ctxt_to.start()
    for g in range(groups):
        for copy in qkvc_to(g):
            copy.wait()
    for copy in mask_to + [xt_to, ctxt_to, lse_to, resid_to]:
        copy.wait()


def attend(me, row, rows, x_blocks, seg_blocks, w, before):
    n, local, width = len(x_blocks), seg_blocks[0].shape[1] - 16, x_blocks[0].shape[2]
    length = n * local
    count = rows * length
    out_shape = [
        jax.ShapeDtypeStruct((count, width), BF),
        jax.ShapeDtypeStruct((count, width), BF),
        jax.ShapeDtypeStruct((count, width), BF),
        jax.ShapeDtypeStruct((count, width), BF),
        jax.ShapeDtypeStruct((count, 128), F32),
        jax.ShapeDtypeStruct((count, width), F32),
        jax.ShapeDtypeStruct((rows, 2, 8, 48, length), BF),
        jax.ShapeDtypeStruct((rows, 2, 8, 48, length), BF),
        jax.ShapeDtypeStruct((count, 128), BF),
        jax.ShapeDtypeStruct((count, 128), BF),
    ]
    aliased = [] if before is None else list(before)
    first = 1 + 2 * n + 5
    any_spec = pl.BlockSpec(memory_space=pl.ANY)
    return pl.pallas_call(
        functools.partial(attend_kernel, n, row, len(aliased), local),
        grid_spec=pltpu.PrefetchScalarGridSpec(
            num_scalar_prefetch=1,
            grid=(1,),
            in_specs=[any_spec] * (2 * n + 5 + len(aliased)),
            out_specs=[any_spec] * len(out_shape),
            scratch_shapes=[
                pltpu.VMEM((length, width), BF),
                pltpu.VMEM((n, 16, width), BF),
                pltpu.VMEM((3, width, width), BF),
                pltpu.VMEM((width, width), BF),
                pltpu.VMEM((16, width), F32),
                pltpu.VMEM((4, length, width), BF),
                pltpu.VMEM((length, 128), F32),
                pltpu.VMEM((length, width), F32),
                pltpu.VMEM((width, length), BF),
                pltpu.VMEM((2, 8, 48, length), BF),
                pltpu.VMEM((2, 8, 48, length), BF),
                pltpu.VMEM((2, length, 128), BF),
                pltpu.SemaphoreType.DMA((2 * n + 2 + 7 * (width // 256) + 6,)),
            ],
        ),
        out_shape=out_shape,
        input_output_aliases={first + i: i for i in range(len(aliased))},
        compiler_params=pltpu.CompilerParams(vmem_limit_bytes=VMEM),
        cost_estimate=LONG,
        name=f"attend_row{row}",
    )(me, *x_blocks, *seg_blocks, w["wq"], w["wk"], w["wv"], w["wo"], w["vec"], *aliased)


CHUNK = 768
TILE = 256


def forward_kernel(
    n, rows, me_ref, vec_ref, resid_ref, wi_ref, wo_ref, *refs,
):
    up_refs, refs = refs[:n], refs[n:]
    slope_out, branch_out, grad_out, ht_out, keep_out, send_out, vec_out = refs[:7]
    y_outs, refs = refs[7 : 7 + n], refs[7 + n :]
    h_s, low_s, wi_s, wo_s, act_s, slope_s, up_s, y_s, t_s, ht_s, branch_s, gt_s, keep_s, send_s, sem = refs
    core, y, place = place_of(me_ref)
    count, width = h_s.shape
    local = up_s.shape[2]
    tiles, chunks = count // TILE, wi_s.shape[1] // CHUNK
    move = pltpu.make_async_copy
    at_wi, at_wo, at_up = tiles, tiles + chunks, tiles + chunks + 1
    at_out = at_up + n
    resid_in = lambda i: move(resid_ref.at[lines(i, TILE)], h_s.at[lines(i, TILE)], sem.at[i])
    wi_in = lambda c: move(wi_ref.at[:, lines(c, CHUNK)], wi_s.at[:, lines(c, CHUNK)], sem.at[at_wi + c])
    wo_in = move(wo_ref, wo_s, sem.at[at_wo])
    up_in = [move(up_refs[k], up_s.at[k], sem.at[at_up + k]) for k in range(n)]
    slope_to = lambda c: move(slope_s.at[:, lines(c, CHUNK)], slope_out.at[:, lines(c, CHUNK)], sem.at[at_out + c])
    keep_to = lambda z: move(keep_s.at[:, :, z], keep_out.at[:, :, z], sem.at[at_out + chunks + z])
    send_to = lambda z: move(send_s.at[:, :, z], send_out.at[:, :, z], sem.at[at_out + chunks + 4 + z])
    at_late = at_out + chunks + 8
    ht_to = move(ht_s, ht_out, sem.at[at_late])
    late = []

    for i in range(tiles):
        resid_in(i).start()
    for c in range(chunks):
        wi_in(c).start()
    wo_in.start()
    for copy in up_in:
        copy.start()

    def first_norm(i, carry):
        at = lines(i, TILE)
        resid_in(i).wait()
        normed, _ = norm_parts(h_s[at, :])
        hidden = normed * vec_ref[3:4, :] + vec_ref[4:5, :]
        h_s[at, :] = hidden
        low = hidden.astype(BF)
        low_s[at, :] = low
        t_s[:, at] = low.T
        return carry

    lax.fori_loop(0, tiles, first_norm, 0)
    for p in range(8):
        source = pl.multiple_of((place ^ dp_rel(p)) * 96, 32)
        ht_s[p * 96 : (p + 1) * 96, :] = t_s[pl.ds(source, 96), :]
    ht_to.start()

    def hidden_chunk(c, carry):
        cols = lines(c, CHUNK)
        wi_in(c).wait()
        bias = vec_ref[pl.ds(8 + c, 1), :]
        project = lambda i: dot_nn(low_s[i * TILE : (i + 1) * TILE, :], wi_s[:, cols]) + bias
        ahead = project(0)
        for i in range(tiles):
            inner = ahead
            if i + 1 < tiles:
                ahead = project(i + 1)
            phi, rest = normal_laws(inner)
            act_s[i * TILE : (i + 1) * TILE, cols] = (inner * phi).astype(BF)
            slope_s[i * TILE : (i + 1) * TILE, cols] = (phi + rest).astype(BF)
        slope_to(c).start()
        return carry

    lax.fori_loop(0, chunks, hidden_chunk, 0)
    wo_in.wait()
    for copy in up_in:
        copy.wait()
    gain, shift, bias = vec_ref[5:6, :], vec_ref[6:7, :], vec_ref[7:8, :]
    sums = [jnp.zeros((1, width), F32)] * 3
    second = lambda i: dot_nn(act_s[i * TILE : (i + 1) * TILE, :], wo_s[...])
    ahead = second(0)
    per_tile = TILE // local
    for i in range(tiles):
        product = ahead
        if i + 1 < tiles:
            ahead = second(i + 1)
        for j in range(per_tile):
            block = i * per_tile + j
            r, k = block // n, block % n
            at = slice(block * local, (block + 1) * local)
            normed, inverse = norm_parts(h_s[at, :] + product[j * local : (j + 1) * local] + bias)
            up = up_s[k, r].astype(F32)
            y_s[k, r] = (normed * gain + shift).astype(BF)
            grad = norm_back(up * gain, normed, inverse)
            h_s[at, :] = grad
            branch = grad.astype(BF)
            branch_s[at, :] = branch
            t_s[:, at] = branch.T
            for q, piece in enumerate((up * normed, up, branch.astype(F32))):
                sums[q] = sums[q] + jnp.sum(piece, 0, keepdims=True)
    late += [move(h_s, grad_out, sem.at[at_late + 1]), move(branch_s, branch_out, sem.at[at_late + 2])]
    late += [move(y_s.at[k], y_outs[k], sem.at[at_late + 3 + k]) for k in range(n)]
    for copy in late:
        copy.start()
    vec_out[...] = jnp.concatenate(sums + [jnp.zeros((5, width), F32)], 0)
    for c in range(2):
        for yy in range(2):
            source = pl.multiple_of(((y ^ yy) * 2 + (core ^ c)) * 192, 64)
            gt_s[(c * 2 + yy) * 192 : (c * 2 + yy + 1) * 192, :] = t_s[pl.ds(source, 192), :]

    def outer_grad(z, carry):
        cols = lines((place >> 1) ^ z, 768)
        for c, out in ((1, send_s), (0, keep_s)):
            for yy in range(2):
                first = (c * 2 + yy) * 192
                product = dot_nn(gt_s[first : first + 192, :], act_s[:, cols]).astype(BF)
                for x in range(2):
                    for half in range(2):
                        out[yy, x ^ (place & 1), z, :, half * 384 : half * 384 + 384] = product[
                            half * 96 : half * 96 + 96, x * 384 : (x + 1) * 384
                        ]
        send_to(z).start()
        keep_to(z).start()
        return carry

    lax.fori_loop(0, 4, outer_grad, 0)
    ht_to.wait()
    for copy in late:
        copy.wait()
    for c in range(chunks):
        slope_to(c).wait()
    for z in range(4):
        send_to(z).wait()
        keep_to(z).wait()


def forward(me, rows, resid, up_blocks, w):
    count, width = resid.shape
    n, local = len(up_blocks), up_blocks[0].shape[1]
    ff = w["wi"].shape[1]
    any_spec = pl.BlockSpec(memory_space=pl.ANY)
    blocks = (2, 2, 4, 96, 768)
    out_shape = [
        ((count, ff), BF),
        ((count, width), BF),
        ((count, width), F32),
        ((width, count), BF),
        (blocks, BF),
        (blocks, BF),
        ((8, width), F32),
    ] + [((rows, local, width), BF)] * n
    specs = [any_spec] * len(out_shape)
    specs[6] = pl.BlockSpec((8, width), lambda i, m: (0, 0))
    semaphores = count // TILE + ff // CHUNK + 1 + n + ff // CHUNK + 8 + 3 + n
    return pl.pallas_call(
        functools.partial(forward_kernel, n, rows),
        grid_spec=pltpu.PrefetchScalarGridSpec(
            num_scalar_prefetch=1,
            grid=(1,),
            in_specs=[pl.BlockSpec((16, width), lambda i, m: (0, 0))] + [any_spec] * (3 + n),
            out_specs=specs,
            scratch_shapes=[
                pltpu.VMEM((count, width), F32),
                pltpu.VMEM((count, width), BF),
                pltpu.VMEM((width, ff), BF),
                pltpu.VMEM((ff, width), BF),
                pltpu.VMEM((count, ff), BF),
                pltpu.VMEM((count, ff), BF),
                pltpu.VMEM((n, rows, local, width), BF),
                pltpu.VMEM((n, rows, local, width), BF),
                pltpu.VMEM((width, count), BF),
                pltpu.VMEM((width, count), BF),
                pltpu.VMEM((count, width), BF),
                pltpu.VMEM((width, count), BF),
                pltpu.VMEM(blocks, BF),
                pltpu.VMEM(blocks, BF),
                pltpu.SemaphoreType.DMA((semaphores,)),
            ],
        ),
        out_shape=[jax.ShapeDtypeStruct(shape, dtype) for shape, dtype in out_shape],
        compiler_params=pltpu.CompilerParams(vmem_limit_bytes=VMEM),
        cost_estimate=LONG,
        name="feed_forward",
    )(me, w["vec"], resid, w["wi"], w["wo2"], *up_blocks)


def backward_kernel(last, ndeps, me_ref, vec_ref, branch_ref, slope_ref, wi_ref, wo_ref, ht_ref, *refs):
    if last:
        (resid_ref, grad2_ref, partial_ref), refs = refs[:3], refs[3:]
    refs = refs[ndeps:]
    grad_out, acc_out, bi_out = refs[:3]
    refs = refs[3:]
    if last:
        (attn_out, sums_out, resid_s, grad2_s, attn_s), refs = refs[:5], refs[5:]
    branch_s, slope_s, wi_s, wo_s, ht_s, gi_s, acc_s, grad_s, sem = refs
    core, y, _ = place_of(me_ref)
    count, width = branch_s.shape
    tiles = count // TILE
    move = pltpu.make_async_copy
    chunk = lambda c: lines((y ^ c) * 2 + (core ^ (0 if last else 1)), CHUNK)
    branch_in, ht_in = move(branch_ref, branch_s, sem.at[0]), move(ht_ref, ht_s, sem.at[1])
    wo_in = lambda c: move(wo_ref.at[chunk(c)], wo_s.at[lines(c, CHUNK)], sem.at[2 + c])
    slope_in = lambda c: move(slope_ref.at[:, chunk(c)], slope_s.at[:, lines(c, CHUNK)], sem.at[4 + c])
    wi_in = lambda c: move(wi_ref.at[:, chunk(c)], wi_s.at[:, lines(c, CHUNK)], sem.at[6 + c])
    grad_to = lambda c: move(grad_s.at[c], grad_out.at[c], sem.at[8 + c])
    acc_to = lambda i: move(acc_s.at[lines(i, TILE)], acc_out.at[lines(i, TILE)], sem.at[10 + i])
    attn_to = lambda i: move(attn_s.at[lines(i, TILE)], attn_out.at[lines(i, TILE)], sem.at[10 + tiles + i])
    late_in = []
    if last:
        late_in = [move(partial_ref, acc_s, sem.at[10 + 2 * tiles])]
        late_in += [move(grad2_ref, grad2_s, sem.at[11 + 2 * tiles]), move(resid_ref, resid_s, sem.at[12 + 2 * tiles])]

    branch_in.start()
    wo_in(0).start()
    slope_in(0).start()
    ht_in.start()
    wo_in(1).start()
    slope_in(1).start()
    wi_in(0).start()
    wi_in(1).start()
    for copy in late_in:
        copy.start()
    branch_in.wait()

    def hidden_chunk(c, carry):
        cols = lines(c, CHUNK)
        wo_in(c).wait()
        slope_in(c).wait()
        back = lambda i: dot_nt(branch_s[i * TILE : (i + 1) * TILE, :], wo_s[cols, :])
        bias = jnp.zeros((1, CHUNK), F32)
        ahead = back(0)
        for i in range(tiles):
            at = slice(i * TILE, (i + 1) * TILE)
            gi = (ahead * slope_s[at, cols].astype(F32)).astype(BF)
            if i + 1 < tiles:
                ahead = back(i + 1)
            gi_s[at, cols] = gi
            bias = bias + jnp.sum(gi.astype(F32), 0, keepdims=True)
        bi_out[:, cols] = jnp.broadcast_to(bias, (8, CHUNK))

        @pl.when(c == 0)
        def _():
            ht_in.wait()

        for first in range(0, width, 192):
            product = dot_nn(ht_s[first : first + 192, :], gi_s[:, cols]).astype(BF)
            for p in range(2):
                grad_s[c, first // 96 + p] = product[p * 96 : p * 96 + 96, :]
        grad_to(c).start()
        return carry

    lax.fori_loop(0, 2, hidden_chunk, 0)
    wi_in(0).wait()
    wi_in(1).wait()
    for copy in late_in:
        copy.wait()
    gain = vec_ref[3:4, :]
    sums = [jnp.zeros((1, width), F32)] * 3
    back = lambda i: dot_nt(gi_s[i * TILE : (i + 1) * TILE, :], wi_s[...])
    ahead = back(0)
    for i in range(tiles):
        at = slice(i * TILE, (i + 1) * TILE)
        hidden = ahead
        if i + 1 < tiles:
            ahead = back(i + 1)
        if last:
            hidden = hidden + acc_s[at, :] + grad2_s[at, :]
            normed, inverse = norm_parts(resid_s[at, :])
            grad = norm_back(hidden * gain, normed, inverse)
            low = grad.astype(BF)
            acc_s[at, :] = grad
            attn_s[at, :] = low
            for q, piece in enumerate((hidden * normed, hidden, low.astype(F32))):
                sums[q] = sums[q] + jnp.sum(piece, 0, keepdims=True)
            attn_to(i).start()
        else:
            acc_s[at, :] = hidden
        acc_to(i).start()
    if last:
        sums_out[...] = jnp.concatenate(sums + [jnp.zeros((5, width), F32)], 0)
    for i in range(tiles):
        acc_to(i).wait()
        if last:
            attn_to(i).wait()
    for c in range(2):
        grad_to(c).wait()


def backward(me, last, branch, slope, ht, w, more, deps):
    count, width = branch.shape
    ff = w["wi"].shape[1]
    any_spec = pl.BlockSpec(memory_space=pl.ANY)
    row = lambda wide: pl.BlockSpec((8, wide), lambda i, m: (0, 0))
    out_shape = [((2, 8, 96, CHUNK), BF), ((count, width), F32), ((8, ff // 2), F32)]
    out_specs = [any_spec, any_spec, row(ff // 2)]
    scratch = []
    if last:
        out_shape += [((count, width), BF), ((8, width), F32)]
        out_specs += [any_spec, row(width)]
        scratch = [pltpu.VMEM((count, width), F32), pltpu.VMEM((count, width), F32), pltpu.VMEM((count, width), BF)]
    return pl.pallas_call(
        functools.partial(backward_kernel, last, len(deps)),
        grid_spec=pltpu.PrefetchScalarGridSpec(
            num_scalar_prefetch=1,
            grid=(1,),
            in_specs=[pl.BlockSpec((16, width), lambda i, m: (0, 0))] + [any_spec] * (5 + len(more) + len(deps)),
            out_specs=out_specs,
            scratch_shapes=scratch
            + [
                pltpu.VMEM((count, width), BF),
                pltpu.VMEM((count, 2 * CHUNK), BF),
                pltpu.VMEM((width, 2 * CHUNK), BF),
                pltpu.VMEM((2 * CHUNK, width), BF),
                pltpu.VMEM((width, count), BF),
                pltpu.VMEM((count, 2 * CHUNK), BF),
                pltpu.VMEM((count, width), F32),
                pltpu.VMEM((2, 8, 96, CHUNK), BF),
                pltpu.SemaphoreType.DMA((13 + 2 * (count // TILE),)),
            ],
        ),
        out_shape=[jax.ShapeDtypeStruct(shape, dtype) for shape, dtype in out_shape],
        compiler_params=pltpu.CompilerParams(vmem_limit_bytes=VMEM),
        cost_estimate=LONG,
        name="feed_forward_back" + ("_last" if last else ""),
    )(me, w["vec"], branch, slope, w["wi"], w["wo2"], ht, *more, *deps)


def attend_back_kernel(part, n, last, ndeps, me_ref, *refs):
    sources, refs = refs[:4], refs[4:]
    lse_ref, attn_ref, mq_ref, mk_ref, xt_ref, acc_ref = refs[:6]
    weights, refs = refs[6:10], refs[10:]
    if part == 0:
        (ctxt_ref, shares_ref), refs = refs[:2], refs[2:]
    refs = refs[ndeps:]
    keep_out, send_out, vec_out = refs[:3]
    tok_outs = refs[3 : 3 + (n if last else 1)]
    refs = refs[3 + len(tok_outs) :]
    heads_s, lse_s, attn_s, mask_s, xt_s, acc_s, wo_s, w_s, g_s, keep_s, send_s, vec_s, tok_s = refs[:13]
    if part == 0:
        ctxt_s, shares_s = refs[13:15]
    sem = refs[-1]
    _, y, place = place_of(me_ref)
    rows, length, width = attn_s.shape
    local = length // n
    move = pltpu.make_async_copy
    cols = [slice((part + 3 * i) * 128, (part + 3 * i) * 128 + 128) for i in range(2)]
    per_row = 14
    at_row = lambda r: lines(r, length)

    def early(r):
        copies = [move(attn_ref.at[at_row(r)], attn_s.at[r], sem.at[r * per_row])]
        for j, source in enumerate(sources):
            for i in range(2):
                copies.append(move(source.at[at_row(r), cols[i]], heads_s.at[r, j, i], sem.at[r * per_row + 1 + 2 * j + i]))
        copies.append(move(lse_ref.at[at_row(r)], lse_s.at[r], sem.at[r * per_row + 9]))
        copies.append(move(mq_ref.at[at_row(r)], mask_s.at[r, 0], sem.at[r * per_row + 10]))
        copies.append(move(mk_ref.at[at_row(r)], mask_s.at[r, 1], sem.at[r * per_row + 11]))
        return copies

    acc_in = lambda r: move(acc_ref.at[at_row(r)], acc_s.at[r], sem.at[r * per_row + 12])
    base = rows * per_row
    wo_in = [move(weights[0].at[cols[i]], wo_s.at[slice(i * 128, i * 128 + 128)], sem.at[base + i]) for i in range(2)]
    w_in = [
        move(weights[1 + j].at[:, cols[i]], w_s.at[j, :, slice(i * 128, i * 128 + 128)], sem.at[base + 2 + 2 * j + i])
        for j in range(3)
        for i in range(2)
    ]
    late_in = [move(xt_ref, xt_s, sem.at[base + 8])]
    if part == 0:
        late_in += [move(ctxt_ref, ctxt_s, sem.at[base + 9]), move(shares_ref, shares_s, sem.at[base + 10])]
    at_tok, at_out = base + 11, base + 11 + rows * n

    def tok_to(r):
        if last:
            return [
                move(tok_s.at[r, lines(k, local)], tok_outs[k].at[r], sem.at[at_tok + r * n + k]) for k in range(n)
            ]
        return [move(acc_s.at[r], tok_outs[0].at[at_row(r)], sem.at[at_tok + r * n])]

    for copy in wo_in + early(0) + w_in + [acc_in(0)]:
        copy.start()
    for r in range(1, rows):
        for copy in early(r) + [acc_in(r)]:
            copy.start()
    for copy in late_in:
        copy.start()
    for copy in wo_in:
        copy.wait()

    lanes = lane_of((length, 128))
    low = lanes < 64
    spot = lanes % 64
    ones = jnp.where((spot >= 4) & (spot < 7), 1.0, 0.0).astype(BF)

    def split3(column):
        high = column.astype(BF)
        rest = column - high.astype(F32)
        middle = rest.astype(BF)
        return high, middle, (rest - middle.astype(F32)).astype(BF)

    def with_columns(base, column):
        for i, piece in enumerate(split3(-column)):
            base = jnp.where(spot == 4 + i, piece, base)
        return base

    block = 256

    def one_row(row, carry):
        for copy in early(row):
            copy.wait()
        mq, mk = mask_s[row, 0], mask_s[row, 1]
        lse_all = lse_s[row]
        grad_ctx = dot_nt(attn_s[row], wo_s[...]).astype(BF)
        items = [(pair, half, first) for pair in range(2) for half in range(2) for first in range(0, length, block)]
        pairs, halves_of = [], {}
        for pair in range(2):
            q2, k2, v2, ctx2 = (heads_s[row, j, pair] for j in range(4))
            do2 = grad_ctx[:, pair * 128 : pair * 128 + 128]
            pairs.append((q2, k2, v2, do2, do2.astype(F32) * ctx2.astype(F32)))

        def operands(pair, half):
            if (pair, half) not in halves_of:
                q2, k2, v2, do2, both = pairs[pair]
                mine = low if half == 0 else jnp.logical_not(low)
                head = (part + 3 * pair) * 2 + half
                delta = jnp.sum(jnp.where(mine, both, 0.0), -1, keepdims=True)
                halves_of[pair, half] = (
                    jnp.where(mine, q2, with_columns(mq, lse_all[:, head : head + 1])),
                    jnp.where(mine, do2, with_columns(jnp.zeros_like(mq), delta)),
                    jnp.where(mine, k2, mk),
                    jnp.where(mine, v2, ones),
                )
            return halves_of[pair, half]

        def products(pair, half, first):
            q_ext, do_ext, k_ext, v_ext = operands(pair, half)
            at = slice(first, first + block)
            return dot_nt(k_ext[at], q_ext), dot_nt(v_ext[at], do_ext)

        dq, dk, dv = {}, {}, {}
        ahead = products(*items[0])
        for i, (pair, half, first) in enumerate(items):
            power, slope = ahead
            if i + 1 < len(items):
                ahead = products(*items[i + 1])
            q2, k2, _, do2, _ = pairs[pair]
            prob = jnp.exp(power)
            ds = (prob * slope).astype(BF)
            key = (pair, half)
            dv.setdefault(key, []).append(dot_nn(prob.astype(BF), do2))
            dk.setdefault(key, []).append(dot_nn(ds, q2))
            add = dot_tn(ds, k2[first : first + block])
            dq[key] = dq[key] + add if key in dq else add
        for pair in range(2):
            at = slice(pair * 128, pair * 128 + 128)
            g_s[row, 0, :, at] = (jnp.where(low, dq[pair, 0], dq[pair, 1]) * 0.125).astype(BF)
            for j, pieces in ((1, dk), (2, dv)):
                whole = [jnp.concatenate(pieces[pair, half], 0) for half in range(2)]
                g_s[row, j, :, at] = jnp.where(low, whole[0], whole[1]).astype(BF)

        @pl.when(row == 0)
        def _():
            for copy in w_in:
                copy.wait()

        acc_in(row).wait()
        token = acc_s[row]
        for j in range(3):
            token = token + dot_nt(g_s[row, j], w_s[j])
        if last:
            tok_s[row] = token.astype(BF)
        else:
            acc_s[row] = token
        for copy in tok_to(row):
            copy.start()
        return carry

    lax.fori_loop(0, rows, one_row, 0)
    for copy in late_in:
        copy.wait()
    count = 6 if part == 0 else 3
    sums = [sum(jnp.sum(g_s[r, j].astype(F32), 0, keepdims=True) for r in range(rows)) for j in (0, 2)]
    vec_s[...] = jnp.concatenate(sums + [jnp.zeros((6, 256), F32)], 0)
    bias = vec_s[...]
    bias = jnp.concatenate([bias[:, :128], bias[:, 128:]], 0).astype(BF)
    for out in (keep_s, send_s):
        for yy in range(2):
            for p in range(8):
                out[yy, p, count * 48 : count * 48 + 16, :] = bias
                if part == 0:
                    out[yy, p, count * 48 + 16 : count * 48 + 32, :] = shares_s[place ^ dp_rel(p)]

    def place_blocks(product, yy, j, first):
        for c, out in ((0, keep_s), (1, send_s)):
            for p in range(8):
                out[yy ^ y, p, j * 48 : (j + 1) * 48, :] = product[(c * 8 + p) * 48 : (c * 8 + p + 1) * 48, first : first + 128]

    for j in range(3):
        product = sum(dot_nn(xt_s[r].reshape(width, length), g_s[r, j]) for r in range(rows)).astype(BF)
        for yy in range(2):
            place_blocks(product, yy, j, yy * 128)
    if part == 0:
        for yy in range(2):
            at = slice(yy * 384, yy * 384 + 384)
            product = sum(dot_nn(ctxt_s[r].reshape(width, length), attn_s[r, :, at]) for r in range(rows)).astype(BF)
            for j in range(3):
                place_blocks(product, yy, 3 + j, j * 128)
    out_copies = [move(send_s, send_out, sem.at[at_out]), move(keep_s, keep_out, sem.at[at_out + 1])]
    out_copies.append(move(vec_s, vec_out, sem.at[at_out + 2]))
    for copy in out_copies:
        copy.start()
    for r in range(rows):
        for copy in tok_to(r):
            copy.wait()
    for copy in out_copies:
        copy.wait()


def attend_back(me, part, n, rows, saved, attn, acc, w, extra, deps):
    q, k, v, ctx, lse, xt, ctxt, mq, mk = saved
    count, width = attn.shape
    length = count // rows
    local = length // n
    last = part == 2
    shape = (2, 8, (6 if part == 0 else 3) * 48 + (32 if part == 0 else 16), 128)
    if last:
        tok_shape = [jax.ShapeDtypeStruct((rows, local, width), BF)] * n
    else:
        tok_shape = [jax.ShapeDtypeStruct((count, width), F32)]
    more = (ctxt, extra) if part == 0 else ()
    any_spec = pl.BlockSpec(memory_space=pl.ANY)
    inputs = (q, k, v, ctx, lse, attn, mq, mk, xt, acc, w["wo"], w["wq"], w["wk"], w["wv"], *more, *deps)
    scratch = [
        pltpu.VMEM((rows, 4, 2, length, 128), BF),
        pltpu.VMEM((rows, length, 128), F32),
        pltpu.VMEM((rows, length, width), BF),
        pltpu.VMEM((rows, 2, length, 128), BF),
        pltpu.VMEM(xt.shape, BF),
        pltpu.VMEM((rows, length, width), F32),
        pltpu.VMEM((256, width), BF),
        pltpu.VMEM((3, width, 256), BF),
        pltpu.VMEM((rows, 3, length, 256), BF),
        pltpu.VMEM(shape, BF),
        pltpu.VMEM(shape, BF),
        pltpu.VMEM((8, 256), F32),
        pltpu.VMEM((rows, length, width), BF),
    ]
    if part == 0:
        scratch += [pltpu.VMEM(ctxt.shape, BF), pltpu.VMEM((8, 16, 128), BF)]
    out_shape = [jax.ShapeDtypeStruct(shape, BF)] * 2 + [jax.ShapeDtypeStruct((8, 256), F32)] + tok_shape
    return pl.pallas_call(
        functools.partial(attend_back_kernel, part, n, last, len(deps)),
        grid_spec=pltpu.PrefetchScalarGridSpec(
            num_scalar_prefetch=1,
            grid=(1,),
            in_specs=[any_spec] * len(inputs),
            out_specs=[any_spec] * len(out_shape),
            scratch_shapes=scratch + [pltpu.SemaphoreType.DMA((14 * rows + 11 + rows * n + 3,))],
        ),
        out_shape=out_shape,
        compiler_params=pltpu.CompilerParams(vmem_limit_bytes=VMEM),
        cost_estimate=LONG,
        name=f"attend_back{part}",
    )(me, *inputs)


def swap(array, axis, mask):
    size = lax.axis_size(axis)
    return lax.ppermute(array, axis, [(i, i ^ mask) for i in range(size)])


def pack_tokens(place, tokens, segments, row):
    n = lax.axis_size("seq")
    own, local, width = tokens.shape[0] // n, tokens.shape[1], tokens.shape[2]

    def kernel(me_ref, seg_ref, *refs):
        for k in range(n):
            source, out = refs[k], refs[n + k]
            out[0, :local, :] = source[0]
            out[0, local:, :] = jnp.zeros((16, width), BF)
            at = (me_ref[0] ^ k) * own
            ids = jnp.concatenate([seg_ref[pl.ds(at + r, 1), :] for r in range(own)] + [seg_ref[:1, :]] * (16 - own), 0)
            out[0, local:, :local] = ids.astype(F32).astype(BF)

    return pl.pallas_call(
        kernel,
        grid_spec=pltpu.PrefetchScalarGridSpec(
            num_scalar_prefetch=1,
            grid=(1,),
            in_specs=[pl.BlockSpec(segments.shape, lambda i, m: (0, 0))]
            + [pl.BlockSpec((1, local, width), lambda i, m, k=k: ((m[0] ^ k) * own + row, 0, 0)) for k in range(n)],
            out_specs=[pl.BlockSpec((1, local + 16, width), lambda i, m: (0, 0, 0))] * n,
        ),
        out_shape=[jax.ShapeDtypeStruct((1, local + 16, width), BF)] * n,
        compiler_params=pltpu.CompilerParams(vmem_limit_bytes=VMEM),
        cost_estimate=TINY,
        name="pack_first",
    )(place, segments, *[tokens] * n)


def pack_rest(place, tokens, cotangent, first_row, deps):
    n = lax.axis_size("seq")
    own, local, width = tokens.shape[0] // n, tokens.shape[1], tokens.shape[2]
    rows = range(first_row, own)
    count = len(rows) * n + n

    def kernel(me_ref, *refs):
        for source, out in zip(refs[:count], refs[count + len(deps) :]):
            out[...] = source[...]

    one = [
        pl.BlockSpec((1, local, width), lambda i, m, k=k, r=r: ((m[0] ^ k) * own + r, 0, 0))
        for r in rows
        for k in range(n)
    ]
    many = [pl.BlockSpec((own, local, width), lambda i, m, k=k: (m[0] ^ k, 0, 0)) for k in range(n)]
    return pl.pallas_call(
        kernel,
        grid_spec=pltpu.PrefetchScalarGridSpec(
            num_scalar_prefetch=1,
            grid=(1,),
            in_specs=one + many + [pl.BlockSpec(memory_space=pl.ANY)] * len(deps),
            out_specs=[pl.BlockSpec((1, local, width), lambda i, m: (0, 0, 0))] * len(one)
            + [pl.BlockSpec((own, local, width), lambda i, m: (0, 0, 0))] * n,
        ),
        out_shape=[jax.ShapeDtypeStruct((1, local, width), BF)] * len(one)
        + [jax.ShapeDtypeStruct((own, local, width), BF)] * n,
        compiler_params=pltpu.CompilerParams(vmem_limit_bytes=VMEM),
        cost_estimate=TINY,
        name="pack_rest",
    )(place, *[tokens] * len(one), *[cotangent] * n, *deps)


def unpack(place, blocks, deps=()):
    n = len(blocks)
    own, local, width = blocks[0].shape

    any_spec = pl.BlockSpec(memory_space=pl.ANY)

    def kernel(me_ref, *refs):
        sources, (out, held, sem) = refs[:n], refs[n + len(deps) :]
        ins = [pltpu.make_async_copy(sources[k], held.at[k], sem.at[k]) for k in range(n)]
        outs = [
            pltpu.make_async_copy(held.at[k], out.at[pl.ds((me_ref[0] ^ k) * own, own)], sem.at[n + k]) for k in range(n)
        ]
        for copy in ins:
            copy.start()
        for k in range(n):
            ins[k].wait()
            outs[k].start()
        for copy in outs:
            copy.wait()

    return pl.pallas_call(
        kernel,
        grid_spec=pltpu.PrefetchScalarGridSpec(
            num_scalar_prefetch=1,
            grid=(1,),
            in_specs=[any_spec] * (n + len(deps)),
            out_specs=any_spec,
            scratch_shapes=[pltpu.VMEM((n, own, local, width), blocks[0].dtype), pltpu.SemaphoreType.DMA((2 * n,))],
        ),
        out_shape=jax.ShapeDtypeStruct((own * n, local, width), blocks[0].dtype),
        compiler_params=pltpu.CompilerParams(vmem_limit_bytes=VMEM),
        cost_estimate=TINY,
        name="unpack_rows",
    )(place, *blocks, *deps)


def exchange(blocks):
    return [swap(block, "seq", k) if k else block for k, block in enumerate(blocks)]


def bits_of(size):
    return [1 << b for b in range(size.bit_length() - 1)]


def reduce_matrix(grad):
    sn, dn = lax.axis_size("seq"), lax.axis_size("dp")
    ms, md = lax.axis_index("seq"), lax.axis_index("dp")
    high, wide = grad.shape[0] // dn, grad.shape[1] // sn
    blocks = grad.astype(BF).reshape(dn, high, sn, wide).transpose(2, 0, 1, 3)
    blocks = jnp.take(blocks, ms ^ jnp.arange(sn), axis=0)
    blocks = jnp.take(blocks, md ^ jnp.arange(dn), axis=1)
    left = {"seq": sn, "dp": dn}
    for axis, mask in [("seq", m) for m in bits_of(sn)] + [("dp", m) for m in bits_of(dn)]:
        size = left[axis]
        dim = 0 if axis == "seq" else 1
        split = blocks.reshape(blocks.shape[:dim] + (size // 2, 2) + blocks.shape[dim + 1 :])
        keep = lax.index_in_dim(split, 0, dim + 1, keepdims=False)
        send = lax.index_in_dim(split, 1, dim + 1, keepdims=False)
        blocks = keep + swap(send, axis, mask)
        left[axis] = size // 2
    return blocks.reshape(high, wide).astype(F32)


def reduce_vectors(vectors):
    for axis in ("seq", "dp"):
        for mask in bits_of(lax.axis_size(axis)):
            vectors = vectors + swap(vectors, axis, mask)
    return vectors


def my_share(vector):
    own = vector.shape[0] // lax.axis_size("dp")
    return lax.dynamic_slice_in_dim(vector, lax.axis_index("dp") * own, own, 0)


X, Y = ("dp", 1), ("seq", 2)


def stage(name, work, arrays, shapes, deps=(), place=None, room=24 * MIB):
    scalars = [] if place is None else [place]

    def kernel(*refs):
        lead, refs = refs[: len(scalars)], refs[len(scalars) :]
        work(*lead, *refs[: len(arrays)], *refs[len(arrays) + len(deps) :])

    full = lambda shape: pl.BlockSpec(shape, lambda i, *m: (0,) * len(shape))
    return pl.pallas_call(
        kernel,
        grid_spec=pltpu.PrefetchScalarGridSpec(
            num_scalar_prefetch=len(scalars),
            grid=(1,),
            in_specs=[full(a.shape) for a in arrays] + [pl.BlockSpec(memory_space=pl.ANY)] * len(deps),
            out_specs=[full(shape) for shape, _ in shapes],
        ),
        out_shape=[jax.ShapeDtypeStruct(shape, dtype) for shape, dtype in shapes],
        compiler_params=pltpu.CompilerParams(vmem_limit_bytes=room),
        cost_estimate=LONG,
        name=name,
    )(*scalars, *arrays, *deps)


def halves(kept, came, keep_out, send_out, lead, rows=None):
    tail = () if rows is None else (Ellipsis, rows, slice(None))
    for i, out in ((0, keep_out), (1, send_out)):
        at = (slice(None),) * lead + (i,) + tail
        out[...] = kept[at] + came[at]


def body(
    tokens,
    cotangent,
    segments,
    w_query,
    b_query,
    w_key,
    w_value,
    b_value,
    w_out,
    b_out,
    gain_one,
    shift_one,
    w_inner,
    b_inner,
    w_outer,
    b_outer,
    gain_two,
    shift_two,
):
    width = tokens.shape[-1]
    n, dn = lax.axis_size("seq"), lax.axis_size("dp")
    ms, md = lax.axis_index("seq"), lax.axis_index("dp")
    fast = n == 4 and dn == 8
    me = (jnp.stack([ms % 2, ms // 2, md]) if fast else jnp.zeros((3,))).astype(jnp.int32)
    seq_place = ms.astype(jnp.int32).reshape(1)
    rows, local = tokens.shape[0] // n, tokens.shape[1]
    length = n * local
    vectors = (b_query, b_value, b_out, gain_one, shift_one, gain_two, shift_two, b_outer, b_inner)
    packed = jnp.concatenate(vectors + (jnp.zeros((4 * width,), BF),)).reshape(16, width).astype(F32)
    w = dict(wq=w_query, wk=w_key, wv=w_value, wo=w_out, wi=w_inner, wo2=w_outer, vec=packed)

    first_blocks = pack_tokens(seq_place, tokens, segments, 0)
    x_blocks = [exchange(first_blocks)]
    seg_blocks = x_blocks[0]
    rest = pack_rest(seq_place, tokens, cotangent, 1, first_blocks[:1])
    for r in range(1, rows):
        x_blocks.append(exchange(rest[(r - 1) * n : r * n]))
    up_blocks = exchange(rest[(rows - 1) * n :])

    before = None
    for r in range(rows):
        before = attend(me, r, rows, x_blocks[r], seg_blocks, w, before)
    q, k, v, ctx, lse, resid, xt, ctxt, mq, mk = before
    slope, branch, grad2, ht, outer_keep, outer_send, vec2, *y_blocks = forward(me, rows, resid, up_blocks, w)
    outer = (outer_keep, outer_send)
    y_blocks = exchange(y_blocks)
    inner_send, partial, bi_send = backward(me, False, branch, slope, ht, w, [], [])
    saved = (q, k, v, ctx, lse, xt, ctxt, mq, mk)

    if not fast:
        inner_keep, grad1, bi_keep, attn, vec1 = backward(me, True, branch, slope, ht, w, [resid, grad2, partial], [])
        shares = jnp.zeros((8, 16, 128), BF)
        early = jnp.concatenate([vec2[:3], vec1[:3]], 0)
        vec_bi = jnp.stack([bi_keep[0].reshape(2, -1), bi_send[0].reshape(2, -1)], 1).reshape(1, -1)
        parts, vec_parts = [], []
        acc = grad1
        for part in range(3):
            keep, send, vec, *tail = attend_back(me, part, n, rows, saved, attn, acc, w, shares, [])
            parts.append((keep, send))
            vec_parts.append(vec)
            acc = tail[0]
        output = unpack(seq_place, y_blocks)
        grad_tokens = unpack(seq_place, exchange(tail))
        early = reduce_vectors(jnp.concatenate([early, vec_bi[:1].reshape(4, width)], 0))
        late = jnp.stack([p[:2] for p in vec_parts], 1).reshape(2, 3, 2, 128)
        late = reduce_vectors(late.transpose(0, 2, 1, 3).reshape(2, width))
        stack = lambda pair: jnp.stack(list(pair))
        outer_t = stack(outer).reshape(2, 2, 2, 4, 96, 2, 384).transpose(1, 0, 5, 4, 3, 2, 6).reshape(width, -1)
        inner_b = stack((inner_keep, inner_send)).reshape(2, 2, 2, 4, 96, -1).transpose(3, 2, 4, 1, 0, 5)
        inner_b = inner_b.reshape(width, -1)
        three = [stack(pair)[:, :, :, -160:-16] if i else stack(pair)[:, :, :, :144] for i, pair in enumerate(parts)]
        qkv = jnp.stack(three).reshape(3, 2, 2, 2, 4, 3, 48, 128).transpose(5, 4, 3, 1, 6, 2, 0, 7).reshape(3, width, width)
        out_b = stack(parts[0])[:, :, :, 144:288].reshape(2, 2, 2, 4, 3, 48, 128).transpose(3, 2, 0, 5, 1, 4, 6)
        grad_w_outer = reduce_matrix(outer_t.T)
        grad_w_inner = reduce_matrix(inner_b)
        grad_w_out = reduce_matrix(out_b.reshape(width, width))
        grad_w_query, grad_w_key, grad_w_value = (reduce_matrix(qkv[i]) for i in range(3))
        b_query_g, b_value_g = my_share(late[0]), my_share(late[1])
        gain2_g, shift2_g, b_outer_g, gain1_g, shift1_g, b_out_g = (my_share(early[i]) for i in range(6))
        b_inner_g = my_share(early[6:10].reshape(-1))
    else:
        by_axes = lambda a: a.reshape((2, 2, 4) + a.shape[2:])
        one = lambda *shape: (shape, BF)
        top, low = slice(0, 48), slice(48, 96)
        z_swap = lambda pieces: [pieces[0]] + [swap(pieces[j], "dp", 2 * j) for j in (1, 2, 3)]
        first_shapes, second_shapes, z_shapes = [one(2, 4, 48, 768)] * 4, [one(4, 48, 768)] * 4, [one(192, 768)] * 4

        def z_split(first, top_keep, top_came, low_keep, low_came, outs):
            for j, out in enumerate(outs):
                out[first : first + 48, :] = top_keep[j] + top_came[j]
                out[first + 48 : first + 96, :] = low_keep[j] + low_came[j]

        outer_came = swap(outer[1], "seq", 1)

        def stage_a(kept, came, a_keep, a_send, b_keep, b_send):
            halves(kept, came, a_keep, a_send, 1, top)
            halves(kept, came, b_keep, b_send, 0, low)

        a_keep, a_send, b_keep, b_send = stage(
            "stage_a", stage_a, [outer[0], outer_came], first_shapes, [inner_send], room=VMEM
        )

        a_came, b_came = swap(a_send, *X), swap(b_send, *Y)
        inner_came = swap(inner_send, "seq", 1)
        inner_keep, grad1, bi_keep, attn, vec1 = backward(
            me, True, branch, slope, ht, w, [resid, grad2, partial], [a_keep, *y_blocks]
        )

        def stage_b(
            me_ref, a_keep, a_came, b_keep, b_came, i_keep, i_came, vec2, vec1, bi_keep, bi_send,
            a2_keep, a2_send, b2_keep, b2_send, c_keep, c_send, d_keep, d_send, shares,
        ):
            halves(a_keep, a_came, a2_keep, a2_send, 0)
            halves(b_keep, b_came, b2_keep, b2_send, 0)
            halves(i_keep, i_came, c_keep, c_send, 1, top)
            halves(i_keep, i_came, d_keep, d_send, 0, low)
            vector_shares(me_ref, vec2, vec1, bi_keep, bi_send, shares)

        def vector_shares(me_ref, vec2, vec1, bi_keep, bi_send, shares):
            early = jnp.concatenate([vec2[0:3], vec1[0:3]], 0)
            kept, sent = bi_keep[0:1], bi_send[0:1]
            blank = jnp.zeros((6, 32), F32)
            for d in range(8):
                core, y = me_ref[0], me_ref[1]
                at = slice((d % 2) * 384, (d % 2) * 384 + 384)
                other = slice(768 + at.start, 768 + at.stop)
                own_core = core == (d // 2) % 2
                own_y = y == d // 4
                piece = jnp.where(
                    own_core,
                    jnp.where(own_y, kept[:, at], kept[:, other]),
                    jnp.where(own_y, sent[:, at], sent[:, other]),
                )
                rows = [jnp.concatenate([early[:, d * 96 : d * 96 + 96], blank], 1)]
                rows += [piece[:, j * 128 : j * 128 + 128] for j in range(3)] + [jnp.zeros((7, 128), F32)]
                shares[d] = jnp.concatenate(rows, 0).astype(BF)

        *stage_b_outs, shares = stage(
            "stage_b",
            stage_b,
            [a_keep, a_came, b_keep, b_came, by_axes(inner_keep), by_axes(inner_came), vec2, vec1, bi_keep, bi_send],
            second_shapes + first_shapes + [one(8, 16, 128)],
            place=me,
            room=VMEM,
        )
        a_keep, a_send, b_keep, b_send, c_keep, c_send, d_keep, d_send = stage_b_outs

        a_came, b_came = swap(a_send, *Y), swap(b_send, *X)
        c_came, d_came = swap(c_send, *X), swap(d_send, *Y)
        keep0, send0, vec_0, acc = attend_back(me, 0, n, rows, saved, attn, grad1, w, shares, [a_keep])

        def stage_c(c_keep, c_came, d_keep, d_came, *outs):
            halves(c_keep, c_came, outs[0], outs[1], 0)
            halves(d_keep, d_came, outs[2], outs[3], 0)

        c_keep, c_send, d_keep, d_send = stage(
            "stage_c",
            stage_c,
            [c_keep, c_came, d_keep, d_came],
            second_shapes,
            [keep0, a_came, b_came],
            room=VMEM,
        )

        c_came, d_came = swap(c_send, *Y), swap(d_send, *X)
        came0 = swap(send0, "seq", 1)
        keep1, send1, vec_1, acc = attend_back(me, 1, n, rows, saved, attn, acc, w, None, [c_keep])

        def stage_d(a_keep, a_came, b_keep, b_came, c_keep, c_came, d_keep, d_came, keep0, came0, *outs):
            z_split(0, a_keep, a_came, b_keep, b_came, outs[:4])
            z_split(96, c_keep, c_came, d_keep, d_came, outs[:4])
            halves(keep0, came0, outs[4], outs[5], 0)

        *forward_z, p0_keep, p0_send = stage(
            "stage_d",
            stage_d,
            [a_keep, a_came, b_keep, b_came, c_keep, c_came, d_keep, d_came, by_axes(keep0), by_axes(came0)],
            z_shapes + [one(2, 4, 320, 128)] * 2,
            [keep1],
            room=VMEM,
        )

        p0_came = swap(p0_send, *Y)
        came1 = swap(send1, "seq", 1)
        forward_z = z_swap(forward_z)
        keep2, send2, vec_2, *tok_blocks = attend_back(me, 2, n, rows, saved, attn, acc, w, None, [p0_keep])

        came2 = swap(send2, "seq", 1)
        tok_blocks = exchange(tok_blocks)
        add = lambda four: sum(r[...].astype(F32) for r in four)
        x_split = lambda kept, came, a, b: halves(kept, came, a, b, 1)
        y_split = lambda kept, came, a, b: halves(kept, came, a, b, 0)
        quarter, eighth = [one(2, 4, 160, 128)] * 2, [one(4, 160, 128)] * 2

        def stage_e(p0_keep, p0_came, keep1, came1, *outs):
            halves(p0_keep, p0_came, outs[0], outs[1], 0)
            halves(keep1, came1, outs[2], outs[3], 0)

        p0_keep, p0_send, p1_keep, p1_send = stage(
            "stage_e",
            stage_e,
            [p0_keep, p0_came, by_axes(keep1), by_axes(came1)],
            [one(4, 320, 128)] * 2 + quarter,
            [keep2, *forward_z[1:]],
        )
        p1_came, p0_came = swap(p1_send, *Y), swap(p0_send, *X)
        p2_keep, p2_send = stage(
            "stage_f", x_split, [by_axes(keep2), by_axes(came2)], quarter, [p1_keep]
        )
        p2_came = swap(p2_send, *X)

        def forward_grads(*refs):
            total = add(refs[0:4])
            refs[4][0:96, :] = total[:96, :384]
            refs[4][96:192, :] = total[:96, 384:]
            refs[5][...] = total[96:]

        grad_w_outer, grad_w_inner = stage(
            "forward_grads", forward_grads, forward_z, [((192, 384), F32), ((96, 768), F32)], [p2_keep]
        )
        grad_w_outer = grad_w_outer.T
        output = unpack(seq_place, y_blocks, [grad_w_inner])

        p1_keep, p1_send = stage("stage_g", y_split, [p1_keep, p1_came], eighth, [output])
        p1_came = swap(p1_send, *X)
        p2_keep, p2_send = stage(
            "stage_h", y_split, [p2_keep, p2_came], eighth, [p1_keep, tok_blocks[2]]
        )
        p2_came = swap(p2_send, *Y)

        def stage_i(p0_keep, p0_came, p1_keep, p1_came, p2_keep, p2_came, *outs):
            for j in range(4):
                outs[j][0:320, :] = p0_keep[j] + p0_came[j]
                outs[j][320:480, :] = p1_keep[j] + p1_came[j]
                outs[j][480:640, :] = p2_keep[j] + p2_came[j]

        z_pieces = z_swap(
            stage(
                "stage_i", stage_i, [p0_keep, p0_came, p1_keep, p1_came, p2_keep, p2_came], [one(640, 128)] * 4
            )
        )
        grad_tokens = unpack(seq_place, tok_blocks)

        def gather_up(me_ref, *refs):
            total = add(refs[0:4])
            z0, z12 = total[0:320], total[320:640]
            mine, other, bq_out, bv_out, bi_out, *vec_outs = refs[4:]
            place = me_ref[2]
            for i, out in enumerate(vec_outs):
                out[...] = z0[304 + i : 305 + i, 0:96]
            bi_out[...] = jnp.concatenate([z0[310 + j : 311 + j] for j in range(3)], 1)
            first_rows = [z0[288:304], z12[144:160], z12[304:320]]
            for i, out in enumerate((bq_out, bv_out)):
                whole = [first_rows[j % 3][(j // 3) * 8 + i : (j // 3) * 8 + i + 1] for j in range(6)]
                whole = jnp.concatenate(whole, 1)
                total = jnp.zeros((1, 96), F32)
                for d in range(8):
                    total = jnp.where(place == d, whole[:, d * 96 : d * 96 + 96], total)
                out[...] = total
            rows = lambda z, first: [z[first + 48 * j : first + 48 * j + 48] for j in range(3)]
            out_w = rows(z0, 144)
            parts = [rows(z0, 0), rows(z12, 0), rows(z12, 160)]
            for i in range(4):
                pieces = out_w if i == 0 else [part[i - 1] for part in parts]
                whole = jnp.concatenate(pieces, 1)
                left, right = whole[:, :192], whole[:, 192:]
                first = me_ref[0] == 0
                mine[i] = jnp.where(first, left, right)
                other[i] = jnp.where(first, right, left).astype(BF)

        mine, other, b_query_g, b_value_g, b_inner_g, *vecs = stage(
            "gather_up",
            gather_up,
            z_pieces,
            [((4, 48, 192), F32), ((4, 48, 192), BF), ((1, 96), F32), ((1, 96), F32), ((1, 384), F32)]
            + [((1, 96), F32)] * 6,
            [grad_tokens],
            place=me,
        )
        other = swap(other, "seq", 1)

        def assemble(me_ref, mine, other, *outs):
            for i, out in enumerate(outs):
                kept, came = mine[i], other[i].astype(F32)
                first = me_ref[0] == 0
                out[0:48, :] = jnp.where(first, kept, came)
                out[48:96, :] = jnp.where(first, came, kept)

        grad_w_out, grad_w_query, grad_w_key, grad_w_value = stage(
            "assemble", assemble, [mine, other], [((96, 192), F32)] * 4, place=me
        )
        b_query_g, b_value_g, b_inner_g = (v.reshape(-1) for v in (b_query_g, b_value_g, b_inner_g))
        gain2_g, shift2_g, b_outer_g, gain1_g, shift1_g, b_out_g = (v.reshape(-1) for v in vecs)

    return (
        output,
        grad_tokens,
        grad_w_query,
        b_query_g,
        grad_w_key,
        grad_w_value,
        b_value_g,
        grad_w_out,
        b_out_g,
        gain1_g,
        shift1_g,
        grad_w_inner,
        b_inner_g,
        grad_w_outer,
        b_outer_g,
        gain2_g,
        shift2_g,
    )


def solution(mesh):
    token = P("dp", "seq", None)
    matrix = P("dp", "seq")
    vector = P("dp")
    return jax.shard_map(
        body,
        mesh=mesh,
        in_specs=(token, token, P("dp", "seq")) + (P(),) * 15,
        out_specs=(
            token,
            token,
            matrix,
            vector,
            matrix,
            matrix,
            vector,
            matrix,
            vector,
            vector,
            vector,
            matrix,
            vector,
            matrix,
            vector,
            vector,
            vector,
        ),
        check_vma=False,
    )
```

```python
import functools

import jax
import jax.numpy as jnp
from jax import lax
from jax.experimental import pallas as pl
from jax.experimental.pallas import tpu as pltpu
from jax.sharding import PartitionSpec as P

HEADS = 12
BF = jnp.bfloat16
F32 = jnp.float32
MIB = 1 << 20
VMEM = 60 * MIB
LONG = pl.CostEstimate(flops=60_000_000_000, bytes_accessed=1, transcendentals=0)
TINY = pl.CostEstimate(flops=1, bytes_accessed=1, transcendentals=0)


def dot_nn(a, b):
    return lax.dot_general(a, b, (((1,), (0,)), ((), ())), preferred_element_type=F32)


def dot_nt(a, b):
    return lax.dot_general(a, b, (((1,), (1,)), ((), ())), preferred_element_type=F32)


def dot_tn(a, b):
    return lax.dot_general(a, b, (((0,), (0,)), ((), ())), preferred_element_type=F32)


def normal_laws(a):
    gauss = jnp.exp(a * a * -0.5)
    return 0.5 + 0.5 * lax.erf(a * 0.7071067811865476), a * (gauss * 0.3989422804014327)


def norm_parts(values):
    mean = jnp.mean(values, -1, keepdims=True)
    centred = values - mean
    inverse = lax.rsqrt(jnp.mean(centred * centred, -1, keepdims=True) + 1e-05)
    return centred * inverse, inverse


def norm_back(scaled, normed, inverse):
    return inverse * (
        scaled
        - jnp.mean(scaled, -1, keepdims=True)
        - normed * jnp.mean(scaled * normed, -1, keepdims=True)
    )


def lines(index, size):
    return pl.ds(pl.multiple_of(index * size, size), size)


def lane_of(shape):
    return lax.broadcasted_iota(jnp.int32, shape, 1)


def place_of(me_ref):
    return me_ref[0], me_ref[1], me_ref[2]


def dp_rel(position):
    return (position % 4) * 2 + position // 4


def split_rows(position_c, position_d, me):
    core, _, place = me
    return pl.multiple_of((place ^ dp_rel(position_d)) * 96 + (core ^ position_c) * 48, 16)


def attend_kernel(n, row, aliased, local, me_ref, *refs):
    x_refs, seg_refs, refs = refs[:n], refs[n : 2 * n], refs[2 * n :]
    w_refs, (wo_ref, vec_ref), refs = refs[:3], refs[3:5], refs[5 + aliased :]
    outs, refs = refs[:10], refs[10:]
    x_s, seg_s, w_s, wo_s, vec_s, qkvc_s, lse_s, resid_s, t_s, xt_s, ctxt_s, mask_s, sem = refs
    q_out, k_out, v_out, ctx_out, lse_out, resid_out, xt_out, ctxt_out, mq_out, mk_out = outs
    length, width = x_s.shape
    groups = width // 256
    me = place_of(me_ref)
    move = pltpu.make_async_copy
    here = slice(row * length, (row + 1) * length)
    x_in = [move(x_refs[k].at[0, slice(0, local)], x_s.at[slice(k * local, (k + 1) * local)], sem.at[k]) for k in range(n)]
    seg_in = [move(seg_refs[k].at[0, slice(local, local + 16)], seg_s.at[k], sem.at[n + k]) for k in range(n)]
    wo_in, vec_in = move(wo_ref, wo_s, sem.at[2 * n]), move(vec_ref, vec_s, sem.at[2 * n + 1])
    at_w = 2 * n + 2

    def w_in(g):
        cols = lines(g, 256)
        return [move(w_refs[j].at[:, cols], w_s.at[j, :, cols], sem.at[at_w + 3 * g + j]) for j in range(3)]

    at_out = at_w + 3 * groups

    def qkvc_to(g):
        cols = lines(g, 256)
        return [
            move(qkvc_s.at[j, :, cols], out.at[here, cols], sem.at[at_out + 4 * g + j])
            for j, out in enumerate((q_out, k_out, v_out, ctx_out))
        ]

    at_late = at_out + 4 * groups
    mask_to = [move(mask_s.at[i], out.at[here], sem.at[at_late + i]) for i, out in enumerate((mq_out, mk_out))]
    xt_to, ctxt_to = move(xt_s, xt_out.at[row], sem.at[at_late + 2]), move(ctxt_s, ctxt_out.at[row], sem.at[at_late + 3])
    lse_to, resid_to = move(lse_s, lse_out.at[here], sem.at[at_late + 4]), move(resid_s, resid_out.at[here], sem.at[at_late + 5])
    for copy in x_in + seg_in + [vec_in] + w_in(0) + w_in(1) + w_in(2) + [wo_in]:
        copy.start()
    for copy in seg_in:
        copy.wait()
    seg = jnp.concatenate([seg_s[k][:, :local].astype(F32)[row : row + 1] for k in range(n)], 1)
    spot = lax.broadcasted_iota(jnp.int32, (128, length), 0) % 64
    same = spot.astype(F32) == seg
    mask_s[0] = jnp.where(same, -1e30, 0.0).T.astype(BF)
    mask_s[1] = jnp.where((spot < 7) & jnp.logical_not(same), 1.0, 0.0).T.astype(BF)
    lse_s[...] = jnp.zeros_like(lse_s)
    for copy in mask_to:
        copy.start()
    for copy in x_in:
        copy.wait()

    def transposed(source, target):
        t_s[...] = source.T
        for c in range(2):
            for d in range(8):
                target[c, d] = t_s[pl.ds(split_rows(c, d, me), 48), :]

    transposed(x_s[...], xt_s)
    xt_to.start()
    vec_in.wait()
    low = lane_of((length, 128)) < 64

    def group(g, carry):
        cols = lines(g, 256)
        for copy in w_in(g):
            copy.wait()
        x, mq, mk = x_s[...], mask_s[0], mask_s[1]
        q = ((dot_nn(x, w_s[0, :, cols]) + vec_s[0:1, cols]).astype(BF).astype(F32) * 0.125).astype(BF)
        kk = dot_nn(x, w_s[1, :, cols]).astype(BF)
        v = (dot_nn(x, w_s[2, :, cols]) + vec_s[1:2, cols]).astype(BF)
        for j, value in enumerate((q, kk, v)):
            qkvc_s[j, :, cols] = value

        def scores(head):
            pair = slice(head // 2 * 128, head // 2 * 128 + 128)
            mine = low if head % 2 == 0 else jnp.logical_not(low)
            return dot_nt(jnp.where(mine, q[:, pair], mq), jnp.where(mine, kk[:, pair], mk))

        stats = lse_s[...]
        lanes = lane_of(stats.shape)
        heads = []
        ahead = scores(0)
        for head in range(4):
            s = ahead
            if head < 3:
                ahead = scores(head + 1)
            top = jnp.max(s, -1, keepdims=True)
            e = jnp.exp(s - top)
            total = jnp.sum(e, -1, keepdims=True)
            v2 = v[:, head // 2 * 128 : head // 2 * 128 + 128]
            heads.append(dot_nn(e.astype(BF), v2) * (1.0 / total))
            stats = jnp.where(lanes == g * 4 + head, top + jnp.log(total), stats)
        lse_s[...] = stats
        qkvc_s[3, :, cols] = jnp.concatenate([jnp.where(low, heads[i], heads[i + 1]).astype(BF) for i in (0, 2)], 1)
        for copy in qkvc_to(g):
            copy.start()
        return carry

    lax.fori_loop(0, groups, group, 0)
    lse_to.start()
    wo_in.wait()
    for first in range(0, length, 256):
        at = slice(first, first + 256)
        resid_s[at, :] = x_s[at, :].astype(F32) + dot_nn(qkvc_s[3, at, :], wo_s[...]) + vec_s[2:3, :]
    resid_to.start()
    transposed(qkvc_s[3], ctxt_s)
    ctxt_to.start()
    for g in range(groups):
        for copy in qkvc_to(g):
            copy.wait()
    for copy in mask_to + [xt_to, ctxt_to, lse_to, resid_to]:
        copy.wait()


def attend(me, row, rows, x_blocks, seg_blocks, w, before):
    n, local, width = len(x_blocks), seg_blocks[0].shape[1] - 16, x_blocks[0].shape[2]
    length = n * local
    count = rows * length
    out_shape = [
        jax.ShapeDtypeStruct((count, width), BF),
        jax.ShapeDtypeStruct((count, width), BF),
        jax.ShapeDtypeStruct((count, width), BF),
        jax.ShapeDtypeStruct((count, width), BF),
        jax.ShapeDtypeStruct((count, 128), F32),
        jax.ShapeDtypeStruct((count, width), F32),
        jax.ShapeDtypeStruct((rows, 2, 8, 48, length), BF),
        jax.ShapeDtypeStruct((rows, 2, 8, 48, length), BF),
        jax.ShapeDtypeStruct((count, 128), BF),
        jax.ShapeDtypeStruct((count, 128), BF),
    ]
    aliased = [] if before is None else list(before)
    first = 1 + 2 * n + 5
    any_spec = pl.BlockSpec(memory_space=pl.ANY)
    return pl.pallas_call(
        functools.partial(attend_kernel, n, row, len(aliased), local),
        grid_spec=pltpu.PrefetchScalarGridSpec(
            num_scalar_prefetch=1,
            grid=(1,),
            in_specs=[any_spec] * (2 * n + 5 + len(aliased)),
            out_specs=[any_spec] * len(out_shape),
            scratch_shapes=[
                pltpu.VMEM((length, width), BF),
                pltpu.VMEM((n, 16, width), BF),
                pltpu.VMEM((3, width, width), BF),
                pltpu.VMEM((width, width), BF),
                pltpu.VMEM((16, width), F32),
                pltpu.VMEM((4, length, width), BF),
                pltpu.VMEM((length, 128), F32),
                pltpu.VMEM((length, width), F32),
                pltpu.VMEM((width, length), BF),
                pltpu.VMEM((2, 8, 48, length), BF),
                pltpu.VMEM((2, 8, 48, length), BF),
                pltpu.VMEM((2, length, 128), BF),
                pltpu.SemaphoreType.DMA((2 * n + 2 + 7 * (width // 256) + 6,)),
            ],
        ),
        out_shape=out_shape,
        input_output_aliases={first + i: i for i in range(len(aliased))},
        compiler_params=pltpu.CompilerParams(vmem_limit_bytes=VMEM),
        cost_estimate=LONG,
        name=f"attend_row{row}",
    )(me, *x_blocks, *seg_blocks, w["wq"], w["wk"], w["wv"], w["wo"], w["vec"], *aliased)


CHUNK = 768
TILE = 256


def forward_kernel(
    n, rows, me_ref, vec_in_ref, resid_ref, wi_ref, wo_ref, *refs,
):
    up_refs, refs = refs[:n], refs[n:]
    slope_out, branch_out, grad_out, ht_out, keep_out, send_out, vec_out = refs[:7]
    y_outs, refs = refs[7 : 7 + n], refs[7 + n :]
    h_s, low_s, wi_s, wo_s, act_s, slope_s, up_s, y_s, t_s, ht_s, branch_s, gt_s, keep_s, send_s, vec_ref, sums_s, sem = refs
    core, y, place = place_of(me_ref)
    count, width = h_s.shape
    local = up_s.shape[2]
    tiles, chunks = count // TILE, wi_s.shape[1] // CHUNK
    move = pltpu.make_async_copy
    at_wi, at_wo, at_up = tiles, tiles + chunks, tiles + chunks + 1
    at_out = at_up + n
    resid_in = lambda i: move(resid_ref.at[lines(i, TILE)], h_s.at[lines(i, TILE)], sem.at[i])
    wi_in = lambda c: move(wi_ref.at[:, lines(c, CHUNK)], wi_s.at[:, lines(c, CHUNK)], sem.at[at_wi + c])
    wo_in = move(wo_ref, wo_s, sem.at[at_wo])
    up_in = [move(up_refs[k], up_s.at[k], sem.at[at_up + k]) for k in range(n)]
    slope_to = lambda c: move(slope_s.at[:, lines(c, CHUNK)], slope_out.at[:, lines(c, CHUNK)], sem.at[at_out + c])
    keep_to = lambda z: move(keep_s.at[:, :, z], keep_out.at[:, :, z], sem.at[at_out + chunks + z])
    send_to = lambda z: move(send_s.at[:, :, z], send_out.at[:, :, z], sem.at[at_out + chunks + 4 + z])
    at_late = at_out + chunks + 8
    ht_to = move(ht_s, ht_out, sem.at[at_late])
    vec_in = move(vec_in_ref, vec_ref, sem.at[at_late + 3 + n])
    late = []

    vec_in.start()
    for i in range(tiles):
        resid_in(i).start()
    for c in range(chunks):
        wi_in(c).start()
    wo_in.start()
    for copy in up_in:
        copy.start()
    vec_in.wait()

    def first_norm(i, carry):
        at = lines(i, TILE)
        resid_in(i).wait()
        normed, _ = norm_parts(h_s[at, :])
        hidden = normed * vec_ref[3:4, :] + vec_ref[4:5, :]
        h_s[at, :] = hidden
        low = hidden.astype(BF)
        low_s[at, :] = low
        t_s[:, at] = low.T
        return carry

    lax.fori_loop(0, tiles, first_norm, 0)
    for p in range(8):
        source = pl.multiple_of((place ^ dp_rel(p)) * 96, 32)
        ht_s[p * 96 : (p + 1) * 96, :] = t_s[pl.ds(source, 96), :]
    ht_to.start()

    def hidden_chunk(c, carry):
        cols = lines(c, CHUNK)
        wi_in(c).wait()
        bias = vec_ref[pl.ds(8 + c, 1), :]
        project = lambda i: dot_nn(low_s[i * TILE : (i + 1) * TILE, :], wi_s[:, cols]) + bias
        ahead = project(0)
        for i in range(tiles):
            inner = ahead
            if i + 1 < tiles:
                ahead = project(i + 1)
            phi, rest = normal_laws(inner)
            act_s[i * TILE : (i + 1) * TILE, cols] = (inner * phi).astype(BF)
            slope_s[i * TILE : (i + 1) * TILE, cols] = (phi + rest).astype(BF)
        slope_to(c).start()
        return carry

    lax.fori_loop(0, chunks, hidden_chunk, 0)
    wo_in.wait()
    for copy in up_in:
        copy.wait()
    gain, shift, bias = vec_ref[5:6, :], vec_ref[6:7, :], vec_ref[7:8, :]
    sums = [jnp.zeros((1, width), F32)] * 3
    second = lambda i: dot_nn(act_s[i * TILE : (i + 1) * TILE, :], wo_s[...])
    ahead = second(0)
    per_tile = TILE // local
    for i in range(tiles):
        product = ahead
        if i + 1 < tiles:
            ahead = second(i + 1)
        for j in range(per_tile):
            block = i * per_tile + j
            r, k = block // n, block % n
            at = slice(block * local, (block + 1) * local)
            normed, inverse = norm_parts(h_s[at, :] + product[j * local : (j + 1) * local] + bias)
            up = up_s[k, r].astype(F32)
            y_s[k, r] = (normed * gain + shift).astype(BF)
            grad = norm_back(up * gain, normed, inverse)
            h_s[at, :] = grad
            branch = grad.astype(BF)
            branch_s[at, :] = branch
            t_s[:, at] = branch.T
            for q, piece in enumerate((up * normed, up, branch.astype(F32))):
                sums[q] = sums[q] + jnp.sum(piece, 0, keepdims=True)
    late += [move(h_s, grad_out, sem.at[at_late + 1]), move(branch_s, branch_out, sem.at[at_late + 2])]
    late += [move(y_s.at[k], y_outs[k], sem.at[at_late + 3 + k]) for k in range(n)]
    sums_s[...] = jnp.concatenate(sums + [jnp.zeros((5, width), F32)], 0)
    late.append(move(sums_s, vec_out, sem.at[at_late + 4 + n]))
    for copy in late:
        copy.start()
    for c in range(2):
        for yy in range(2):
            source = pl.multiple_of(((y ^ yy) * 2 + (core ^ c)) * 192, 64)
            gt_s[(c * 2 + yy) * 192 : (c * 2 + yy + 1) * 192, :] = t_s[pl.ds(source, 192), :]

    def outer_grad(z, carry):
        cols = lines((place >> 1) ^ z, 768)
        for c, out in ((1, send_s), (0, keep_s)):
            for yy in range(2):
                first = (c * 2 + yy) * 192
                product = dot_nn(gt_s[first : first + 192, :], act_s[:, cols]).astype(BF)
                for x in range(2):
                    for half in range(2):
                        out[yy, x ^ (place & 1), z, :, half * 384 : half * 384 + 384] = product[
                            half * 96 : half * 96 + 96, x * 384 : (x + 1) * 384
                        ]
        send_to(z).start()
        keep_to(z).start()
        return carry

    lax.fori_loop(0, 4, outer_grad, 0)
    ht_to.wait()
    for copy in late:
        copy.wait()
    for c in range(chunks):
        slope_to(c).wait()
    for z in range(4):
        send_to(z).wait()
        keep_to(z).wait()


def forward(me, rows, resid, up_blocks, w):
    count, width = resid.shape
    n, local = len(up_blocks), up_blocks[0].shape[1]
    ff = w["wi"].shape[1]
    any_spec = pl.BlockSpec(memory_space=pl.ANY)
    blocks = (2, 2, 4, 96, 768)
    out_shape = [
        ((count, ff), BF),
        ((count, width), BF),
        ((count, width), F32),
        ((width, count), BF),
        (blocks, BF),
        (blocks, BF),
        ((8, width), F32),
    ] + [((rows, local, width), BF)] * n
    semaphores = count // TILE + ff // CHUNK + 1 + n + ff // CHUNK + 8 + 5 + n
    return pl.pallas_call(
        functools.partial(forward_kernel, n, rows),
        grid_spec=pltpu.PrefetchScalarGridSpec(
            num_scalar_prefetch=1,
            grid=(1,),
            in_specs=[any_spec] * (4 + n),
            out_specs=[any_spec] * len(out_shape),
            scratch_shapes=[
                pltpu.VMEM((count, width), F32),
                pltpu.VMEM((count, width), BF),
                pltpu.VMEM((width, ff), BF),
                pltpu.VMEM((ff, width), BF),
                pltpu.VMEM((count, ff), BF),
                pltpu.VMEM((count, ff), BF),
                pltpu.VMEM((n, rows, local, width), BF),
                pltpu.VMEM((n, rows, local, width), BF),
                pltpu.VMEM((width, count), BF),
                pltpu.VMEM((width, count), BF),
                pltpu.VMEM((count, width), BF),
                pltpu.VMEM((width, count), BF),
                pltpu.VMEM(blocks, BF),
                pltpu.VMEM(blocks, BF),
                pltpu.VMEM((16, width), F32),
                pltpu.VMEM((8, width), F32),
                pltpu.SemaphoreType.DMA((semaphores,)),
            ],
        ),
        out_shape=[jax.ShapeDtypeStruct(shape, dtype) for shape, dtype in out_shape],
        compiler_params=pltpu.CompilerParams(vmem_limit_bytes=VMEM),
        cost_estimate=LONG,
        name="feed_forward",
    )(me, w["vec"], resid, w["wi"], w["wo2"], *up_blocks)


def backward_kernel(last, ndeps, me_ref, vec_in_ref, branch_ref, slope_ref, wi_ref, wo_ref, ht_ref, *refs):
    if last:
        (resid_ref, grad2_ref, partial_ref), refs = refs[:3], refs[3:]
    refs = refs[ndeps:]
    grad_out, acc_out, bi_out = refs[:3]
    refs = refs[3:]
    if last:
        (attn_out, sums_out, resid_s, grad2_s, attn_s, sums_s), refs = refs[:6], refs[6:]
    branch_s, slope_s, wi_s, wo_s, ht_s, gi_s, acc_s, grad_s, vec_ref, bi_s, sem = refs
    core, y, _ = place_of(me_ref)
    count, width = branch_s.shape
    tiles = count // TILE
    move = pltpu.make_async_copy
    chunk = lambda c: lines((y ^ c) * 2 + (core ^ (0 if last else 1)), CHUNK)
    branch_in, ht_in = move(branch_ref, branch_s, sem.at[0]), move(ht_ref, ht_s, sem.at[1])
    wo_in = lambda c: move(wo_ref.at[chunk(c)], wo_s.at[lines(c, CHUNK)], sem.at[2 + c])
    slope_in = lambda c: move(slope_ref.at[:, chunk(c)], slope_s.at[:, lines(c, CHUNK)], sem.at[4 + c])
    wi_in = lambda c: move(wi_ref.at[:, chunk(c)], wi_s.at[:, lines(c, CHUNK)], sem.at[6 + c])
    grad_to = lambda c: move(grad_s.at[c], grad_out.at[c], sem.at[8 + c])
    acc_to = lambda i: move(acc_s.at[lines(i, TILE)], acc_out.at[lines(i, TILE)], sem.at[10 + i])
    attn_to = lambda i: move(attn_s.at[lines(i, TILE)], attn_out.at[lines(i, TILE)], sem.at[10 + tiles + i])
    late_in = [move(vec_in_ref, vec_ref, sem.at[13 + 2 * tiles])]
    late_to = [move(bi_s, bi_out, sem.at[14 + 2 * tiles])]
    if last:
        late_to.append(move(sums_s, sums_out, sem.at[15 + 2 * tiles]))
        late_in += [move(partial_ref, acc_s, sem.at[10 + 2 * tiles])]
        late_in += [move(grad2_ref, grad2_s, sem.at[11 + 2 * tiles]), move(resid_ref, resid_s, sem.at[12 + 2 * tiles])]

    branch_in.start()
    wo_in(0).start()
    slope_in(0).start()
    ht_in.start()
    wo_in(1).start()
    slope_in(1).start()
    wi_in(0).start()
    wi_in(1).start()
    for copy in late_in:
        copy.start()
    branch_in.wait()

    def hidden_chunk(c, carry):
        cols = lines(c, CHUNK)
        wo_in(c).wait()
        slope_in(c).wait()
        back = lambda i: dot_nt(branch_s[i * TILE : (i + 1) * TILE, :], wo_s[cols, :])
        bias = jnp.zeros((1, CHUNK), F32)
        ahead = back(0)
        for i in range(tiles):
            at = slice(i * TILE, (i + 1) * TILE)
            gi = (ahead * slope_s[at, cols].astype(F32)).astype(BF)
            if i + 1 < tiles:
                ahead = back(i + 1)
            gi_s[at, cols] = gi
            bias = bias + jnp.sum(gi.astype(F32), 0, keepdims=True)
        bi_s[:, cols] = jnp.broadcast_to(bias, (8, CHUNK))

        @pl.when(c == 0)
        def _():
            ht_in.wait()

        for first in range(0, width, 192):
            product = dot_nn(ht_s[first : first + 192, :], gi_s[:, cols]).astype(BF)
            for p in range(2):
                grad_s[c, first // 96 + p] = product[p * 96 : p * 96 + 96, :]
        grad_to(c).start()
        return carry

    lax.fori_loop(0, 2, hidden_chunk, 0)
    wi_in(0).wait()
    wi_in(1).wait()
    for copy in late_in:
        copy.wait()
    gain = vec_ref[3:4, :]
    sums = [jnp.zeros((1, width), F32)] * 3
    back = lambda i: dot_nt(gi_s[i * TILE : (i + 1) * TILE, :], wi_s[...])
    ahead = back(0)
    for i in range(tiles):
        at = slice(i * TILE, (i + 1) * TILE)
        hidden = ahead
        if i + 1 < tiles:
            ahead = back(i + 1)
        if last:
            hidden = hidden + acc_s[at, :] + grad2_s[at, :]
            normed, inverse = norm_parts(resid_s[at, :])
            grad = norm_back(hidden * gain, normed, inverse)
            low = grad.astype(BF)
            acc_s[at, :] = grad
            attn_s[at, :] = low
            for q, piece in enumerate((hidden * normed, hidden, low.astype(F32))):
                sums[q] = sums[q] + jnp.sum(piece, 0, keepdims=True)
            attn_to(i).start()
        else:
            acc_s[at, :] = hidden
        acc_to(i).start()
    if last:
        sums_s[...] = jnp.concatenate(sums + [jnp.zeros((5, width), F32)], 0)
    for copy in late_to:
        copy.start()
    for copy in late_to:
        copy.wait()
    for i in range(tiles):
        acc_to(i).wait()
        if last:
            attn_to(i).wait()
    for c in range(2):
        grad_to(c).wait()


def backward(me, last, branch, slope, ht, w, more, deps):
    count, width = branch.shape
    ff = w["wi"].shape[1]
    any_spec = pl.BlockSpec(memory_space=pl.ANY)
    out_shape = [((2, 8, 96, CHUNK), BF), ((count, width), F32), ((8, ff // 2), F32)]
    scratch = []
    if last:
        out_shape += [((count, width), BF), ((8, width), F32)]
        scratch = [pltpu.VMEM((count, width), F32), pltpu.VMEM((count, width), F32), pltpu.VMEM((count, width), BF)]
        scratch += [pltpu.VMEM((8, width), F32)]
    return pl.pallas_call(
        functools.partial(backward_kernel, last, len(deps)),
        grid_spec=pltpu.PrefetchScalarGridSpec(
            num_scalar_prefetch=1,
            grid=(1,),
            in_specs=[any_spec] * (6 + len(more) + len(deps)),
            out_specs=[any_spec] * len(out_shape),
            scratch_shapes=scratch
            + [
                pltpu.VMEM((count, width), BF),
                pltpu.VMEM((count, 2 * CHUNK), BF),
                pltpu.VMEM((width, 2 * CHUNK), BF),
                pltpu.VMEM((2 * CHUNK, width), BF),
                pltpu.VMEM((width, count), BF),
                pltpu.VMEM((count, 2 * CHUNK), BF),
                pltpu.VMEM((count, width), F32),
                pltpu.VMEM((2, 8, 96, CHUNK), BF),
                pltpu.VMEM((16, width), F32),
                pltpu.VMEM((8, 2 * CHUNK), F32),
                pltpu.SemaphoreType.DMA((16 + 2 * (count // TILE),)),
            ],
        ),
        out_shape=[jax.ShapeDtypeStruct(shape, dtype) for shape, dtype in out_shape],
        compiler_params=pltpu.CompilerParams(vmem_limit_bytes=VMEM),
        cost_estimate=LONG,
        name="feed_forward_back" + ("_last" if last else ""),
    )(me, w["vec"], branch, slope, w["wi"], w["wo2"], ht, *more, *deps)


def attend_back_kernel(part, n, last, ndeps, me_ref, *refs):
    sources, refs = refs[:4], refs[4:]
    lse_ref, attn_ref, mq_ref, mk_ref, xt_ref, acc_ref = refs[:6]
    weights, refs = refs[6:10], refs[10:]
    if part == 0:
        (ctxt_ref, shares_ref), refs = refs[:2], refs[2:]
    refs = refs[ndeps:]
    keep_out, send_out, vec_out = refs[:3]
    tok_outs = refs[3 : 3 + (n if last else 1)]
    refs = refs[3 + len(tok_outs) :]
    heads_s, lse_s, attn_s, mask_s, xt_s, acc_s, wo_s, w_s, g_s, keep_s, send_s, vec_s, tok_s = refs[:13]
    if part == 0:
        ctxt_s, shares_s = refs[13:15]
    sem = refs[-1]
    _, y, place = place_of(me_ref)
    rows, length, width = attn_s.shape
    local = length // n
    move = pltpu.make_async_copy
    cols = [slice((part + 3 * i) * 128, (part + 3 * i) * 128 + 128) for i in range(2)]
    per_row = 14
    at_row = lambda r: lines(r, length)

    def early(r):
        copies = [move(attn_ref.at[at_row(r)], attn_s.at[r], sem.at[r * per_row])]
        for j, source in enumerate(sources):
            for i in range(2):
                copies.append(move(source.at[at_row(r), cols[i]], heads_s.at[r, j, i], sem.at[r * per_row + 1 + 2 * j + i]))
        copies.append(move(lse_ref.at[at_row(r)], lse_s.at[r], sem.at[r * per_row + 9]))
        copies.append(move(mq_ref.at[at_row(r)], mask_s.at[r, 0], sem.at[r * per_row + 10]))
        copies.append(move(mk_ref.at[at_row(r)], mask_s.at[r, 1], sem.at[r * per_row + 11]))
        return copies

    acc_in = lambda r: move(acc_ref.at[at_row(r)], acc_s.at[r], sem.at[r * per_row + 12])
    base = rows * per_row
    wo_in = [move(weights[0].at[cols[i]], wo_s.at[slice(i * 128, i * 128 + 128)], sem.at[base + i]) for i in range(2)]
    w_in = [
        move(weights[1 + j].at[:, cols[i]], w_s.at[j, :, slice(i * 128, i * 128 + 128)], sem.at[base + 2 + 2 * j + i])
        for j in range(3)
        for i in range(2)
    ]
    late_in = [move(xt_ref, xt_s, sem.at[base + 8])]
    if part == 0:
        late_in += [move(ctxt_ref, ctxt_s, sem.at[base + 9]), move(shares_ref, shares_s, sem.at[base + 10])]
    at_tok, at_out = base + 11, base + 11 + rows * n

    def tok_to(r):
        if last:
            return [
                move(tok_s.at[r, lines(k, local)], tok_outs[k].at[r], sem.at[at_tok + r * n + k]) for k in range(n)
            ]
        return [move(acc_s.at[r], tok_outs[0].at[at_row(r)], sem.at[at_tok + r * n])]

    for copy in wo_in + early(0) + w_in + [acc_in(0)]:
        copy.start()
    for r in range(1, rows):
        for copy in early(r) + [acc_in(r)]:
            copy.start()
    for copy in late_in:
        copy.start()
    for copy in wo_in:
        copy.wait()

    lanes = lane_of((length, 128))
    low = lanes < 64
    spot = lanes % 64
    ones = jnp.where((spot >= 4) & (spot < 7), 1.0, 0.0).astype(BF)

    def split3(column):
        high = column.astype(BF)
        rest = column - high.astype(F32)
        middle = rest.astype(BF)
        return high, middle, (rest - middle.astype(F32)).astype(BF)

    def with_columns(base, column):
        for i, piece in enumerate(split3(-column)):
            base = jnp.where(spot == 4 + i, piece, base)
        return base

    block = 256

    def one_row(row, carry):
        for copy in early(row):
            copy.wait()
        mq, mk = mask_s[row, 0], mask_s[row, 1]
        lse_all = lse_s[row]
        grad_ctx = dot_nt(attn_s[row], wo_s[...]).astype(BF)
        items = [(pair, half, first) for pair in range(2) for half in range(2) for first in range(0, length, block)]
        pairs, halves_of = [], {}
        for pair in range(2):
            q2, k2, v2, ctx2 = (heads_s[row, j, pair] for j in range(4))
            do2 = grad_ctx[:, pair * 128 : pair * 128 + 128]
            pairs.append((q2, k2, v2, do2, do2.astype(F32) * ctx2.astype(F32)))

        def operands(pair, half):
            if (pair, half) not in halves_of:
                q2, k2, v2, do2, both = pairs[pair]
                mine = low if half == 0 else jnp.logical_not(low)
                head = (part + 3 * pair) * 2 + half
                delta = jnp.sum(jnp.where(mine, both, 0.0), -1, keepdims=True)
                halves_of[pair, half] = (
                    jnp.where(mine, q2, with_columns(mq, lse_all[:, head : head + 1])),
                    jnp.where(mine, do2, with_columns(jnp.zeros_like(mq), delta)),
                    jnp.where(mine, k2, mk),
                    jnp.where(mine, v2, ones),
                )
            return halves_of[pair, half]

        def products(pair, half, first):
            q_ext, do_ext, k_ext, v_ext = operands(pair, half)
            at = slice(first, first + block)
            return dot_nt(k_ext[at], q_ext), dot_nt(v_ext[at], do_ext)

        dq, dk, dv = {}, {}, {}
        ahead = products(*items[0])
        for i, (pair, half, first) in enumerate(items):
            power, slope = ahead
            if i + 1 < len(items):
                ahead = products(*items[i + 1])
            q2, k2, _, do2, _ = pairs[pair]
            prob = jnp.exp(power)
            ds = (prob * slope).astype(BF)
            key = (pair, half)
            dv.setdefault(key, []).append(dot_nn(prob.astype(BF), do2))
            dk.setdefault(key, []).append(dot_nn(ds, q2))
            add = dot_tn(ds, k2[first : first + block])
            dq[key] = dq[key] + add if key in dq else add
        for pair in range(2):
            at = slice(pair * 128, pair * 128 + 128)
            g_s[row, 0, :, at] = (jnp.where(low, dq[pair, 0], dq[pair, 1]) * 0.125).astype(BF)
            for j, pieces in ((1, dk), (2, dv)):
                whole = [jnp.concatenate(pieces[pair, half], 0) for half in range(2)]
                g_s[row, j, :, at] = jnp.where(low, whole[0], whole[1]).astype(BF)

        @pl.when(row == 0)
        def _():
            for copy in w_in:
                copy.wait()

        acc_in(row).wait()
        token = acc_s[row]
        for j in range(3):
            token = token + dot_nt(g_s[row, j], w_s[j])
        if last:
            tok_s[row] = token.astype(BF)
        else:
            acc_s[row] = token
        for copy in tok_to(row):
            copy.start()
        return carry

    lax.fori_loop(0, rows, one_row, 0)
    for copy in late_in:
        copy.wait()
    count = 6 if part == 0 else 3
    sums = [sum(jnp.sum(g_s[r, j].astype(F32), 0, keepdims=True) for r in range(rows)) for j in (0, 2)]
    vec_s[...] = jnp.concatenate(sums + [jnp.zeros((6, 256), F32)], 0)
    bias = vec_s[...]
    bias = jnp.concatenate([bias[:, :128], bias[:, 128:]], 0).astype(BF)
    for out in (keep_s, send_s):
        for yy in range(2):
            for p in range(8):
                out[yy, p, count * 48 : count * 48 + 16, :] = bias
                if part == 0:
                    out[yy, p, count * 48 + 16 : count * 48 + 32, :] = shares_s[place ^ dp_rel(p)]

    def place_blocks(product, yy, j, first):
        for c, out in ((0, keep_s), (1, send_s)):
            for p in range(8):
                out[yy ^ y, p, j * 48 : (j + 1) * 48, :] = product[(c * 8 + p) * 48 : (c * 8 + p + 1) * 48, first : first + 128]

    for j in range(3):
        product = sum(dot_nn(xt_s[r].reshape(width, length), g_s[r, j]) for r in range(rows)).astype(BF)
        for yy in range(2):
            place_blocks(product, yy, j, yy * 128)
    if part == 0:
        for yy in range(2):
            at = slice(yy * 384, yy * 384 + 384)
            product = sum(dot_nn(ctxt_s[r].reshape(width, length), attn_s[r, :, at]) for r in range(rows)).astype(BF)
            for j in range(3):
                place_blocks(product, yy, 3 + j, j * 128)
    out_copies = [move(send_s, send_out, sem.at[at_out]), move(keep_s, keep_out, sem.at[at_out + 1])]
    out_copies.append(move(vec_s, vec_out, sem.at[at_out + 2]))
    for copy in out_copies:
        copy.start()
    for r in range(rows):
        for copy in tok_to(r):
            copy.wait()
    for copy in out_copies:
        copy.wait()


def attend_back(me, part, n, rows, saved, attn, acc, w, extra, deps):
    q, k, v, ctx, lse, xt, ctxt, mq, mk = saved
    count, width = attn.shape
    length = count // rows
    local = length // n
    last = part == 2
    shape = (2, 8, (6 if part == 0 else 3) * 48 + (32 if part == 0 else 16), 128)
    if last:
        tok_shape = [jax.ShapeDtypeStruct((rows, local, width), BF)] * n
    else:
        tok_shape = [jax.ShapeDtypeStruct((count, width), F32)]
    more = (ctxt, extra) if part == 0 else ()
    any_spec = pl.BlockSpec(memory_space=pl.ANY)
    inputs = (q, k, v, ctx, lse, attn, mq, mk, xt, acc, w["wo"], w["wq"], w["wk"], w["wv"], *more, *deps)
    scratch = [
        pltpu.VMEM((rows, 4, 2, length, 128), BF),
        pltpu.VMEM((rows, length, 128), F32),
        pltpu.VMEM((rows, length, width), BF),
        pltpu.VMEM((rows, 2, length, 128), BF),
        pltpu.VMEM(xt.shape, BF),
        pltpu.VMEM((rows, length, width), F32),
        pltpu.VMEM((256, width), BF),
        pltpu.VMEM((3, width, 256), BF),
        pltpu.VMEM((rows, 3, length, 256), BF),
        pltpu.VMEM(shape, BF),
        pltpu.VMEM(shape, BF),
        pltpu.VMEM((8, 256), F32),
        pltpu.VMEM((rows, length, width), BF),
    ]
    if part == 0:
        scratch += [pltpu.VMEM(ctxt.shape, BF), pltpu.VMEM((8, 16, 128), BF)]
    out_shape = [jax.ShapeDtypeStruct(shape, BF)] * 2 + [jax.ShapeDtypeStruct((8, 256), F32)] + tok_shape
    return pl.pallas_call(
        functools.partial(attend_back_kernel, part, n, last, len(deps)),
        grid_spec=pltpu.PrefetchScalarGridSpec(
            num_scalar_prefetch=1,
            grid=(1,),
            in_specs=[any_spec] * len(inputs),
            out_specs=[any_spec] * len(out_shape),
            scratch_shapes=scratch + [pltpu.SemaphoreType.DMA((14 * rows + 11 + rows * n + 3,))],
        ),
        out_shape=out_shape,
        compiler_params=pltpu.CompilerParams(vmem_limit_bytes=VMEM),
        cost_estimate=LONG,
        name=f"attend_back{part}",
    )(me, *inputs)


def swap(array, axis, mask):
    size = lax.axis_size(axis)
    return lax.ppermute(array, axis, [(i, i ^ mask) for i in range(size)])


def pack_tokens(place, tokens, segments, row):
    n = lax.axis_size("seq")
    own, local, width = tokens.shape[0] // n, tokens.shape[1], tokens.shape[2]

    def kernel(me_ref, seg_ref, *refs):
        for k in range(n):
            source, out = refs[k], refs[n + k]
            out[0, :local, :] = source[0]
            out[0, local:, :] = jnp.zeros((16, width), BF)
            at = (me_ref[0] ^ k) * own
            ids = jnp.concatenate([seg_ref[pl.ds(at + r, 1), :] for r in range(own)] + [seg_ref[:1, :]] * (16 - own), 0)
            out[0, local:, :local] = ids.astype(F32).astype(BF)

    return pl.pallas_call(
        kernel,
        grid_spec=pltpu.PrefetchScalarGridSpec(
            num_scalar_prefetch=1,
            grid=(1,),
            in_specs=[pl.BlockSpec(segments.shape, lambda i, m: (0, 0))]
            + [pl.BlockSpec((1, local, width), lambda i, m, k=k: ((m[0] ^ k) * own + row, 0, 0)) for k in range(n)],
            out_specs=[pl.BlockSpec((1, local + 16, width), lambda i, m: (0, 0, 0))] * n,
        ),
        out_shape=[jax.ShapeDtypeStruct((1, local + 16, width), BF)] * n,
        compiler_params=pltpu.CompilerParams(vmem_limit_bytes=VMEM),
        cost_estimate=TINY,
        name="pack_first",
    )(place, segments, *[tokens] * n)


def pack_rest(place, tokens, cotangent, first_row, deps):
    n = lax.axis_size("seq")
    own, local, width = tokens.shape[0] // n, tokens.shape[1], tokens.shape[2]
    rows = range(first_row, own)
    count = len(rows) * n + n

    def kernel(me_ref, *refs):
        for source, out in zip(refs[:count], refs[count + len(deps) :]):
            out[...] = source[...]

    one = [
        pl.BlockSpec((1, local, width), lambda i, m, k=k, r=r: ((m[0] ^ k) * own + r, 0, 0))
        for r in rows
        for k in range(n)
    ]
    many = [pl.BlockSpec((own, local, width), lambda i, m, k=k: (m[0] ^ k, 0, 0)) for k in range(n)]
    return pl.pallas_call(
        kernel,
        grid_spec=pltpu.PrefetchScalarGridSpec(
            num_scalar_prefetch=1,
            grid=(1,),
            in_specs=one + many + [pl.BlockSpec(memory_space=pl.ANY)] * len(deps),
            out_specs=[pl.BlockSpec((1, local, width), lambda i, m: (0, 0, 0))] * len(one)
            + [pl.BlockSpec((own, local, width), lambda i, m: (0, 0, 0))] * n,
        ),
        out_shape=[jax.ShapeDtypeStruct((1, local, width), BF)] * len(one)
        + [jax.ShapeDtypeStruct((own, local, width), BF)] * n,
        compiler_params=pltpu.CompilerParams(vmem_limit_bytes=VMEM),
        cost_estimate=TINY,
        name="pack_rest",
    )(place, *[tokens] * len(one), *[cotangent] * n, *deps)


def unpack(place, blocks, deps=()):
    n = len(blocks)
    own, local, width = blocks[0].shape

    any_spec = pl.BlockSpec(memory_space=pl.ANY)

    def kernel(me_ref, *refs):
        sources, (out, held, sem) = refs[:n], refs[n + len(deps) :]
        ins = [pltpu.make_async_copy(sources[k], held.at[k], sem.at[k]) for k in range(n)]
        outs = [
            pltpu.make_async_copy(held.at[k], out.at[pl.ds((me_ref[0] ^ k) * own, own)], sem.at[n + k]) for k in range(n)
        ]
        for copy in ins:
            copy.start()
        for k in range(n):
            ins[k].wait()
            outs[k].start()
        for copy in outs:
            copy.wait()

    return pl.pallas_call(
        kernel,
        grid_spec=pltpu.PrefetchScalarGridSpec(
            num_scalar_prefetch=1,
            grid=(1,),
            in_specs=[any_spec] * (n + len(deps)),
            out_specs=any_spec,
            scratch_shapes=[pltpu.VMEM((n, own, local, width), blocks[0].dtype), pltpu.SemaphoreType.DMA((2 * n,))],
        ),
        out_shape=jax.ShapeDtypeStruct((own * n, local, width), blocks[0].dtype),
        compiler_params=pltpu.CompilerParams(vmem_limit_bytes=VMEM),
        cost_estimate=TINY,
        name="unpack_rows",
    )(place, *blocks, *deps)


def exchange(blocks):
    return [swap(block, "seq", k) if k else block for k, block in enumerate(blocks)]


def bits_of(size):
    return [1 << b for b in range(size.bit_length() - 1)]


def reduce_matrix(grad):
    sn, dn = lax.axis_size("seq"), lax.axis_size("dp")
    ms, md = lax.axis_index("seq"), lax.axis_index("dp")
    high, wide = grad.shape[0] // dn, grad.shape[1] // sn
    blocks = grad.astype(BF).reshape(dn, high, sn, wide).transpose(2, 0, 1, 3)
    blocks = jnp.take(blocks, ms ^ jnp.arange(sn), axis=0)
    blocks = jnp.take(blocks, md ^ jnp.arange(dn), axis=1)
    left = {"seq": sn, "dp": dn}
    for axis, mask in [("seq", m) for m in bits_of(sn)] + [("dp", m) for m in bits_of(dn)]:
        size = left[axis]
        dim = 0 if axis == "seq" else 1
        split = blocks.reshape(blocks.shape[:dim] + (size // 2, 2) + blocks.shape[dim + 1 :])
        keep = lax.index_in_dim(split, 0, dim + 1, keepdims=False)
        send = lax.index_in_dim(split, 1, dim + 1, keepdims=False)
        blocks = keep + swap(send, axis, mask)
        left[axis] = size // 2
    return blocks.reshape(high, wide).astype(F32)


def reduce_vectors(vectors):
    for axis in ("seq", "dp"):
        for mask in bits_of(lax.axis_size(axis)):
            vectors = vectors + swap(vectors, axis, mask)
    return vectors


def my_share(vector):
    own = vector.shape[0] // lax.axis_size("dp")
    return lax.dynamic_slice_in_dim(vector, lax.axis_index("dp") * own, own, 0)


X, Y = ("dp", 1), ("seq", 2)


def stage(name, work, arrays, shapes, deps=(), place=None, room=24 * MIB):
    scalars = [] if place is None else [place]

    def kernel(*refs):
        lead, refs = refs[: len(scalars)], refs[len(scalars) :]
        work(*lead, *refs[: len(arrays)], *refs[len(arrays) + len(deps) :])

    full = lambda shape: pl.BlockSpec(shape, lambda i, *m: (0,) * len(shape))
    return pl.pallas_call(
        kernel,
        grid_spec=pltpu.PrefetchScalarGridSpec(
            num_scalar_prefetch=len(scalars),
            grid=(1,),
            in_specs=[full(a.shape) for a in arrays] + [pl.BlockSpec(memory_space=pl.ANY)] * len(deps),
            out_specs=[full(shape) for shape, _ in shapes],
        ),
        out_shape=[jax.ShapeDtypeStruct(shape, dtype) for shape, dtype in shapes],
        compiler_params=pltpu.CompilerParams(vmem_limit_bytes=room),
        cost_estimate=LONG,
        name=name,
    )(*scalars, *arrays, *deps)


def halves(kept, came, keep_out, send_out, lead, rows=None):
    tail = () if rows is None else (Ellipsis, rows, slice(None))
    for i, out in ((0, keep_out), (1, send_out)):
        at = (slice(None),) * lead + (i,) + tail
        out[...] = kept[at] + came[at]


def body(
    tokens,
    cotangent,
    segments,
    w_query,
    b_query,
    w_key,
    w_value,
    b_value,
    w_out,
    b_out,
    gain_one,
    shift_one,
    w_inner,
    b_inner,
    w_outer,
    b_outer,
    gain_two,
    shift_two,
):
    width = tokens.shape[-1]
    n, dn = lax.axis_size("seq"), lax.axis_size("dp")
    ms, md = lax.axis_index("seq"), lax.axis_index("dp")
    fast = n == 4 and dn == 8
    me = (jnp.stack([ms % 2, ms // 2, md]) if fast else jnp.zeros((3,))).astype(jnp.int32)
    seq_place = ms.astype(jnp.int32).reshape(1)
    rows, local = tokens.shape[0] // n, tokens.shape[1]
    length = n * local
    vectors = (b_query, b_value, b_out, gain_one, shift_one, gain_two, shift_two, b_outer, b_inner)
    packed = jnp.concatenate(vectors + (jnp.zeros((4 * width,), BF),)).reshape(16, width).astype(F32)
    w = dict(wq=w_query, wk=w_key, wv=w_value, wo=w_out, wi=w_inner, wo2=w_outer, vec=packed)

    first_blocks = pack_tokens(seq_place, tokens, segments, 0)
    x_blocks = [exchange(first_blocks)]
    seg_blocks = x_blocks[0]
    rest = pack_rest(seq_place, tokens, cotangent, 1, first_blocks[:1])
    for r in range(1, rows):
        x_blocks.append(exchange(rest[(r - 1) * n : r * n]))
    up_blocks = exchange(rest[(rows - 1) * n :])

    before = None
    for r in range(rows):
        before = attend(me, r, rows, x_blocks[r], seg_blocks, w, before)
    q, k, v, ctx, lse, resid, xt, ctxt, mq, mk = before
    slope, branch, grad2, ht, outer_keep, outer_send, vec2, *y_blocks = forward(me, rows, resid, up_blocks, w)
    outer = (outer_keep, outer_send)
    y_blocks = exchange(y_blocks)
    inner_send, partial, bi_send = backward(me, False, branch, slope, ht, w, [], [])
    saved = (q, k, v, ctx, lse, xt, ctxt, mq, mk)

    if not fast:
        inner_keep, grad1, bi_keep, attn, vec1 = backward(me, True, branch, slope, ht, w, [resid, grad2, partial], [])
        shares = jnp.zeros((8, 16, 128), BF)
        early = jnp.concatenate([vec2[:3], vec1[:3]], 0)
        vec_bi = jnp.stack([bi_keep[0].reshape(2, -1), bi_send[0].reshape(2, -1)], 1).reshape(1, -1)
        parts, vec_parts = [], []
        acc = grad1
        for part in range(3):
            keep, send, vec, *tail = attend_back(me, part, n, rows, saved, attn, acc, w, shares, [])
            parts.append((keep, send))
            vec_parts.append(vec)
            acc = tail[0]
        output = unpack(seq_place, y_blocks)
        grad_tokens = unpack(seq_place, exchange(tail))
        early = reduce_vectors(jnp.concatenate([early, vec_bi[:1].reshape(4, width)], 0))
        late = jnp.stack([p[:2] for p in vec_parts], 1).reshape(2, 3, 2, 128)
        late = reduce_vectors(late.transpose(0, 2, 1, 3).reshape(2, width))
        stack = lambda pair: jnp.stack(list(pair))
        outer_t = stack(outer).reshape(2, 2, 2, 4, 96, 2, 384).transpose(1, 0, 5, 4, 3, 2, 6).reshape(width, -1)
        inner_b = stack((inner_keep, inner_send)).reshape(2, 2, 2, 4, 96, -1).transpose(3, 2, 4, 1, 0, 5)
        inner_b = inner_b.reshape(width, -1)
        three = [stack(pair)[:, :, :, -160:-16] if i else stack(pair)[:, :, :, :144] for i, pair in enumerate(parts)]
        qkv = jnp.stack(three).reshape(3, 2, 2, 2, 4, 3, 48, 128).transpose(5, 4, 3, 1, 6, 2, 0, 7).reshape(3, width, width)
        out_b = stack(parts[0])[:, :, :, 144:288].reshape(2, 2, 2, 4, 3, 48, 128).transpose(3, 2, 0, 5, 1, 4, 6)
        grad_w_outer = reduce_matrix(outer_t.T)
        grad_w_inner = reduce_matrix(inner_b)
        grad_w_out = reduce_matrix(out_b.reshape(width, width))
        grad_w_query, grad_w_key, grad_w_value = (reduce_matrix(qkv[i]) for i in range(3))
        b_query_g, b_value_g = my_share(late[0]), my_share(late[1])
        gain2_g, shift2_g, b_outer_g, gain1_g, shift1_g, b_out_g = (my_share(early[i]) for i in range(6))
        b_inner_g = my_share(early[6:10].reshape(-1))
    else:
        by_axes = lambda a: a.reshape((2, 2, 4) + a.shape[2:])
        one = lambda *shape: (shape, BF)
        top, low = slice(0, 48), slice(48, 96)
        z_swap = lambda pieces: [pieces[0]] + [swap(pieces[j], "dp", 2 * j) for j in (1, 2, 3)]
        first_shapes, second_shapes, z_shapes = [one(2, 4, 48, 768)] * 4, [one(4, 48, 768)] * 4, [one(192, 768)] * 4

        def z_split(first, top_keep, top_came, low_keep, low_came, outs):
            for j, out in enumerate(outs):
                out[first : first + 48, :] = top_keep[j] + top_came[j]
                out[first + 48 : first + 96, :] = low_keep[j] + low_came[j]

        outer_came = swap(outer[1], "seq", 1)

        def stage_a(kept, came, a_keep, a_send, b_keep, b_send):
            halves(kept, came, a_keep, a_send, 1, top)
            halves(kept, came, b_keep, b_send, 0, low)

        a_keep, a_send, b_keep, b_send = stage(
            "stage_a", stage_a, [outer[0], outer_came], first_shapes, [inner_send], room=VMEM
        )

        a_came, b_came = swap(a_send, *X), swap(b_send, *Y)
        inner_came = swap(inner_send, "seq", 1)
        inner_keep, grad1, bi_keep, attn, vec1 = backward(
            me, True, branch, slope, ht, w, [resid, grad2, partial], [a_keep, *y_blocks]
        )

        def stage_b(
            me_ref, a_keep, a_came, b_keep, b_came, i_keep, i_came, vec2, vec1, bi_keep, bi_send,
            a2_keep, a2_send, b2_keep, b2_send, c_keep, c_send, d_keep, d_send, shares,
        ):
            halves(a_keep, a_came, a2_keep, a2_send, 0)
            halves(b_keep, b_came, b2_keep, b2_send, 0)
            halves(i_keep, i_came, c_keep, c_send, 1, top)
            halves(i_keep, i_came, d_keep, d_send, 0, low)
            vector_shares(me_ref, vec2, vec1, bi_keep, bi_send, shares)

        def vector_shares(me_ref, vec2, vec1, bi_keep, bi_send, shares):
            early = jnp.concatenate([vec2[0:3], vec1[0:3]], 0)
            kept, sent = bi_keep[0:1], bi_send[0:1]
            blank = jnp.zeros((6, 32), F32)
            for d in range(8):
                core, y = me_ref[0], me_ref[1]
                at = slice((d % 2) * 384, (d % 2) * 384 + 384)
                other = slice(768 + at.start, 768 + at.stop)
                own_core = core == (d // 2) % 2
                own_y = y == d // 4
                piece = jnp.where(
                    own_core,
                    jnp.where(own_y, kept[:, at], kept[:, other]),
                    jnp.where(own_y, sent[:, at], sent[:, other]),
                )
                rows = [jnp.concatenate([early[:, d * 96 : d * 96 + 96], blank], 1)]
                rows += [piece[:, j * 128 : j * 128 + 128] for j in range(3)] + [jnp.zeros((7, 128), F32)]
                shares[d] = jnp.concatenate(rows, 0).astype(BF)

        *stage_b_outs, shares = stage(
            "stage_b",
            stage_b,
            [a_keep, a_came, b_keep, b_came, by_axes(inner_keep), by_axes(inner_came), vec2, vec1, bi_keep, bi_send],
            second_shapes + first_shapes + [one(8, 16, 128)],
            place=me,
            room=VMEM,
        )
        a_keep, a_send, b_keep, b_send, c_keep, c_send, d_keep, d_send = stage_b_outs

        a_came, b_came = swap(a_send, *Y), swap(b_send, *X)
        c_came, d_came = swap(c_send, *X), swap(d_send, *Y)
        keep0, send0, vec_0, acc = attend_back(me, 0, n, rows, saved, attn, grad1, w, shares, [a_keep])

        def stage_c(c_keep, c_came, d_keep, d_came, *outs):
            halves(c_keep, c_came, outs[0], outs[1], 0)
            halves(d_keep, d_came, outs[2], outs[3], 0)

        c_keep, c_send, d_keep, d_send = stage(
            "stage_c",
            stage_c,
            [c_keep, c_came, d_keep, d_came],
            second_shapes,
            [keep0, a_came, b_came],
            room=VMEM,
        )

        c_came, d_came = swap(c_send, *Y), swap(d_send, *X)
        came0 = swap(send0, "seq", 1)
        keep1, send1, vec_1, acc = attend_back(me, 1, n, rows, saved, attn, acc, w, None, [c_keep])

        def stage_d(a_keep, a_came, b_keep, b_came, c_keep, c_came, d_keep, d_came, keep0, came0, *outs):
            z_split(0, a_keep, a_came, b_keep, b_came, outs[:4])
            z_split(96, c_keep, c_came, d_keep, d_came, outs[:4])
            halves(keep0, came0, outs[4], outs[5], 0)

        *forward_z, p0_keep, p0_send = stage(
            "stage_d",
            stage_d,
            [a_keep, a_came, b_keep, b_came, c_keep, c_came, d_keep, d_came, by_axes(keep0), by_axes(came0)],
            z_shapes + [one(2, 4, 320, 128)] * 2,
            [keep1],
            room=VMEM,
        )

        p0_came = swap(p0_send, *Y)
        came1 = swap(send1, "seq", 1)
        forward_z = z_swap(forward_z)
        keep2, send2, vec_2, *tok_blocks = attend_back(me, 2, n, rows, saved, attn, acc, w, None, [p0_keep])

        came2 = swap(send2, "seq", 1)
        tok_blocks = exchange(tok_blocks)
        add = lambda four: sum(r[...].astype(F32) for r in four)
        x_split = lambda kept, came, a, b: halves(kept, came, a, b, 1)
        y_split = lambda kept, came, a, b: halves(kept, came, a, b, 0)
        quarter, eighth = [one(2, 4, 160, 128)] * 2, [one(4, 160, 128)] * 2

        def stage_e(p0_keep, p0_came, keep1, came1, *outs):
            halves(p0_keep, p0_came, outs[0], outs[1], 0)
            halves(keep1, came1, outs[2], outs[3], 0)

        p0_keep, p0_send, p1_keep, p1_send = stage(
            "stage_e",
            stage_e,
            [p0_keep, p0_came, by_axes(keep1), by_axes(came1)],
            [one(4, 320, 128)] * 2 + quarter,
            [keep2, *forward_z[1:]],
        )
        p1_came, p0_came = swap(p1_send, *Y), swap(p0_send, *X)
        p2_keep, p2_send = stage(
            "stage_f", x_split, [by_axes(keep2), by_axes(came2)], quarter, [p1_keep]
        )
        p2_came = swap(p2_send, *X)

        def forward_grads(*refs):
            total = add(refs[0:4])
            refs[4][0:96, :] = total[:96, :384]
            refs[4][96:192, :] = total[:96, 384:]
            refs[5][...] = total[96:]

        grad_w_outer, grad_w_inner = stage(
            "forward_grads", forward_grads, forward_z, [((192, 384), F32), ((96, 768), F32)], [p2_keep]
        )
        grad_w_outer = grad_w_outer.T
        output = unpack(seq_place, y_blocks, [grad_w_inner])

        p1_keep, p1_send = stage("stage_g", y_split, [p1_keep, p1_came], eighth, [output])
        p1_came = swap(p1_send, *X)
        p2_keep, p2_send = stage(
            "stage_h", y_split, [p2_keep, p2_came], eighth, [p1_keep, tok_blocks[2]]
        )
        p2_came = swap(p2_send, *Y)

        def stage_i(p0_keep, p0_came, p1_keep, p1_came, p2_keep, p2_came, *outs):
            for j in range(4):
                outs[j][0:320, :] = p0_keep[j] + p0_came[j]
                outs[j][320:480, :] = p1_keep[j] + p1_came[j]
                outs[j][480:640, :] = p2_keep[j] + p2_came[j]

        z_pieces = z_swap(
            stage(
                "stage_i", stage_i, [p0_keep, p0_came, p1_keep, p1_came, p2_keep, p2_came], [one(640, 128)] * 4
            )
        )
        grad_tokens = unpack(seq_place, tok_blocks)

        def gather_up(me_ref, *refs):
            total = add(refs[0:4])
            z0, z12 = total[0:320], total[320:640]
            mine, other, bq_out, bv_out, bi_out, *vec_outs = refs[4:]
            place = me_ref[2]
            for i, out in enumerate(vec_outs):
                out[...] = z0[304 + i : 305 + i, 0:96]
            bi_out[...] = jnp.concatenate([z0[310 + j : 311 + j] for j in range(3)], 1)
            first_rows = [z0[288:304], z12[144:160], z12[304:320]]
            for i, out in enumerate((bq_out, bv_out)):
                whole = [first_rows[j % 3][(j // 3) * 8 + i : (j // 3) * 8 + i + 1] for j in range(6)]
                whole = jnp.concatenate(whole, 1)
                total = jnp.zeros((1, 96), F32)
                for d in range(8):
                    total = jnp.where(place == d, whole[:, d * 96 : d * 96 + 96], total)
                out[...] = total
            rows = lambda z, first: [z[first + 48 * j : first + 48 * j + 48] for j in range(3)]
            out_w = rows(z0, 144)
            parts = [rows(z0, 0), rows(z12, 0), rows(z12, 160)]
            for i in range(4):
                pieces = out_w if i == 0 else [part[i - 1] for part in parts]
                whole = jnp.concatenate(pieces, 1)
                left, right = whole[:, :192], whole[:, 192:]
                first = me_ref[0] == 0
                mine[i] = jnp.where(first, left, right)
                other[i] = jnp.where(first, right, left).astype(BF)

        mine, other, b_query_g, b_value_g, b_inner_g, *vecs = stage(
            "gather_up",
            gather_up,
            z_pieces,
            [((4, 48, 192), F32), ((4, 48, 192), BF), ((1, 96), F32), ((1, 96), F32), ((1, 384), F32)]
            + [((1, 96), F32)] * 6,
            [grad_tokens],
            place=me,
        )
        other = swap(other, "seq", 1)

        def assemble(me_ref, mine, other, *outs):
            for i, out in enumerate(outs):
                kept, came = mine[i], other[i].astype(F32)
                first = me_ref[0] == 0
                out[0:48, :] = jnp.where(first, kept, came)
                out[48:96, :] = jnp.where(first, came, kept)

        grad_w_out, grad_w_query, grad_w_key, grad_w_value = stage(
            "assemble", assemble, [mine, other], [((96, 192), F32)] * 4, place=me
        )
        b_query_g, b_value_g, b_inner_g = (v.reshape(-1) for v in (b_query_g, b_value_g, b_inner_g))
        gain2_g, shift2_g, b_outer_g, gain1_g, shift1_g, b_out_g = (v.reshape(-1) for v in vecs)

    return (
        output,
        grad_tokens,
        grad_w_query,
        b_query_g,
        grad_w_key,
        grad_w_value,
        b_value_g,
        grad_w_out,
        b_out_g,
        gain1_g,
        shift1_g,
        grad_w_inner,
        b_inner_g,
        grad_w_outer,
        b_outer_g,
        gain2_g,
        shift2_g,
    )


def solution(mesh):
    token = P("dp", "seq", None)
    matrix = P("dp", "seq")
    vector = P("dp")
    return jax.shard_map(
        body,
        mesh=mesh,
        in_specs=(token, token, P("dp", "seq")) + (P(),) * 15,
        out_specs=(
            token,
            token,
            matrix,
            vector,
            matrix,
            matrix,
            vector,
            matrix,
            vector,
            vector,
            vector,
            matrix,
            vector,
            matrix,
            vector,
            vector,
            vector,
        ),
        check_vma=False,
    )
```

```python
import functools

import jax
import jax.numpy as jnp
from jax import lax
from jax.experimental import pallas as pl
from jax.experimental.pallas import tpu as pltpu
from jax.sharding import PartitionSpec as P

HEADS = 12
BF = jnp.bfloat16
F32 = jnp.float32
MIB = 1 << 20
VMEM = 60 * MIB
LONG = pl.CostEstimate(flops=60_000_000_000, bytes_accessed=1, transcendentals=0)
TINY = pl.CostEstimate(flops=1, bytes_accessed=1, transcendentals=0)


def dot_nn(a, b):
    return lax.dot_general(a, b, (((1,), (0,)), ((), ())), preferred_element_type=F32)


def dot_nt(a, b):
    return lax.dot_general(a, b, (((1,), (1,)), ((), ())), preferred_element_type=F32)


def dot_tn(a, b):
    return lax.dot_general(a, b, (((0,), (0,)), ((), ())), preferred_element_type=F32)


def normal_laws(a):
    gauss = jnp.exp(a * a * -0.5)
    return 0.5 + 0.5 * lax.erf(a * 0.7071067811865476), a * (gauss * 0.3989422804014327)


def norm_parts(values):
    mean = jnp.mean(values, -1, keepdims=True)
    centred = values - mean
    inverse = lax.rsqrt(jnp.mean(centred * centred, -1, keepdims=True) + 1e-05)
    return centred * inverse, inverse


def norm_back(scaled, normed, inverse):
    return inverse * (
        scaled
        - jnp.mean(scaled, -1, keepdims=True)
        - normed * jnp.mean(scaled * normed, -1, keepdims=True)
    )


def lines(index, size):
    return pl.ds(pl.multiple_of(index * size, size), size)


def lane_of(shape):
    return lax.broadcasted_iota(jnp.int32, shape, 1)


def place_of(me_ref):
    return me_ref[0], me_ref[1], me_ref[2]


def dp_rel(position):
    return (position % 4) * 2 + position // 4


def split_rows(position_c, position_d, me):
    core, _, place = me
    return pl.multiple_of((place ^ dp_rel(position_d)) * 96 + (core ^ position_c) * 48, 16)


def attend_kernel(n, row, aliased, local, me_ref, *refs):
    x_refs, seg_refs, refs = refs[:n], refs[n : 2 * n], refs[2 * n :]
    w_refs, (wo_ref, vec_ref), refs = refs[:3], refs[3:5], refs[5 + aliased :]
    outs, refs = refs[:10], refs[10:]
    x_s, seg_s, w_s, wo_s, vec_s, qkvc_s, lse_s, resid_s, t_s, xt_s, ctxt_s, mask_s, sem = refs
    q_out, k_out, v_out, ctx_out, lse_out, resid_out, xt_out, ctxt_out, mq_out, mk_out = outs
    length, width = x_s.shape
    groups = width // 256
    me = place_of(me_ref)
    move = pltpu.make_async_copy
    here = slice(row * length, (row + 1) * length)
    x_in = [move(x_refs[k].at[0, slice(0, local)], x_s.at[slice(k * local, (k + 1) * local)], sem.at[k]) for k in range(n)]
    seg_in = [move(seg_refs[k].at[0, slice(local, local + 16)], seg_s.at[k], sem.at[n + k]) for k in range(n)]
    wo_in, vec_in = move(wo_ref, wo_s, sem.at[2 * n]), move(vec_ref, vec_s, sem.at[2 * n + 1])
    at_w = 2 * n + 2

    def w_in(g):
        cols = lines(g, 256)
        return [move(w_refs[j].at[:, cols], w_s.at[j, :, cols], sem.at[at_w + 3 * g + j]) for j in range(3)]

    at_out = at_w + 3 * groups

    def qkvc_to(g):
        cols = lines(g, 256)
        return [
            move(qkvc_s.at[j, :, cols], out.at[here, cols], sem.at[at_out + 4 * g + j])
            for j, out in enumerate((q_out, k_out, v_out, ctx_out))
        ]

    at_late = at_out + 4 * groups
    mask_to = [move(mask_s.at[i], out.at[here], sem.at[at_late + i]) for i, out in enumerate((mq_out, mk_out))]
    xt_to, ctxt_to = move(xt_s, xt_out.at[row], sem.at[at_late + 2]), move(ctxt_s, ctxt_out.at[row], sem.at[at_late + 3])
    lse_to, resid_to = move(lse_s, lse_out.at[here], sem.at[at_late + 4]), move(resid_s, resid_out.at[here], sem.at[at_late + 5])
    for copy in x_in + seg_in + [vec_in] + w_in(0) + w_in(1) + w_in(2) + [wo_in]:
        copy.start()
    for copy in seg_in:
        copy.wait()
    seg = jnp.concatenate([seg_s[k][:, :local].astype(F32)[row : row + 1] for k in range(n)], 1)
    spot = lax.broadcasted_iota(jnp.int32, (128, length), 0) % 64
    same = spot.astype(F32) == seg
    mask_s[0] = jnp.where(same, -1e30, 0.0).T.astype(BF)
    mask_s[1] = jnp.where((spot < 7) & jnp.logical_not(same), 1.0, 0.0).T.astype(BF)
    lse_s[...] = jnp.zeros_like(lse_s)
    for copy in mask_to:
        copy.start()
    for copy in x_in:
        copy.wait()

    def transposed(source, target):
        t_s[...] = source.T
        for c in range(2):
            for d in range(8):
                target[c, d] = t_s[pl.ds(split_rows(c, d, me), 48), :]

    transposed(x_s[...], xt_s)
    xt_to.start()
    vec_in.wait()
    low = lane_of((length, 128)) < 64

    def group(g, carry):
        cols = lines(g, 256)
        for copy in w_in(g):
            copy.wait()
        x, mq, mk = x_s[...], mask_s[0], mask_s[1]
        q = ((dot_nn(x, w_s[0, :, cols]) + vec_s[0:1, cols]).astype(BF).astype(F32) * 0.125).astype(BF)
        kk = dot_nn(x, w_s[1, :, cols]).astype(BF)
        v = (dot_nn(x, w_s[2, :, cols]) + vec_s[1:2, cols]).astype(BF)
        for j, value in enumerate((q, kk, v)):
            qkvc_s[j, :, cols] = value

        def scores(head):
            pair = slice(head // 2 * 128, head // 2 * 128 + 128)
            mine = low if head % 2 == 0 else jnp.logical_not(low)
            return dot_nt(jnp.where(mine, q[:, pair], mq), jnp.where(mine, kk[:, pair], mk))

        stats = lse_s[...]
        lanes = lane_of(stats.shape)
        heads = []
        ahead = scores(0)
        for head in range(4):
            s = ahead
            if head < 3:
                ahead = scores(head + 1)
            top = jnp.max(s, -1, keepdims=True)
            e = jnp.exp(s - top)
            total = jnp.sum(e, -1, keepdims=True)
            v2 = v[:, head // 2 * 128 : head // 2 * 128 + 128]
            heads.append(dot_nn(e.astype(BF), v2) * (1.0 / total))
            stats = jnp.where(lanes == g * 4 + head, top + jnp.log(total), stats)
        lse_s[...] = stats
        qkvc_s[3, :, cols] = jnp.concatenate([jnp.where(low, heads[i], heads[i + 1]).astype(BF) for i in (0, 2)], 1)
        for copy in qkvc_to(g):
            copy.start()
        return carry

    lax.fori_loop(0, groups, group, 0)
    lse_to.start()
    wo_in.wait()
    for first in range(0, length, 256):
        at = slice(first, first + 256)
        resid_s[at, :] = x_s[at, :].astype(F32) + dot_nn(qkvc_s[3, at, :], wo_s[...]) + vec_s[2:3, :]
    resid_to.start()
    transposed(qkvc_s[3], ctxt_s)
    ctxt_to.start()
    for g in range(groups):
        for copy in qkvc_to(g):
            copy.wait()
    for copy in mask_to + [xt_to, ctxt_to, lse_to, resid_to]:
        copy.wait()


def attend(me, row, rows, x_blocks, seg_blocks, w, before):
    n, local, width = len(x_blocks), seg_blocks[0].shape[1] - 16, x_blocks[0].shape[2]
    length = n * local
    count = rows * length
    out_shape = [
        jax.ShapeDtypeStruct((count, width), BF),
        jax.ShapeDtypeStruct((count, width), BF),
        jax.ShapeDtypeStruct((count, width), BF),
        jax.ShapeDtypeStruct((count, width), BF),
        jax.ShapeDtypeStruct((count, 128), F32),
        jax.ShapeDtypeStruct((count, width), F32),
        jax.ShapeDtypeStruct((rows, 2, 8, 48, length), BF),
        jax.ShapeDtypeStruct((rows, 2, 8, 48, length), BF),
        jax.ShapeDtypeStruct((count, 128), BF),
        jax.ShapeDtypeStruct((count, 128), BF),
    ]
    aliased = [] if before is None else list(before)
    first = 1 + 2 * n + 5
    any_spec = pl.BlockSpec(memory_space=pl.ANY)
    return pl.pallas_call(
        functools.partial(attend_kernel, n, row, len(aliased), local),
        grid_spec=pltpu.PrefetchScalarGridSpec(
            num_scalar_prefetch=1,
            grid=(1,),
            in_specs=[any_spec] * (2 * n + 5 + len(aliased)),
            out_specs=[any_spec] * len(out_shape),
            scratch_shapes=[
                pltpu.VMEM((length, width), BF),
                pltpu.VMEM((n, 16, width), BF),
                pltpu.VMEM((3, width, width), BF),
                pltpu.VMEM((width, width), BF),
                pltpu.VMEM((16, width), F32),
                pltpu.VMEM((4, length, width), BF),
                pltpu.VMEM((length, 128), F32),
                pltpu.VMEM((length, width), F32),
                pltpu.VMEM((width, length), BF),
                pltpu.VMEM((2, 8, 48, length), BF),
                pltpu.VMEM((2, 8, 48, length), BF),
                pltpu.VMEM((2, length, 128), BF),
                pltpu.SemaphoreType.DMA((2 * n + 2 + 7 * (width // 256) + 6,)),
            ],
        ),
        out_shape=out_shape,
        input_output_aliases={first + i: i for i in range(len(aliased))},
        compiler_params=pltpu.CompilerParams(vmem_limit_bytes=VMEM),
        cost_estimate=LONG,
        name=f"attend_row{row}",
    )(me, *x_blocks, *seg_blocks, w["wq"], w["wk"], w["wv"], w["wo"], w["vec"], *aliased)


CHUNK = 768
TILE = 256


def forward_kernel(
    n, rows, me_ref, vec_in_ref, resid_ref, wi_ref, wo_ref, *refs,
):
    up_refs, refs = refs[:n], refs[n:]
    slope_out, branch_out, grad_out, ht_out, keep_out, send_out, vec_out = refs[:7]
    y_outs, refs = refs[7 : 7 + n], refs[7 + n :]
    h_s, low_s, wi_s, wo_s, act_s, slope_s, up_s, y_s, t_s, ht_s, branch_s, gt_s, keep_s, send_s, vec_ref, sums_s, sem = refs
    core, y, place = place_of(me_ref)
    count, width = h_s.shape
    local = up_s.shape[2]
    tiles, chunks = count // TILE, wi_s.shape[1] // CHUNK
    move = pltpu.make_async_copy
    at_wi, at_wo, at_up = tiles, tiles + chunks, tiles + chunks + 1
    at_out = at_up + n
    resid_in = lambda i: move(resid_ref.at[lines(i, TILE)], h_s.at[lines(i, TILE)], sem.at[i])
    wi_in = lambda c: move(wi_ref.at[:, lines(c, CHUNK)], wi_s.at[:, lines(c, CHUNK)], sem.at[at_wi + c])
    wo_in = move(wo_ref, wo_s, sem.at[at_wo])
    up_in = [move(up_refs[k], up_s.at[k], sem.at[at_up + k]) for k in range(n)]
    slope_to = lambda c: move(slope_s.at[:, lines(c, CHUNK)], slope_out.at[:, lines(c, CHUNK)], sem.at[at_out + c])
    keep_to = lambda z: move(keep_s.at[:, :, z], keep_out.at[:, :, z], sem.at[at_out + chunks + z])
    send_to = lambda z: move(send_s.at[:, :, z], send_out.at[:, :, z], sem.at[at_out + chunks + 4 + z])
    at_late = at_out + chunks + 8
    ht_to = move(ht_s, ht_out, sem.at[at_late])
    vec_in = move(vec_in_ref, vec_ref, sem.at[at_late + 3 + n])
    late = []

    vec_in.start()
    for i in range(tiles):
        resid_in(i).start()
    for c in range(chunks):
        wi_in(c).start()
    wo_in.start()
    for copy in up_in:
        copy.start()
    vec_in.wait()

    def first_norm(i, carry):
        at = lines(i, TILE)
        resid_in(i).wait()
        normed, _ = norm_parts(h_s[at, :])
        hidden = normed * vec_ref[3:4, :] + vec_ref[4:5, :]
        h_s[at, :] = hidden
        low = hidden.astype(BF)
        low_s[at, :] = low
        t_s[:, at] = low.T
        return carry

    lax.fori_loop(0, tiles, first_norm, 0)
    for p in range(8):
        source = pl.multiple_of((place ^ dp_rel(p)) * 96, 32)
        ht_s[p * 96 : (p + 1) * 96, :] = t_s[pl.ds(source, 96), :]
    ht_to.start()

    def hidden_chunk(c, carry):
        cols = lines(c, CHUNK)
        wi_in(c).wait()
        bias = vec_ref[pl.ds(8 + c, 1), :]
        project = lambda i: dot_nn(low_s[i * TILE : (i + 1) * TILE, :], wi_s[:, cols]) + bias
        ahead = project(0)
        for i in range(tiles):
            inner = ahead
            if i + 1 < tiles:
                ahead = project(i + 1)
            phi, rest = normal_laws(inner)
            act_s[i * TILE : (i + 1) * TILE, cols] = (inner * phi).astype(BF)
            slope_s[i * TILE : (i + 1) * TILE, cols] = (phi + rest).astype(BF)
        slope_to(c).start()
        return carry

    lax.fori_loop(0, chunks, hidden_chunk, 0)
    wo_in.wait()
    for copy in up_in:
        copy.wait()
    gain, shift, bias = vec_ref[5:6, :], vec_ref[6:7, :], vec_ref[7:8, :]
    sums = [jnp.zeros((1, width), F32)] * 3
    second = lambda i: dot_nn(act_s[i * TILE : (i + 1) * TILE, :], wo_s[...])
    ahead = second(0)
    per_tile = TILE // local
    for i in range(tiles):
        product = ahead
        if i + 1 < tiles:
            ahead = second(i + 1)
        for j in range(per_tile):
            block = i * per_tile + j
            r, k = block // n, block % n
            at = slice(block * local, (block + 1) * local)
            normed, inverse = norm_parts(h_s[at, :] + product[j * local : (j + 1) * local] + bias)
            up = up_s[k, r].astype(F32)
            y_s[k, r] = (normed * gain + shift).astype(BF)
            grad = norm_back(up * gain, normed, inverse)
            h_s[at, :] = grad
            branch = grad.astype(BF)
            branch_s[at, :] = branch
            t_s[:, at] = branch.T
            for q, piece in enumerate((up * normed, up, branch.astype(F32))):
                sums[q] = sums[q] + jnp.sum(piece, 0, keepdims=True)
    late += [move(h_s, grad_out, sem.at[at_late + 1]), move(branch_s, branch_out, sem.at[at_late + 2])]
    late += [move(y_s.at[k], y_outs[k], sem.at[at_late + 3 + k]) for k in range(n)]
    sums_s[...] = jnp.concatenate(sums + [jnp.zeros((5, width), F32)], 0)
    late.append(move(sums_s, vec_out, sem.at[at_late + 4 + n]))
    for copy in late:
        copy.start()
    for c in range(2):
        for yy in range(2):
            source = pl.multiple_of(((y ^ yy) * 2 + (core ^ c)) * 192, 64)
            gt_s[(c * 2 + yy) * 192 : (c * 2 + yy + 1) * 192, :] = t_s[pl.ds(source, 192), :]

    def outer_grad(z, carry):
        cols = lines((place >> 1) ^ z, 768)
        for c, out in ((1, send_s), (0, keep_s)):
            for yy in range(2):
                first = (c * 2 + yy) * 192
                product = dot_nn(gt_s[first : first + 192, :], act_s[:, cols]).astype(BF)
                for x in range(2):
                    for half in range(2):
                        out[yy, x ^ (place & 1), z, :, half * 384 : half * 384 + 384] = product[
                            half * 96 : half * 96 + 96, x * 384 : (x + 1) * 384
                        ]
        send_to(z).start()
        keep_to(z).start()
        return carry

    lax.fori_loop(0, 4, outer_grad, 0)
    ht_to.wait()
    for copy in late:
        copy.wait()
    for c in range(chunks):
        slope_to(c).wait()
    for z in range(4):
        send_to(z).wait()
        keep_to(z).wait()


def forward(me, rows, resid, up_blocks, w):
    count, width = resid.shape
    n, local = len(up_blocks), up_blocks[0].shape[1]
    ff = w["wi"].shape[1]
    any_spec = pl.BlockSpec(memory_space=pl.ANY)
    blocks = (2, 2, 4, 96, 768)
    out_shape = [
        ((count, ff), BF),
        ((count, width), BF),
        ((count, width), F32),
        ((width, count), BF),
        (blocks, BF),
        (blocks, BF),
        ((8, width), F32),
    ] + [((rows, local, width), BF)] * n
    semaphores = count // TILE + ff // CHUNK + 1 + n + ff // CHUNK + 8 + 5 + n
    return pl.pallas_call(
        functools.partial(forward_kernel, n, rows),
        grid_spec=pltpu.PrefetchScalarGridSpec(
            num_scalar_prefetch=1,
            grid=(1,),
            in_specs=[any_spec] * (4 + n),
            out_specs=[any_spec] * len(out_shape),
            scratch_shapes=[
                pltpu.VMEM((count, width), F32),
                pltpu.VMEM((count, width), BF),
                pltpu.VMEM((width, ff), BF),
                pltpu.VMEM((ff, width), BF),
                pltpu.VMEM((count, ff), BF),
                pltpu.VMEM((count, ff), BF),
                pltpu.VMEM((n, rows, local, width), BF),
                pltpu.VMEM((n, rows, local, width), BF),
                pltpu.VMEM((width, count), BF),
                pltpu.VMEM((width, count), BF),
                pltpu.VMEM((count, width), BF),
                pltpu.VMEM((width, count), BF),
                pltpu.VMEM(blocks, BF),
                pltpu.VMEM(blocks, BF),
                pltpu.VMEM((16, width), F32),
                pltpu.VMEM((8, width), F32),
                pltpu.SemaphoreType.DMA((semaphores,)),
            ],
        ),
        out_shape=[jax.ShapeDtypeStruct(shape, dtype) for shape, dtype in out_shape],
        compiler_params=pltpu.CompilerParams(vmem_limit_bytes=VMEM),
        cost_estimate=LONG,
        name="feed_forward",
    )(me, w["vec"], resid, w["wi"], w["wo2"], *up_blocks)


def backward_kernel(last, ndeps, me_ref, vec_in_ref, branch_ref, slope_ref, wi_ref, wo_ref, ht_ref, *refs):
    if last:
        (resid_ref, grad2_ref, partial_ref), refs = refs[:3], refs[3:]
    refs = refs[ndeps:]
    grad_out, acc_out, bi_out = refs[:3]
    refs = refs[3:]
    if last:
        (attn_out, sums_out, resid_s, grad2_s, attn_s, sums_s), refs = refs[:6], refs[6:]
    branch_s, slope_s, wi_s, wo_s, ht_s, gi_s, acc_s, grad_s, vec_ref, bi_s, sem = refs
    core, y, _ = place_of(me_ref)
    count, width = branch_s.shape
    tiles = count // TILE
    move = pltpu.make_async_copy
    chunk = lambda c: lines((y ^ c) * 2 + (core ^ (0 if last else 1)), CHUNK)
    branch_in, ht_in = move(branch_ref, branch_s, sem.at[0]), move(ht_ref, ht_s, sem.at[1])
    wo_in = lambda c: move(wo_ref.at[chunk(c)], wo_s.at[lines(c, CHUNK)], sem.at[2 + c])
    slope_in = lambda c: move(slope_ref.at[:, chunk(c)], slope_s.at[:, lines(c, CHUNK)], sem.at[4 + c])
    wi_in = lambda c: move(wi_ref.at[:, chunk(c)], wi_s.at[:, lines(c, CHUNK)], sem.at[6 + c])
    grad_to = lambda c: move(grad_s.at[c], grad_out.at[c], sem.at[8 + c])
    acc_to = lambda i: move(acc_s.at[lines(i, TILE)], acc_out.at[lines(i, TILE)], sem.at[10 + i])
    attn_to = lambda i: move(attn_s.at[lines(i, TILE)], attn_out.at[lines(i, TILE)], sem.at[10 + tiles + i])
    late_in = [move(vec_in_ref, vec_ref, sem.at[13 + 2 * tiles])]
    late_to = [move(bi_s, bi_out, sem.at[14 + 2 * tiles])]
    if last:
        late_to.append(move(sums_s, sums_out, sem.at[15 + 2 * tiles]))
        late_in += [move(partial_ref, acc_s, sem.at[10 + 2 * tiles])]
        late_in += [move(grad2_ref, grad2_s, sem.at[11 + 2 * tiles]), move(resid_ref, resid_s, sem.at[12 + 2 * tiles])]

    branch_in.start()
    wo_in(0).start()
    slope_in(0).start()
    ht_in.start()
    wo_in(1).start()
    slope_in(1).start()
    wi_in(0).start()
    wi_in(1).start()
    for copy in late_in:
        copy.start()
    branch_in.wait()

    def hidden_chunk(c, carry):
        cols = lines(c, CHUNK)
        wo_in(c).wait()
        slope_in(c).wait()
        back = lambda i: dot_nt(branch_s[i * TILE : (i + 1) * TILE, :], wo_s[cols, :])
        bias = jnp.zeros((1, CHUNK), F32)
        ahead = back(0)
        for i in range(tiles):
            at = slice(i * TILE, (i + 1) * TILE)
            gi = (ahead * slope_s[at, cols].astype(F32)).astype(BF)
            if i + 1 < tiles:
                ahead = back(i + 1)
            gi_s[at, cols] = gi
            bias = bias + jnp.sum(gi.astype(F32), 0, keepdims=True)
        bi_s[:, cols] = jnp.broadcast_to(bias, (8, CHUNK))

        @pl.when(c == 0)
        def _():
            ht_in.wait()

        for first in range(0, width, 192):
            product = dot_nn(ht_s[first : first + 192, :], gi_s[:, cols]).astype(BF)
            for p in range(2):
                grad_s[c, first // 96 + p] = product[p * 96 : p * 96 + 96, :]
        grad_to(c).start()
        return carry

    lax.fori_loop(0, 2, hidden_chunk, 0)
    wi_in(0).wait()
    wi_in(1).wait()
    for copy in late_in:
        copy.wait()
    gain = vec_ref[3:4, :]
    sums = [jnp.zeros((1, width), F32)] * 3
    back = lambda i: dot_nt(gi_s[i * TILE : (i + 1) * TILE, :], wi_s[...])
    ahead = back(0)
    for i in range(tiles):
        at = slice(i * TILE, (i + 1) * TILE)
        hidden = ahead
        if i + 1 < tiles:
            ahead = back(i + 1)
        if last:
            hidden = hidden + acc_s[at, :] + grad2_s[at, :]
            normed, inverse = norm_parts(resid_s[at, :])
            grad = norm_back(hidden * gain, normed, inverse)
            low = grad.astype(BF)
            acc_s[at, :] = grad
            attn_s[at, :] = low
            for q, piece in enumerate((hidden * normed, hidden, low.astype(F32))):
                sums[q] = sums[q] + jnp.sum(piece, 0, keepdims=True)
            attn_to(i).start()
        else:
            acc_s[at, :] = hidden
        acc_to(i).start()
    if last:
        sums_s[...] = jnp.concatenate(sums + [jnp.zeros((5, width), F32)], 0)
    for copy in late_to:
        copy.start()
    for copy in late_to:
        copy.wait()
    for i in range(tiles):
        acc_to(i).wait()
        if last:
            attn_to(i).wait()
    for c in range(2):
        grad_to(c).wait()


def backward(me, last, branch, slope, ht, w, more, deps):
    count, width = branch.shape
    ff = w["wi"].shape[1]
    any_spec = pl.BlockSpec(memory_space=pl.ANY)
    out_shape = [((2, 8, 96, CHUNK), BF), ((count, width), F32), ((8, ff // 2), F32)]
    scratch = []
    if last:
        out_shape += [((count, width), BF), ((8, width), F32)]
        scratch = [pltpu.VMEM((count, width), F32), pltpu.VMEM((count, width), F32), pltpu.VMEM((count, width), BF)]
        scratch += [pltpu.VMEM((8, width), F32)]
    return pl.pallas_call(
        functools.partial(backward_kernel, last, len(deps)),
        grid_spec=pltpu.PrefetchScalarGridSpec(
            num_scalar_prefetch=1,
            grid=(1,),
            in_specs=[any_spec] * (6 + len(more) + len(deps)),
            out_specs=[any_spec] * len(out_shape),
            scratch_shapes=scratch
            + [
                pltpu.VMEM((count, width), BF),
                pltpu.VMEM((count, 2 * CHUNK), BF),
                pltpu.VMEM((width, 2 * CHUNK), BF),
                pltpu.VMEM((2 * CHUNK, width), BF),
                pltpu.VMEM((width, count), BF),
                pltpu.VMEM((count, 2 * CHUNK), BF),
                pltpu.VMEM((count, width), F32),
                pltpu.VMEM((2, 8, 96, CHUNK), BF),
                pltpu.VMEM((16, width), F32),
                pltpu.VMEM((8, 2 * CHUNK), F32),
                pltpu.SemaphoreType.DMA((16 + 2 * (count // TILE),)),
            ],
        ),
        out_shape=[jax.ShapeDtypeStruct(shape, dtype) for shape, dtype in out_shape],
        compiler_params=pltpu.CompilerParams(vmem_limit_bytes=VMEM),
        cost_estimate=LONG,
        name="feed_forward_back" + ("_last" if last else ""),
    )(me, w["vec"], branch, slope, w["wi"], w["wo2"], ht, *more, *deps)


def attend_back_kernel(part, n, last, ndeps, me_ref, *refs):
    sources, refs = refs[:4], refs[4:]
    lse_ref, attn_ref, mq_ref, mk_ref, xt_ref, acc_ref = refs[:6]
    weights, refs = refs[6:10], refs[10:]
    if part == 0:
        (ctxt_ref, shares_ref), refs = refs[:2], refs[2:]
    refs = refs[ndeps:]
    keep_out, send_out, vec_out = refs[:3]
    tok_outs = refs[3 : 3 + (n if last else 1)]
    refs = refs[3 + len(tok_outs) :]
    heads_s, lse_s, attn_s, mask_s, xt_s, acc_s, wo_s, w_s, g_s, keep_s, send_s, vec_s, tok_s = refs[:13]
    if part == 0:
        ctxt_s, shares_s = refs[13:15]
    sem = refs[-1]
    _, y, place = place_of(me_ref)
    rows, length, width = attn_s.shape
    local = length // n
    move = pltpu.make_async_copy
    cols = [slice((part + 3 * i) * 128, (part + 3 * i) * 128 + 128) for i in range(2)]
    per_row = 14
    at_row = lambda r: lines(r, length)

    def early(r):
        copies = [move(attn_ref.at[at_row(r)], attn_s.at[r], sem.at[r * per_row])]
        for j, source in enumerate(sources):
            for i in range(2):
                copies.append(move(source.at[at_row(r), cols[i]], heads_s.at[r, j, i], sem.at[r * per_row + 1 + 2 * j + i]))
        copies.append(move(lse_ref.at[at_row(r)], lse_s.at[r], sem.at[r * per_row + 9]))
        copies.append(move(mq_ref.at[at_row(r)], mask_s.at[r, 0], sem.at[r * per_row + 10]))
        copies.append(move(mk_ref.at[at_row(r)], mask_s.at[r, 1], sem.at[r * per_row + 11]))
        return copies

    acc_in = lambda r: move(acc_ref.at[at_row(r)], acc_s.at[r], sem.at[r * per_row + 12])
    base = rows * per_row
    wo_in = [move(weights[0].at[cols[i]], wo_s.at[slice(i * 128, i * 128 + 128)], sem.at[base + i]) for i in range(2)]
    w_in = [
        move(weights[1 + j].at[:, cols[i]], w_s.at[j, :, slice(i * 128, i * 128 + 128)], sem.at[base + 2 + 2 * j + i])
        for j in range(3)
        for i in range(2)
    ]
    late_in = [move(xt_ref, xt_s, sem.at[base + 8])]
    if part == 0:
        late_in += [move(ctxt_ref, ctxt_s, sem.at[base + 9]), move(shares_ref, shares_s, sem.at[base + 10])]
    at_tok, at_out = base + 11, base + 11 + rows * n

    def tok_to(r):
        if last:
            return [
                move(tok_s.at[r, lines(k, local)], tok_outs[k].at[r], sem.at[at_tok + r * n + k]) for k in range(n)
            ]
        return [move(acc_s.at[r], tok_outs[0].at[at_row(r)], sem.at[at_tok + r * n])]

    for copy in wo_in + early(0) + w_in + [acc_in(0)]:
        copy.start()
    for r in range(1, rows):
        for copy in early(r) + [acc_in(r)]:
            copy.start()
    for copy in late_in:
        copy.start()
    for copy in wo_in:
        copy.wait()

    lanes = lane_of((length, 128))
    low = lanes < 64
    spot = lanes % 64
    ones = jnp.where((spot >= 4) & (spot < 7), 1.0, 0.0).astype(BF)

    def split3(column):
        high = column.astype(BF)
        rest = column - high.astype(F32)
        middle = rest.astype(BF)
        return high, middle, (rest - middle.astype(F32)).astype(BF)

    def with_columns(base, column):
        for i, piece in enumerate(split3(-column)):
            base = jnp.where(spot == 4 + i, piece, base)
        return base

    block = 256

    def one_row(row, carry):
        for copy in early(row):
            copy.wait()
        mq, mk = mask_s[row, 0], mask_s[row, 1]
        lse_all = lse_s[row]
        grad_ctx = dot_nt(attn_s[row], wo_s[...]).astype(BF)
        items = [(pair, half, first) for pair in range(2) for half in range(2) for first in range(0, length, block)]
        pairs, halves_of = [], {}
        for pair in range(2):
            q2, k2, v2, ctx2 = (heads_s[row, j, pair] for j in range(4))
            do2 = grad_ctx[:, pair * 128 : pair * 128 + 128]
            pairs.append((q2, k2, v2, do2, do2.astype(F32) * ctx2.astype(F32)))

        def operands(pair, half):
            if (pair, half) not in halves_of:
                q2, k2, v2, do2, both = pairs[pair]
                mine = low if half == 0 else jnp.logical_not(low)
                head = (part + 3 * pair) * 2 + half
                delta = jnp.sum(jnp.where(mine, both, 0.0), -1, keepdims=True)
                halves_of[pair, half] = (
                    jnp.where(mine, q2, with_columns(mq, lse_all[:, head : head + 1])),
                    jnp.where(mine, do2, with_columns(jnp.zeros_like(mq), delta)),
                    jnp.where(mine, k2, mk),
                    jnp.where(mine, v2, ones),
                )
            return halves_of[pair, half]

        def products(pair, half, first):
            q_ext, do_ext, k_ext, v_ext = operands(pair, half)
            at = slice(first, first + block)
            return dot_nt(k_ext[at], q_ext), dot_nt(v_ext[at], do_ext)

        dq, dk, dv = {}, {}, {}
        ahead = products(*items[0])
        for i, (pair, half, first) in enumerate(items):
            power, slope = ahead
            if i + 1 < len(items):
                ahead = products(*items[i + 1])
            q2, k2, _, do2, _ = pairs[pair]
            prob = jnp.exp(power)
            ds = (prob * slope).astype(BF)
            key = (pair, half)
            dv.setdefault(key, []).append(dot_nn(prob.astype(BF), do2))
            dk.setdefault(key, []).append(dot_nn(ds, q2))
            add = dot_tn(ds, k2[first : first + block])
            dq[key] = dq[key] + add if key in dq else add
        for pair in range(2):
            at = slice(pair * 128, pair * 128 + 128)
            g_s[row, 0, :, at] = (jnp.where(low, dq[pair, 0], dq[pair, 1]) * 0.125).astype(BF)
            for j, pieces in ((1, dk), (2, dv)):
                whole = [jnp.concatenate(pieces[pair, half], 0) for half in range(2)]
                g_s[row, j, :, at] = jnp.where(low, whole[0], whole[1]).astype(BF)

        @pl.when(row == 0)
        def _():
            for copy in w_in:
                copy.wait()

        acc_in(row).wait()
        token = acc_s[row]
        for j in range(3):
            token = token + dot_nt(g_s[row, j], w_s[j])
        if last:
            tok_s[row] = token.astype(BF)
        else:
            acc_s[row] = token
        for copy in tok_to(row):
            copy.start()
        return carry

    lax.fori_loop(0, rows, one_row, 0)
    for copy in late_in:
        copy.wait()
    count = 6 if part == 0 else 3
    sums = [sum(jnp.sum(g_s[r, j].astype(F32), 0, keepdims=True) for r in range(rows)) for j in (0, 2)]
    vec_s[...] = jnp.concatenate(sums + [jnp.zeros((6, 256), F32)], 0)
    bias = vec_s[...]
    bias = jnp.concatenate([bias[:, :128], bias[:, 128:]], 0).astype(BF)
    for out in (keep_s, send_s):
        for yy in range(2):
            for p in range(8):
                out[yy, p, count * 48 : count * 48 + 16, :] = bias
                if part == 0:
                    out[yy, p, count * 48 + 16 : count * 48 + 32, :] = shares_s[place ^ dp_rel(p)]

    def place_blocks(product, yy, j, first):
        for c, out in ((0, keep_s), (1, send_s)):
            for p in range(8):
                out[yy ^ y, p, j * 48 : (j + 1) * 48, :] = product[(c * 8 + p) * 48 : (c * 8 + p + 1) * 48, first : first + 128]

    for j in range(3):
        product = sum(dot_nn(xt_s[r].reshape(width, length), g_s[r, j]) for r in range(rows)).astype(BF)
        for yy in range(2):
            place_blocks(product, yy, j, yy * 128)
    if part == 0:
        for yy in range(2):
            at = slice(yy * 384, yy * 384 + 384)
            product = sum(dot_nn(ctxt_s[r].reshape(width, length), attn_s[r, :, at]) for r in range(rows)).astype(BF)
            for j in range(3):
                place_blocks(product, yy, 3 + j, j * 128)
    out_copies = [move(send_s, send_out, sem.at[at_out]), move(keep_s, keep_out, sem.at[at_out + 1])]
    out_copies.append(move(vec_s, vec_out, sem.at[at_out + 2]))
    for copy in out_copies:
        copy.start()
    for r in range(rows):
        for copy in tok_to(r):
            copy.wait()
    for copy in out_copies:
        copy.wait()


def attend_back(me, part, n, rows, saved, attn, acc, w, extra, deps):
    q, k, v, ctx, lse, xt, ctxt, mq, mk = saved
    count, width = attn.shape
    length = count // rows
    local = length // n
    last = part == 2
    shape = (2, 8, (6 if part == 0 else 3) * 48 + (32 if part == 0 else 16), 128)
    if last:
        tok_shape = [jax.ShapeDtypeStruct((rows, local, width), BF)] * n
    else:
        tok_shape = [jax.ShapeDtypeStruct((count, width), F32)]
    more = (ctxt, extra) if part == 0 else ()
    any_spec = pl.BlockSpec(memory_space=pl.ANY)
    inputs = (q, k, v, ctx, lse, attn, mq, mk, xt, acc, w["wo"], w["wq"], w["wk"], w["wv"], *more, *deps)
    scratch = [
        pltpu.VMEM((rows, 4, 2, length, 128), BF),
        pltpu.VMEM((rows, length, 128), F32),
        pltpu.VMEM((rows, length, width), BF),
        pltpu.VMEM((rows, 2, length, 128), BF),
        pltpu.VMEM(xt.shape, BF),
        pltpu.VMEM((rows, length, width), F32),
        pltpu.VMEM((256, width), BF),
        pltpu.VMEM((3, width, 256), BF),
        pltpu.VMEM((rows, 3, length, 256), BF),
        pltpu.VMEM(shape, BF),
        pltpu.VMEM(shape, BF),
        pltpu.VMEM((8, 256), F32),
        pltpu.VMEM((rows, length, width), BF),
    ]
    if part == 0:
        scratch += [pltpu.VMEM(ctxt.shape, BF), pltpu.VMEM((8, 16, 128), BF)]
    out_shape = [jax.ShapeDtypeStruct(shape, BF)] * 2 + [jax.ShapeDtypeStruct((8, 256), F32)] + tok_shape
    return pl.pallas_call(
        functools.partial(attend_back_kernel, part, n, last, len(deps)),
        grid_spec=pltpu.PrefetchScalarGridSpec(
            num_scalar_prefetch=1,
            grid=(1,),
            in_specs=[any_spec] * len(inputs),
            out_specs=[any_spec] * len(out_shape),
            scratch_shapes=scratch + [pltpu.SemaphoreType.DMA((14 * rows + 11 + rows * n + 3,))],
        ),
        out_shape=out_shape,
        compiler_params=pltpu.CompilerParams(vmem_limit_bytes=VMEM),
        cost_estimate=LONG,
        name=f"attend_back{part}",
    )(me, *inputs)


def swap(array, axis, mask):
    size = lax.axis_size(axis)
    return lax.ppermute(array, axis, [(i, i ^ mask) for i in range(size)])


def pack_tokens(place, tokens, segments, row):
    n = lax.axis_size("seq")
    own, local, width = tokens.shape[0] // n, tokens.shape[1], tokens.shape[2]

    def kernel(me_ref, seg_ref, *refs):
        for k in range(n):
            source, out = refs[k], refs[n + k]
            out[0, :local, :] = source[0]
            out[0, local:, :] = jnp.zeros((16, width), BF)
            at = (me_ref[0] ^ k) * own
            ids = jnp.concatenate([seg_ref[pl.ds(at + r, 1), :] for r in range(own)] + [seg_ref[:1, :]] * (16 - own), 0)
            out[0, local:, :local] = ids.astype(F32).astype(BF)

    return pl.pallas_call(
        kernel,
        grid_spec=pltpu.PrefetchScalarGridSpec(
            num_scalar_prefetch=1,
            grid=(1,),
            in_specs=[pl.BlockSpec(segments.shape, lambda i, m: (0, 0))]
            + [pl.BlockSpec((1, local, width), lambda i, m, k=k: ((m[0] ^ k) * own + row, 0, 0)) for k in range(n)],
            out_specs=[pl.BlockSpec((1, local + 16, width), lambda i, m: (0, 0, 0))] * n,
        ),
        out_shape=[jax.ShapeDtypeStruct((1, local + 16, width), BF)] * n,
        compiler_params=pltpu.CompilerParams(vmem_limit_bytes=VMEM),
        cost_estimate=TINY,
        name="pack_first",
    )(place, segments, *[tokens] * n)


def pack_rest(place, tokens, cotangent, first_row, deps):
    n = lax.axis_size("seq")
    own, local, width = tokens.shape[0] // n, tokens.shape[1], tokens.shape[2]
    rows = range(first_row, own)
    count = len(rows) * n + n

    def kernel(me_ref, *refs):
        for source, out in zip(refs[:count], refs[count + len(deps) :]):
            out[...] = source[...]

    one = [
        pl.BlockSpec((1, local, width), lambda i, m, k=k, r=r: ((m[0] ^ k) * own + r, 0, 0))
        for r in rows
        for k in range(n)
    ]
    many = [pl.BlockSpec((own, local, width), lambda i, m, k=k: (m[0] ^ k, 0, 0)) for k in range(n)]
    return pl.pallas_call(
        kernel,
        grid_spec=pltpu.PrefetchScalarGridSpec(
            num_scalar_prefetch=1,
            grid=(1,),
            in_specs=one + many + [pl.BlockSpec(memory_space=pl.ANY)] * len(deps),
            out_specs=[pl.BlockSpec((1, local, width), lambda i, m: (0, 0, 0))] * len(one)
            + [pl.BlockSpec((own, local, width), lambda i, m: (0, 0, 0))] * n,
        ),
        out_shape=[jax.ShapeDtypeStruct((1, local, width), BF)] * len(one)
        + [jax.ShapeDtypeStruct((own, local, width), BF)] * n,
        compiler_params=pltpu.CompilerParams(vmem_limit_bytes=VMEM),
        cost_estimate=TINY,
        name="pack_rest",
    )(place, *[tokens] * len(one), *[cotangent] * n, *deps)


def unpack(place, blocks, deps=()):
    n = len(blocks)
    own, local, width = blocks[0].shape

    any_spec = pl.BlockSpec(memory_space=pl.ANY)

    def kernel(me_ref, *refs):
        sources, (out, held, sem) = refs[:n], refs[n + len(deps) :]
        ins = [pltpu.make_async_copy(sources[k], held.at[k], sem.at[k]) for k in range(n)]
        outs = [
            pltpu.make_async_copy(held.at[k], out.at[pl.ds((me_ref[0] ^ k) * own, own)], sem.at[n + k]) for k in range(n)
        ]
        for copy in ins:
            copy.start()
        for k in range(n):
            ins[k].wait()
            outs[k].start()
        for copy in outs:
            copy.wait()

    return pl.pallas_call(
        kernel,
        grid_spec=pltpu.PrefetchScalarGridSpec(
            num_scalar_prefetch=1,
            grid=(1,),
            in_specs=[any_spec] * (n + len(deps)),
            out_specs=pl.BlockSpec(memory_space=pltpu.HBM),
            scratch_shapes=[pltpu.VMEM((n, own, local, width), blocks[0].dtype), pltpu.SemaphoreType.DMA((2 * n,))],
        ),
        out_shape=jax.ShapeDtypeStruct((own * n, local, width), blocks[0].dtype),
        compiler_params=pltpu.CompilerParams(vmem_limit_bytes=VMEM),
        cost_estimate=TINY,
        name="unpack_rows",
    )(place, *blocks, *deps)


def exchange(blocks):
    return [swap(block, "seq", k) if k else block for k, block in enumerate(blocks)]


def bits_of(size):
    return [1 << b for b in range(size.bit_length() - 1)]


def reduce_matrix(grad):
    sn, dn = lax.axis_size("seq"), lax.axis_size("dp")
    ms, md = lax.axis_index("seq"), lax.axis_index("dp")
    high, wide = grad.shape[0] // dn, grad.shape[1] // sn
    blocks = grad.astype(BF).reshape(dn, high, sn, wide).transpose(2, 0, 1, 3)
    blocks = jnp.take(blocks, ms ^ jnp.arange(sn), axis=0)
    blocks = jnp.take(blocks, md ^ jnp.arange(dn), axis=1)
    left = {"seq": sn, "dp": dn}
    for axis, mask in [("seq", m) for m in bits_of(sn)] + [("dp", m) for m in bits_of(dn)]:
        size = left[axis]
        dim = 0 if axis == "seq" else 1
        split = blocks.reshape(blocks.shape[:dim] + (size // 2, 2) + blocks.shape[dim + 1 :])
        keep = lax.index_in_dim(split, 0, dim + 1, keepdims=False)
        send = lax.index_in_dim(split, 1, dim + 1, keepdims=False)
        blocks = keep + swap(send, axis, mask)
        left[axis] = size // 2
    return blocks.reshape(high, wide).astype(F32)


def reduce_vectors(vectors):
    for axis in ("seq", "dp"):
        for mask in bits_of(lax.axis_size(axis)):
            vectors = vectors + swap(vectors, axis, mask)
    return vectors


def my_share(vector):
    own = vector.shape[0] // lax.axis_size("dp")
    return lax.dynamic_slice_in_dim(vector, lax.axis_index("dp") * own, own, 0)


X, Y = ("dp", 1), ("seq", 2)


def stage(name, work, arrays, shapes, deps=(), place=None, room=24 * MIB):
    scalars = [] if place is None else [place]

    def kernel(*refs):
        lead, refs = refs[: len(scalars)], refs[len(scalars) :]
        work(*lead, *refs[: len(arrays)], *refs[len(arrays) + len(deps) :])

    full = lambda shape: pl.BlockSpec(shape, lambda i, *m: (0,) * len(shape))
    return pl.pallas_call(
        kernel,
        grid_spec=pltpu.PrefetchScalarGridSpec(
            num_scalar_prefetch=len(scalars),
            grid=(1,),
            in_specs=[full(a.shape) for a in arrays] + [pl.BlockSpec(memory_space=pl.ANY)] * len(deps),
            out_specs=[full(shape) for shape, _ in shapes],
        ),
        out_shape=[jax.ShapeDtypeStruct(shape, dtype) for shape, dtype in shapes],
        compiler_params=pltpu.CompilerParams(vmem_limit_bytes=room),
        cost_estimate=LONG,
        name=name,
    )(*scalars, *arrays, *deps)


def halves(kept, came, keep_out, send_out, lead, rows=None):
    tail = () if rows is None else (Ellipsis, rows, slice(None))
    for i, out in ((0, keep_out), (1, send_out)):
        at = (slice(None),) * lead + (i,) + tail
        out[...] = kept[at] + came[at]


def body(
    tokens,
    cotangent,
    segments,
    w_query,
    b_query,
    w_key,
    w_value,
    b_value,
    w_out,
    b_out,
    gain_one,
    shift_one,
    w_inner,
    b_inner,
    w_outer,
    b_outer,
    gain_two,
    shift_two,
):
    width = tokens.shape[-1]
    n, dn = lax.axis_size("seq"), lax.axis_size("dp")
    ms, md = lax.axis_index("seq"), lax.axis_index("dp")
    fast = n == 4 and dn == 8
    me = (jnp.stack([ms % 2, ms // 2, md]) if fast else jnp.zeros((3,))).astype(jnp.int32)
    seq_place = ms.astype(jnp.int32).reshape(1)
    rows, local = tokens.shape[0] // n, tokens.shape[1]
    length = n * local
    vectors = (b_query, b_value, b_out, gain_one, shift_one, gain_two, shift_two, b_outer, b_inner)
    packed = jnp.concatenate(vectors + (jnp.zeros((4 * width,), BF),)).reshape(16, width).astype(F32)
    w = dict(wq=w_query, wk=w_key, wv=w_value, wo=w_out, wi=w_inner, wo2=w_outer, vec=packed)

    first_blocks = pack_tokens(seq_place, tokens, segments, 0)
    x_blocks = [exchange(first_blocks)]
    seg_blocks = x_blocks[0]
    rest = pack_rest(seq_place, tokens, cotangent, 1, first_blocks[:1])
    for r in range(1, rows):
        x_blocks.append(exchange(rest[(r - 1) * n : r * n]))
    up_blocks = exchange(rest[(rows - 1) * n :])

    before = None
    for r in range(rows):
        before = attend(me, r, rows, x_blocks[r], seg_blocks, w, before)
    q, k, v, ctx, lse, resid, xt, ctxt, mq, mk = before
    slope, branch, grad2, ht, outer_keep, outer_send, vec2, *y_blocks = forward(me, rows, resid, up_blocks, w)
    outer = (outer_keep, outer_send)
    y_blocks = exchange(y_blocks)
    inner_send, partial, bi_send = backward(me, False, branch, slope, ht, w, [], [])
    saved = (q, k, v, ctx, lse, xt, ctxt, mq, mk)

    if not fast:
        inner_keep, grad1, bi_keep, attn, vec1 = backward(me, True, branch, slope, ht, w, [resid, grad2, partial], [])
        shares = jnp.zeros((8, 16, 128), BF)
        early = jnp.concatenate([vec2[:3], vec1[:3]], 0)
        vec_bi = jnp.stack([bi_keep[0].reshape(2, -1), bi_send[0].reshape(2, -1)], 1).reshape(1, -1)
        parts, vec_parts = [], []
        acc = grad1
        for part in range(3):
            keep, send, vec, *tail = attend_back(me, part, n, rows, saved, attn, acc, w, shares, [])
            parts.append((keep, send))
            vec_parts.append(vec)
            acc = tail[0]
        output = unpack(seq_place, y_blocks)
        grad_tokens = unpack(seq_place, exchange(tail))
        early = reduce_vectors(jnp.concatenate([early, vec_bi[:1].reshape(4, width)], 0))
        late = jnp.stack([p[:2] for p in vec_parts], 1).reshape(2, 3, 2, 128)
        late = reduce_vectors(late.transpose(0, 2, 1, 3).reshape(2, width))
        stack = lambda pair: jnp.stack(list(pair))
        outer_t = stack(outer).reshape(2, 2, 2, 4, 96, 2, 384).transpose(1, 0, 5, 4, 3, 2, 6).reshape(width, -1)
        inner_b = stack((inner_keep, inner_send)).reshape(2, 2, 2, 4, 96, -1).transpose(3, 2, 4, 1, 0, 5)
        inner_b = inner_b.reshape(width, -1)
        three = [stack(pair)[:, :, :, -160:-16] if i else stack(pair)[:, :, :, :144] for i, pair in enumerate(parts)]
        qkv = jnp.stack(three).reshape(3, 2, 2, 2, 4, 3, 48, 128).transpose(5, 4, 3, 1, 6, 2, 0, 7).reshape(3, width, width)
        out_b = stack(parts[0])[:, :, :, 144:288].reshape(2, 2, 2, 4, 3, 48, 128).transpose(3, 2, 0, 5, 1, 4, 6)
        grad_w_outer = reduce_matrix(outer_t.T)
        grad_w_inner = reduce_matrix(inner_b)
        grad_w_out = reduce_matrix(out_b.reshape(width, width))
        grad_w_query, grad_w_key, grad_w_value = (reduce_matrix(qkv[i]) for i in range(3))
        b_query_g, b_value_g = my_share(late[0]), my_share(late[1])
        gain2_g, shift2_g, b_outer_g, gain1_g, shift1_g, b_out_g = (my_share(early[i]) for i in range(6))
        b_inner_g = my_share(early[6:10].reshape(-1))
    else:
        by_axes = lambda a: a.reshape((2, 2, 4) + a.shape[2:])
        one = lambda *shape: (shape, BF)
        top, low = slice(0, 48), slice(48, 96)
        z_swap = lambda pieces: [pieces[0]] + [swap(pieces[j], "dp", 2 * j) for j in (1, 2, 3)]
        first_shapes, second_shapes, z_shapes = [one(2, 4, 48, 768)] * 4, [one(4, 48, 768)] * 4, [one(192, 768)] * 4

        def z_split(first, top_keep, top_came, low_keep, low_came, outs):
            for j, out in enumerate(outs):
                out[first : first + 48, :] = top_keep[j] + top_came[j]
                out[first + 48 : first + 96, :] = low_keep[j] + low_came[j]

        outer_came = swap(outer[1], "seq", 1)

        def stage_a(kept, came, a_keep, a_send, b_keep, b_send):
            halves(kept, came, a_keep, a_send, 1, top)
            halves(kept, came, b_keep, b_send, 0, low)

        a_keep, a_send, b_keep, b_send = stage(
            "stage_a", stage_a, [outer[0], outer_came], first_shapes, [inner_send], room=VMEM
        )

        a_came, b_came = swap(a_send, *X), swap(b_send, *Y)
        inner_came = swap(inner_send, "seq", 1)
        inner_keep, grad1, bi_keep, attn, vec1 = backward(
            me, True, branch, slope, ht, w, [resid, grad2, partial], [a_keep, *y_blocks]
        )

        def stage_b(
            me_ref, a_keep, a_came, b_keep, b_came, i_keep, i_came, vec2, vec1, bi_keep, bi_send,
            a2_keep, a2_send, b2_keep, b2_send, c_keep, c_send, d_keep, d_send, shares,
        ):
            halves(a_keep, a_came, a2_keep, a2_send, 0)
            halves(b_keep, b_came, b2_keep, b2_send, 0)
            halves(i_keep, i_came, c_keep, c_send, 1, top)
            halves(i_keep, i_came, d_keep, d_send, 0, low)
            vector_shares(me_ref, vec2, vec1, bi_keep, bi_send, shares)

        def vector_shares(me_ref, vec2, vec1, bi_keep, bi_send, shares):
            early = jnp.concatenate([vec2[0:3], vec1[0:3]], 0)
            kept, sent = bi_keep[0:1], bi_send[0:1]
            blank = jnp.zeros((6, 32), F32)
            for d in range(8):
                core, y = me_ref[0], me_ref[1]
                at = slice((d % 2) * 384, (d % 2) * 384 + 384)
                other = slice(768 + at.start, 768 + at.stop)
                own_core = core == (d // 2) % 2
                own_y = y == d // 4
                piece = jnp.where(
                    own_core,
                    jnp.where(own_y, kept[:, at], kept[:, other]),
                    jnp.where(own_y, sent[:, at], sent[:, other]),
                )
                rows = [jnp.concatenate([early[:, d * 96 : d * 96 + 96], blank], 1)]
                rows += [piece[:, j * 128 : j * 128 + 128] for j in range(3)] + [jnp.zeros((7, 128), F32)]
                shares[d] = jnp.concatenate(rows, 0).astype(BF)

        *stage_b_outs, shares = stage(
            "stage_b",
            stage_b,
            [a_keep, a_came, b_keep, b_came, by_axes(inner_keep), by_axes(inner_came), vec2, vec1, bi_keep, bi_send],
            second_shapes + first_shapes + [one(8, 16, 128)],
            place=me,
            room=VMEM,
        )
        a_keep, a_send, b_keep, b_send, c_keep, c_send, d_keep, d_send = stage_b_outs

        a_came, b_came = swap(a_send, *Y), swap(b_send, *X)
        c_came, d_came = swap(c_send, *X), swap(d_send, *Y)
        keep0, send0, vec_0, acc = attend_back(me, 0, n, rows, saved, attn, grad1, w, shares, [a_keep])

        def stage_c(c_keep, c_came, d_keep, d_came, *outs):
            halves(c_keep, c_came, outs[0], outs[1], 0)
            halves(d_keep, d_came, outs[2], outs[3], 0)

        c_keep, c_send, d_keep, d_send = stage(
            "stage_c",
            stage_c,
            [c_keep, c_came, d_keep, d_came],
            second_shapes,
            [keep0, a_came, b_came],
            room=VMEM,
        )

        c_came, d_came = swap(c_send, *Y), swap(d_send, *X)
        came0 = swap(send0, "seq", 1)
        keep1, send1, vec_1, acc = attend_back(me, 1, n, rows, saved, attn, acc, w, None, [c_keep])

        def stage_d(a_keep, a_came, b_keep, b_came, c_keep, c_came, d_keep, d_came, keep0, came0, *outs):
            z_split(0, a_keep, a_came, b_keep, b_came, outs[:4])
            z_split(96, c_keep, c_came, d_keep, d_came, outs[:4])
            halves(keep0, came0, outs[4], outs[5], 0)

        *forward_z, p0_keep, p0_send = stage(
            "stage_d",
            stage_d,
            [a_keep, a_came, b_keep, b_came, c_keep, c_came, d_keep, d_came, by_axes(keep0), by_axes(came0)],
            z_shapes + [one(2, 4, 320, 128)] * 2,
            [keep1],
            room=VMEM,
        )

        p0_came = swap(p0_send, *Y)
        came1 = swap(send1, "seq", 1)
        forward_z = z_swap(forward_z)
        keep2, send2, vec_2, *tok_blocks = attend_back(me, 2, n, rows, saved, attn, acc, w, None, [p0_keep])

        came2 = swap(send2, "seq", 1)
        tok_blocks = exchange(tok_blocks)
        add = lambda four: sum(r[...].astype(F32) for r in four)
        x_split = lambda kept, came, a, b: halves(kept, came, a, b, 1)
        y_split = lambda kept, came, a, b: halves(kept, came, a, b, 0)
        quarter, eighth = [one(2, 4, 160, 128)] * 2, [one(4, 160, 128)] * 2

        def stage_e(p0_keep, p0_came, keep1, came1, *outs):
            halves(p0_keep, p0_came, outs[0], outs[1], 0)
            halves(keep1, came1, outs[2], outs[3], 0)

        p0_keep, p0_send, p1_keep, p1_send = stage(
            "stage_e",
            stage_e,
            [p0_keep, p0_came, by_axes(keep1), by_axes(came1)],
            [one(4, 320, 128)] * 2 + quarter,
            [keep2, *forward_z[1:]],
        )
        p1_came, p0_came = swap(p1_send, *Y), swap(p0_send, *X)
        p2_keep, p2_send = stage(
            "stage_f", x_split, [by_axes(keep2), by_axes(came2)], quarter, [p1_keep]
        )
        p2_came = swap(p2_send, *X)

        def forward_grads(*refs):
            total = add(refs[0:4])
            refs[4][0:96, :] = total[:96, :384]
            refs[4][96:192, :] = total[:96, 384:]
            refs[5][...] = total[96:]

        grad_w_outer, grad_w_inner = stage(
            "forward_grads", forward_grads, forward_z, [((192, 384), F32), ((96, 768), F32)], [p2_keep]
        )
        grad_w_outer = grad_w_outer.T
        output = unpack(seq_place, y_blocks, [grad_w_inner])

        p1_keep, p1_send = stage("stage_g", y_split, [p1_keep, p1_came], eighth, [output])
        p1_came = swap(p1_send, *X)
        p2_keep, p2_send = stage(
            "stage_h", y_split, [p2_keep, p2_came], eighth, [p1_keep, tok_blocks[2]]
        )
        p2_came = swap(p2_send, *Y)

        def stage_i(p0_keep, p0_came, p1_keep, p1_came, p2_keep, p2_came, *outs):
            for j in range(4):
                outs[j][0:320, :] = p0_keep[j] + p0_came[j]
                outs[j][320:480, :] = p1_keep[j] + p1_came[j]
                outs[j][480:640, :] = p2_keep[j] + p2_came[j]

        z_pieces = z_swap(
            stage(
                "stage_i", stage_i, [p0_keep, p0_came, p1_keep, p1_came, p2_keep, p2_came], [one(640, 128)] * 4
            )
        )
        grad_tokens = unpack(seq_place, tok_blocks)

        def gather_up(me_ref, *refs):
            total = add(refs[0:4])
            z0, z12 = total[0:320], total[320:640]
            mine, other, bq_out, bv_out, bi_out, *vec_outs = refs[4:]
            place = me_ref[2]
            for i, out in enumerate(vec_outs):
                out[...] = z0[304 + i : 305 + i, 0:96]
            bi_out[...] = jnp.concatenate([z0[310 + j : 311 + j] for j in range(3)], 1)
            first_rows = [z0[288:304], z12[144:160], z12[304:320]]
            for i, out in enumerate((bq_out, bv_out)):
                whole = [first_rows[j % 3][(j // 3) * 8 + i : (j // 3) * 8 + i + 1] for j in range(6)]
                whole = jnp.concatenate(whole, 1)
                total = jnp.zeros((1, 96), F32)
                for d in range(8):
                    total = jnp.where(place == d, whole[:, d * 96 : d * 96 + 96], total)
                out[...] = total
            rows = lambda z, first: [z[first + 48 * j : first + 48 * j + 48] for j in range(3)]
            out_w = rows(z0, 144)
            parts = [rows(z0, 0), rows(z12, 0), rows(z12, 160)]
            for i in range(4):
                pieces = out_w if i == 0 else [part[i - 1] for part in parts]
                whole = jnp.concatenate(pieces, 1)
                left, right = whole[:, :192], whole[:, 192:]
                first = me_ref[0] == 0
                mine[i] = jnp.where(first, left, right)
                other[i] = jnp.where(first, right, left).astype(BF)

        mine, other, b_query_g, b_value_g, b_inner_g, *vecs = stage(
            "gather_up",
            gather_up,
            z_pieces,
            [((4, 48, 192), F32), ((4, 48, 192), BF), ((1, 96), F32), ((1, 96), F32), ((1, 384), F32)]
            + [((1, 96), F32)] * 6,
            [grad_tokens],
            place=me,
        )
        other = swap(other, "seq", 1)

        def assemble(me_ref, mine, other, *outs):
            for i, out in enumerate(outs):
                kept, came = mine[i], other[i].astype(F32)
                first = me_ref[0] == 0
                out[0:48, :] = jnp.where(first, kept, came)
                out[48:96, :] = jnp.where(first, came, kept)

        grad_w_out, grad_w_query, grad_w_key, grad_w_value = stage(
            "assemble", assemble, [mine, other], [((96, 192), F32)] * 4, place=me
        )
        b_query_g, b_value_g, b_inner_g = (v.reshape(-1) for v in (b_query_g, b_value_g, b_inner_g))
        gain2_g, shift2_g, b_outer_g, gain1_g, shift1_g, b_out_g = (v.reshape(-1) for v in vecs)

    return (
        output,
        grad_tokens,
        grad_w_query,
        b_query_g,
        grad_w_key,
        grad_w_value,
        b_value_g,
        grad_w_out,
        b_out_g,
        gain1_g,
        shift1_g,
        grad_w_inner,
        b_inner_g,
        grad_w_outer,
        b_outer_g,
        gain2_g,
        shift2_g,
    )


def solution(mesh):
    token = P("dp", "seq", None)
    matrix = P("dp", "seq")
    vector = P("dp")
    return jax.shard_map(
        body,
        mesh=mesh,
        in_specs=(token, token, P("dp", "seq")) + (P(),) * 15,
        out_specs=(
            token,
            token,
            matrix,
            vector,
            matrix,
            matrix,
            vector,
            matrix,
            vector,
            vector,
            vector,
            matrix,
            vector,
            matrix,
            vector,
            vector,
            vector,
        ),
        check_vma=False,
    )
```
